32 devices in a mesh: task: 4 (over y, core), batch: 8 (over z, x).
Axes of the slice: x: 2, y: 2, z: 4, core: 2. Of those that a mesh axis runs over, the one named last changes fastest.
Arguments:
- tokens: bfloat16 [64, 512, 768], P(('task', 'batch')), may hold values from -6 to 6
- out_cot: bfloat16 [64, 512, 768], P(('task', 'batch')), may hold values from -6 to 6
- lengths: int32 [64], P(('task', 'batch')), may hold values from 128 to 512, as said below
- labels: int32 [64], P(('task', 'batch')), may hold values from 0 to 2
- task_ids: int32 [4], P('task'), may hold values from 0 to 7
- task_weights: float32 [4], P('task'), may hold values from 0.5 to 2
- query_weight: bfloat16 [768, 768], replicated, may hold values from -0.21875 to 0.21875
- key_weight: bfloat16 [768, 768], replicated, may hold values from -0.21875 to 0.21875
- value_weight: bfloat16 [768, 768], replicated, may hold values from -0.21875 to 0.21875
- query_bias: bfloat16 [768], replicated, may hold values from -1.5 to 1.5
- value_bias: bfloat16 [768], replicated, may hold values from -1.5 to 1.5
- output_weight: bfloat16 [768, 768], replicated, may hold values from -2.5 to 2.5
- output_bias: bfloat16 [768], replicated, may hold values from -1.5 to 1.5
- norm1_gain: bfloat16 [768], replicated, may hold values from 0.5 to 1.5
- norm1_bias: bfloat16 [768], replicated, may hold values from -1.5 to 1.5
- inner_weight: bfloat16 [768, 3072], replicated, may hold values from -0.21875 to 0.21875
- inner_bias: bfloat16 [3072], replicated, may hold values from -1.5 to 1.5
- outer_weight: bfloat16 [3072, 768], replicated, may hold values from -0.21875 to 0.21875
- outer_bias: bfloat16 [768], replicated, may hold values from -1.5 to 1.5
- norm2_gain: bfloat16 [768], replicated, may hold values from 0.5 to 1.5
- norm2_bias: bfloat16 [768], replicated, may hold values from -1.5 to 1.5
- head_table: bfloat16 [8, 3, 768], replicated, may hold values from -0.625 to 0.625
Outputs:
- block_out: bfloat16 [64, 512, 768], P(('task', 'batch'))
- token_grad: float32 [64, 512, 768], P(('task', 'batch'))
- group_loss: float32 [4], P('task')
- query_weight_grad: float32 [768, 768], P(('task', 'batch'))
- key_weight_grad: float32 [768, 768], P(('task', 'batch'))
- value_weight_grad: float32 [768, 768], P(('task', 'batch'))
- query_bias_grad: float32 [768], P(('task', 'batch'))
- value_bias_grad: float32 [768], P(('task', 'batch'))
- output_weight_grad: float32 [768, 768], P(('task', 'batch'))
- output_bias_grad: float32 [768], P(('task', 'batch'))
- norm1_gain_grad: float32 [768], P(('task', 'batch'))
- norm1_bias_grad: float32 [768], P(('task', 'batch'))
- inner_weight_grad: float32 [768, 3072], P(('task', 'batch'))
- inner_bias_grad: float32 [3072], P(('task', 'batch'))
- outer_weight_grad: float32 [3072, 768], P(('task', 'batch'))
- outer_bias_grad: float32 [768], P(('task', 'batch'))
- norm2_gain_grad: float32 [768], P(('task', 'batch'))
- norm2_bias_grad: float32 [768], P(('task', 'batch'))
- head_table_grad: float32 [8, 3, 768], replicated
The draws below stay inside these ranges and needn't reach their ends.
Inputs may be any that keep to these rules, and one draw needn't show every extreme that they name: `lengths`: at least one sequence has the full length 512; token 0 of every sequence is inside its length.
All inputs are finite; a program needn't handle non-finite values.
Results may differ from the reference program's by a relative error of at most 0.015.
Values sent between devices are 32-bit elements; how exact they have to be, the bound alone decides.
No kernel may reach another device: no remote copies, remote signals or barrier semaphores. Data moves between devices by JAX's collectives and lax.ppermute only.
A program may use at most 192 MiB of HBM per device.

```python
import math
import jax
import jax.numpy as jnp
from jax import lax

D = 768
H = 12
HD = 64
FF = 3072
NCLS = 3
NTASKS = 8
LEN = 512
GROUP_SEQS = 16
GROUPS = 4
SEQS = 64


def draw_lengths(key, part):
    key = jax.random.fold_in(key, 11)
    first_key, second_key = jax.random.split(key)
    drawn = jax.random.randint(first_key, (SEQS,), LEN // 4, LEN + 1)
    chosen = jax.random.randint(second_key, (), 0, SEQS)
    return jnp.where(jnp.arange(SEQS) == chosen, LEN, drawn).astype(jnp.int32)


def plant(values, own_key, smallest, top_value):
    shape = values.shape
    spot = [jax.random.randint(jax.random.fold_in(own_key, axis), (), 0, shape[axis]) for axis in range(len(shape))]
    values = values.at[tuple(spot)].set(smallest)
    longest = shape.index(max(shape))
    spot[longest] = (spot[longest] + 1) % shape[longest]
    return values.at[tuple(spot)].set(top_value)


def level_of(rng, extent, pieces, low, top_value):
    loudness = 1.0
    for axis_at, shards_of in pieces:
        heights = jax.random.uniform(jax.random.fold_in(jax.random.fold_in(rng, 6), axis_at), (shards_of,), jnp.float32, low / len(pieces), top_value / len(pieces))
        loudness = loudness * jnp.repeat(jnp.exp(heights), extent[axis_at] // shards_of).reshape((-1,) + (1,) * (len(extent) - 1 - axis_at))
    return loudness


def bell_draw(stream_key, dims, width, limit, cuts=(), kind=jnp.bfloat16):
    values = jax.random.normal(stream_key, dims, jnp.float32) * width
    if len(cuts) > 0:
        values = level_of(stream_key, dims, cuts, -0.22, 0.18) * values
    return jnp.clip(values, min=-limit, max=limit).astype(kind)


def setup_inputs(seed: int = 0) -> dict:
    key_of = jax.random.split(jax.random.key(seed), 23)
    tokens = bell_draw(key_of[0], (SEQS, LEN, D), 1.0, 6.0, ((0, 32),))
    out_cot = bell_draw(key_of[1], (SEQS, LEN, D), 1.0, 6.0, ((0, 32),))
    lengths = draw_lengths(jax.random.fold_in(key_of[22], 71), 0)
    labels = plant(jax.random.randint(key_of[3], (SEQS,), 0, NCLS), jax.random.fold_in(key_of[3], 1), 0, NCLS - 1).astype(jnp.int32)
    task_ids = plant(jax.random.randint(key_of[4], (GROUPS,), 0, NTASKS), jax.random.fold_in(key_of[4], 1), 0, NTASKS - 1).astype(jnp.int32)
    task_weights = jnp.clip(jnp.exp(math.log(2.0) - 1.3862944 * jax.random.uniform(key_of[5], (GROUPS,), jnp.float32) ** level_of(key_of[5], (GROUPS,), ((0, 4),), -0.2, 0.2)), 0.5, 2.0)
    query_weight = bell_draw(key_of[6], (D, D), D ** -0.5, 0.21875)
    key_weight = bell_draw(key_of[7], (D, D), D ** -0.5, 0.21875)
    value_weight = bell_draw(key_of[8], (D, D), D ** -0.5, 0.21875)
    query_bias = bell_draw(key_of[9], (D,), 0.3, 1.5)
    value_bias = bell_draw(key_of[10], (D,), 0.3, 1.5)
    output_weight = bell_draw(key_of[11], (D, D), (max(1, D // 128)) ** -0.5, 2.5)
    output_bias = bell_draw(key_of[12], (D,), 0.3, 1.5)
    norm1_gain = jnp.clip(1.0 + 0.1 * jax.random.normal(key_of[13], (D,), jnp.float32), 0.5, 1.5).astype(jnp.bfloat16)
    norm1_bias = bell_draw(key_of[14], (D,), 0.3, 1.5)
    inner_weight = bell_draw(key_of[15], (D, FF), D ** -0.5, 0.21875)
    inner_bias = bell_draw(key_of[16], (FF,), 0.3, 1.5)
    outer_weight = bell_draw(key_of[17], (FF, D), (FF // 4) ** -0.5, 0.21875)
    outer_bias = bell_draw(key_of[18], (D,), 0.3, 1.5)
    norm2_gain = jnp.clip(1.0 + 0.1 * jax.random.normal(key_of[19], (D,), jnp.float32), 0.5, 1.5).astype(jnp.bfloat16)
    norm2_bias = bell_draw(key_of[20], (D,), 0.3, 1.5)
    head_table = bell_draw(key_of[21], (NTASKS, NCLS, D), (D // 9) ** -0.5, 0.625)
    return dict(tokens=tokens, out_cot=out_cot, lengths=lengths, labels=labels, task_ids=task_ids, task_weights=task_weights, query_weight=query_weight, key_weight=key_weight, value_weight=value_weight, query_bias=query_bias, value_bias=value_bias, output_weight=output_weight, output_bias=output_bias, norm1_gain=norm1_gain, norm1_bias=norm1_bias, inner_weight=inner_weight, inner_bias=inner_bias, outer_weight=outer_weight, outer_bias=outer_bias, norm2_gain=norm2_gain, norm2_bias=norm2_bias, head_table=head_table)


@jax.custom_vjp
def low(v):
    return lax.optimization_barrier(v.astype(jnp.bfloat16)).astype(jnp.float32)

@jax.custom_vjp
def low_back(v):
    return v

def low_keep(v):
    return (low(v), None)

def low_pass(kept, grad):
    return (grad,)

def back_keep(v):
    return (v, None)

def back_low(kept, grad):
    return (low(grad),)
low.defvjp(low_keep, low_pass)
low_back.defvjp(back_keep, back_low)
precise = lax.Precision.HIGHEST
eps_norm = 1e-12

def product(left, right):
    return jnp.matmul(left, right, precision=precise)

def norm_rows(resid, gain, shift):
    center = resid - lax.optimization_barrier(jnp.mean(resid, axis=-1, keepdims=True))
    spread = lax.optimization_barrier(jnp.mean(center * center, axis=-1, keepdims=True))
    return center * lax.rsqrt(spread + eps_norm) * gain + shift

def layer_block(weights_all, inputs, seq_lengths, seq_labels, head_rows):
    query_weight, key_weight, value_weight, query_bias, value_bias, output_weight, output_bias, norm1_gain, norm1_bias, inner_weight, inner_bias, outer_weight, outer_bias, norm2_gain, norm2_bias = weights_all
    block_seqs = inputs.shape[0]
    token_rows = inputs.reshape(block_seqs * LEN, D)
    query_low = low(low_back(product(token_rows, query_weight) + query_bias)).reshape(block_seqs, LEN, H, HD)
    key_low = low(low_back(product(token_rows, key_weight))).reshape(block_seqs, LEN, H, HD)
    value_low = low(low_back(product(token_rows, value_weight) + value_bias)).reshape(block_seqs, LEN, H, HD)
    scores = low_back(jnp.einsum('bqhd,bkhd->bhqk', query_low, key_low, precision=precise) * HD ** (-0.5))
    key_valid = (jnp.arange(LEN, dtype=jnp.int32)[None, :] < seq_lengths[:, None])[:, None, None, :]
    scores = jnp.where(key_valid, scores, -1e+30)
    probs_low = low(jax.nn.softmax(scores, axis=-1))
    context = jnp.einsum('bhqk,bkhd->bqhd', probs_low, value_low, precision=precise)
    ctx_low = low(low_back(context)).reshape(block_seqs * LEN, D)
    attn = low_back(product(ctx_low, output_weight) + output_bias)
    hidden1 = norm_rows(token_rows + attn, norm1_gain, norm1_bias)
    inner = low_back(product(low(hidden1), inner_weight) + inner_bias)
    act_low = low(jax.nn.gelu(inner, approximate=False))
    down = low_back(product(act_low, outer_weight) + outer_bias)
    final = norm_rows(hidden1 + down, norm2_gain, norm2_bias).reshape(block_seqs, LEN, D)
    cls_low = low(final[:, 0, :])
    logits = jnp.einsum('bd,bcd->bc', cls_low, head_rows, precision=precise)
    picked = lax.optimization_barrier(jnp.sum(logits * jax.nn.one_hot(seq_labels, NCLS, dtype=logits.dtype), axis=-1))
    return (final, jax.nn.logsumexp(logits, axis=-1) - picked)

def reference(tokens, out_cot, lengths, labels, task_ids, task_weights, query_weight, key_weight, value_weight, query_bias, value_bias, output_weight, output_bias, norm1_gain, norm1_bias, inner_weight, inner_bias, outer_weight, outer_bias, norm2_gain, norm2_bias, head_table):
    weights_all = tuple((item.astype(jnp.float32) for item in (query_weight, key_weight, value_weight, query_bias, value_bias, output_weight, output_bias, norm1_gain, norm1_bias, inner_weight, inner_bias, outer_weight, outer_bias, norm2_gain, norm2_bias)))
    group_of = (jnp.arange(SEQS, dtype=jnp.int32) // GROUP_SEQS).astype(jnp.int32)
    seq_weight = task_weights[group_of]
    inputs_full = tokens.astype(jnp.float32)
    table_full = head_table.astype(jnp.float32)
    block_size = math.gcd(SEQS, max(1, 4096 // LEN))

    def blocked(array):
        return array.reshape((SEQS // block_size, block_size) + array.shape[1:])

    def forward(inputs, weights, table):
        head_rows = table[task_ids][group_of]
        block_step = jax.checkpoint(partial_block(weights))

        def scan_step(carry, item):
            return (carry, block_step(*item))
        carry_init = jnp.zeros((), jnp.float32)
        unused, (final, losses) = lax.scan(scan_step, carry_init, (blocked(inputs), blocked(lengths), blocked(labels), blocked(head_rows)))
        return (final.reshape(SEQS, LEN, D), losses.reshape(SEQS))
    (final, losses), pullback = jax.vjp(forward, inputs_full, weights_all, table_full)
    final_cot = out_cot.astype(jnp.float32) * seq_weight[:, None, None]
    loss_cot = seq_weight / GROUP_SEQS
    token_grad, weight_grads, head_table_grad = pullback((final_cot, loss_cot))
    query_weight_grad, key_weight_grad, value_weight_grad, query_bias_grad, value_bias_grad, output_weight_grad, output_bias_grad, norm1_gain_grad, norm1_bias_grad, inner_weight_grad, inner_bias_grad, outer_weight_grad, outer_bias_grad, norm2_gain_grad, norm2_bias_grad = weight_grads
    group_loss = task_weights * lax.optimization_barrier(jnp.mean(losses.reshape(GROUPS, GROUP_SEQS), axis=1))
    return (final.astype(jnp.bfloat16), token_grad, group_loss, query_weight_grad, key_weight_grad, value_weight_grad, query_bias_grad, value_bias_grad, output_weight_grad, output_bias_grad, norm1_gain_grad, norm1_bias_grad, inner_weight_grad, inner_bias_grad, outer_weight_grad, outer_bias_grad, norm2_gain_grad, norm2_bias_grad, head_table_grad)

def partial_block(weights):

    def block_call(inputs, seq_lengths, seq_labels, head_rows):
        return layer_block(weights, inputs, seq_lengths, seq_labels, head_rows)
    return block_call
```

```python
import functools

import jax
import jax.numpy as jnp
from jax import lax
from jax.experimental import pallas as pl
from jax.experimental.pallas import tpu as pltpu
from jax.sharding import PartitionSpec as P

HD = 64
TILE = 256
ALL_AXES = ("task", "batch")
NN = (((1,), (0,)), ((), ()))
NT = (((1,), (1,)), ((), ()))
TN = (((0,), (0,)), ((), ()))
half = jnp.bfloat16
single = jnp.float32
eps_norm = 1e-12


def dot(left, right, dims=NN):
    return lax.dot_general(left, right, dims, preferred_element_type=single)


def params(megabytes=56):
    return pltpu.CompilerParams(vmem_limit_bytes=megabytes << 20)


def cost(flops):
    return pl.CostEstimate(flops=int(flops), bytes_accessed=1 << 20, transcendentals=0)


def spec(shape, index):
    return pl.BlockSpec(shape, index)


ANY = pl.BlockSpec(memory_space=pl.ANY)
SMEM = pl.BlockSpec(memory_space=pltpu.SMEM)
TOKEN = jax.ShapeDtypeStruct((8, 128), single)


def pair_operands(q, k, h, n, scale):
    rows = q.shape[0]
    lane = lax.broadcasted_iota(jnp.int32, (rows, 128), 1)
    row = lax.broadcasted_iota(jnp.int32, (rows, 128), 0)
    pair, parity = h // 2, h % 2
    inside = (lane // HD) == parity
    spare = HD * (1 - parity)
    q_pair = q[:, pair * 128 : pair * 128 + 128].astype(single) * scale
    k_pair = k[:, pair * 128 : pair * 128 + 128].astype(single)
    q_one = jnp.where(inside, q_pair, jnp.where(lane == spare, 1.0, 0.0)).astype(half)
    k_one = jnp.where(inside, k_pair, jnp.where((lane == spare) & (row >= n), -1e30, 0.0)).astype(half)
    return q_one, k_one


def attention_kernel(
    n_ref, x_ref, wq_ref, wk_ref, wv_ref, bq_ref, bv_ref, q_ref, k_ref, v_ref, ctx_ref, ctxt_ref, lse_ref
):
    n = n_ref[pl.program_id(0)]
    x = x_ref[0]
    heads = wq_ref.shape[1] // HD
    q = (dot(x, wq_ref[...]) + bq_ref[...].astype(single)).astype(half)
    k = dot(x, wk_ref[...]).astype(half)
    v = (dot(x, wv_ref[...]) + bv_ref[...].astype(single)).astype(half)
    q_ref[0] = q
    k_ref[0] = k
    v_ref[0] = v
    vt = v.T
    scores = []
    for h in range(heads):
        q_one, k_one = pair_operands(q, k, h, n, HD**-0.5)
        scores.append(dot(k_one, q_one, NT))
    weights = []
    for s in scores:
        top = jnp.max(s, axis=0, keepdims=True)
        e = jnp.exp(s - top)
        weights.append((e.astype(half), top, jnp.sum(e, axis=0, keepdims=True)))
    for h, (e, top, total) in enumerate(weights):
        c = dot(vt[h * HD : (h + 1) * HD], e) * (1.0 / total)
        ctxt_ref[h * HD : (h + 1) * HD, :] = c.astype(half)
        lse_ref[0, 0, h : h + 1, :] = top + jnp.log(total)
    ctx_ref[0] = ctxt_ref[...].T


def attention(tokens, lengths, wq, wk, wv, bq, bv):
    seqs, length, width = tokens.shape
    quads = width // 256
    rows = spec((1, length, 256), lambda s, g, n: (s, 0, g))
    w = spec((width, 256), lambda s, g, n: (0, g))
    b = spec((1, 256), lambda s, g, n: (0, g))
    return pl.pallas_call(
        attention_kernel,
        grid_spec=pltpu.PrefetchScalarGridSpec(
            num_scalar_prefetch=1,
            grid=(seqs, quads),
            in_specs=[spec((1, length, width), lambda s, g, n: (s, 0, 0)), w, w, w, b, b],
            out_specs=[
                rows,
                rows,
                rows,
                rows,
                spec((256, length), lambda s, g, n: (g, s)),
                spec((1, 1, 8, length), lambda s, g, n: (s, g, 0, 0)),
            ],
        ),
        out_shape=[jax.ShapeDtypeStruct(tokens.shape, half)] * 4
        + [
            jax.ShapeDtypeStruct((width, seqs * length), half),
            jax.ShapeDtypeStruct((seqs, quads, 8, length), single),
        ],
        compiler_params=params(40),
        cost_estimate=cost(15e9),
        name="attention_forward",
    )(lengths, tokens, wq, wk, wv, bq.reshape(1, -1), bv.reshape(1, -1))


def norm_parts(resid):
    center = resid - jnp.mean(resid, axis=-1, keepdims=True)
    inv_root = lax.rsqrt(jnp.mean(center * center, axis=-1, keepdims=True) + eps_norm)
    return center * inv_root, inv_root


def norm_back(grad_out, normed, inv_root, gain):
    scaled = grad_out * gain
    return inv_root * (
        scaled
        - jnp.mean(scaled, axis=-1, keepdims=True)
        - normed * jnp.mean(scaled * normed, axis=-1, keepdims=True)
    )


def gelu_parts(u):
    cdf = 0.5 * (1.0 + lax.erf(u * 0.7071067811865476))
    pdf = jnp.exp(-0.5 * u * u) * 0.3989422804014327
    return u * cdf, cdf + u * pdf


def column_sum(array):
    return jnp.sum(array, axis=0, keepdims=True)


def middle_kernel(
    task_ref,
    label_ref,
    weight_ref,
    x_ref,
    ctx_ref,
    cot_ref,
    wo_ref,
    wi_ref,
    wd_ref,
    vec_ref,
    bi_ref,
    head_ref,
    out_ref,
    normed1_ref,
    root1_ref,
    h1t_ref,
    act_ref,
    slope_ref,
    dr2_ref,
    ddown_ref,
    sums_ref,
    *,
    tiles_per_seq,
    group_seqs,
):
    step = pl.program_id(0)
    vec = vec_ref[...]
    bo, g1, b1, bd, g2, b2 = [vec[i : i + 1] for i in range(6)]
    x = x_ref[...].astype(single)
    normed1, root1 = norm_parts(x + dot(ctx_ref[...], wo_ref[...]) + bo)
    normed1_ref[...] = normed1
    root1_ref[...] = jnp.broadcast_to(root1, root1_ref.shape)
    hidden1 = normed1 * g1 + b1
    h1 = hidden1.astype(half)
    h1t_ref[...] = h1.T
    ff = wi_ref.shape[1]
    part = 768
    down = None
    for j in range(0, ff, part):
        inner = dot(h1, wi_ref[:, j : j + part]) + bi_ref[:, j : j + part].astype(single)
        value, slope = gelu_parts(inner)
        act = value.astype(half)
        act_ref[:, j : j + part] = act
        slope_ref[:, j : j + part] = slope.astype(half)
        term = dot(act, wd_ref[j : j + part, :])
        down = term if down is None else down + term
    normed2, root2 = norm_parts(hidden1 + down + bd)
    final = normed2 * g2 + b2
    low = final.astype(half)
    out_ref[...] = low
    w = weight_ref[0]
    cls = low[0:1].astype(single)
    head = head_ref[0].astype(single)
    classes = head.shape[0]
    logits = [jnp.sum(cls * head[c : c + 1], axis=1, keepdims=True) for c in range(classes)]
    top = functools.reduce(jnp.maximum, logits)
    lse = top + jnp.log(sum(jnp.exp(v - top) for v in logits))
    label = label_ref[step // tiles_per_seq]
    first = jnp.where(step % tiles_per_seq == 0, 1.0, 0.0)
    picked = sum(jnp.where(label == c, v, 0.0) for c, v in enumerate(logits))
    slopes = [
        (jnp.exp(v - lse) - jnp.where(label == c, 1.0, 0.0)) * (w / group_seqs * first)
        for c, v in enumerate(logits)
    ]
    d_cls = sum(s * head[c : c + 1] for c, s in enumerate(slopes))
    row = lax.broadcasted_iota(jnp.int32, final.shape, 0)
    d_final = cot_ref[...].astype(single) * w + jnp.where(row == 0, d_cls, 0.0)
    dr2 = norm_back(d_final, normed2, root2, g2)
    dr2_ref[...] = dr2
    ddown = dr2.astype(half)
    ddown_ref[...] = ddown

    @pl.when(step == 0)
    def _():
        sums_ref[...] = jnp.zeros_like(sums_ref)

    sums_ref[0:1] += column_sum(d_final * normed2)
    sums_ref[1:2] += column_sum(d_final)
    sums_ref[2:3] += column_sum(ddown.astype(single))
    for c in range(classes):
        sums_ref[3 + c : 4 + c] += slopes[c] * cls
    sums_ref[7:8] += jnp.broadcast_to((lse - picked) * (w / group_seqs * first), cls.shape)


def middle(tokens, ctx, cot, labels, task_ids, task_weights, wo, wi, wd, vec, bi, head_table, group_seqs):
    seqs, length, width = tokens.shape
    rows = seqs * length
    ff = wi.shape[1]
    classes = head_table.shape[1]
    assert classes <= 4
    tile = spec((TILE, width), lambda i, t, l: (i, 0))
    wide = spec((TILE, ff), lambda i, t, l: (i, 0))

    def whole(shape):
        return spec(shape, lambda i, t, l: (0, 0))

    return pl.pallas_call(
        functools.partial(middle_kernel, tiles_per_seq=length // TILE, group_seqs=group_seqs),
        grid_spec=pltpu.PrefetchScalarGridSpec(
            num_scalar_prefetch=2,
            grid=(rows // TILE,),
            in_specs=[
                SMEM,
                tile,
                tile,
                tile,
                whole((width, width)),
                whole((width, ff)),
                whole((ff, width)),
                whole((8, width)),
                whole((1, ff)),
                spec((1, classes, width), lambda i, t, l: (t[0], 0, 0)),
            ],
            out_specs=[
                tile,
                tile,
                spec((TILE, 128), lambda i, t, l: (i, 0)),
                spec((width, TILE), lambda i, t, l: (0, i)),
                wide,
                wide,
                tile,
                tile,
                whole((8, width)),
            ],
        ),
        out_shape=[
            jax.ShapeDtypeStruct((rows, width), half),
            jax.ShapeDtypeStruct((rows, width), single),
            jax.ShapeDtypeStruct((rows, 128), single),
            jax.ShapeDtypeStruct((width, rows), half),
            jax.ShapeDtypeStruct((rows, ff), half),
            jax.ShapeDtypeStruct((rows, ff), half),
            jax.ShapeDtypeStruct((rows, width), single),
            jax.ShapeDtypeStruct((rows, width), half),
            jax.ShapeDtypeStruct((8, width), single),
        ],
        compiler_params=params(),
        cost_estimate=cost(20e9),
        name="middle_forward",
    )(
        task_ids,
        labels,
        task_weights,
        tokens.reshape(rows, width),
        ctx.reshape(rows, width),
        cot.reshape(rows, width),
        wo,
        wi,
        wd,
        vec,
        bi.reshape(1, -1),
        head_table,
    )


def inner_grad_kernel(token_ref, ddown_ref, wd_ref, slope_ref, dinner_ref, bias_ref):
    d = dot(ddown_ref[...], wd_ref[...], NT) * slope_ref[...].astype(single)
    low = d.astype(half)
    dinner_ref[...] = low
    bias_ref[...] = column_sum(low.astype(single))


def inner_grad(token, ddown, wd, slope):
    rows, width = ddown.shape
    ff = wd.shape[0]
    part = 768
    return pl.pallas_call(
        inner_grad_kernel,
        grid=(ff // part,),
        in_specs=[
            ANY,
            spec((rows, width), lambda j: (0, 0)),
            spec((part, width), lambda j: (j, 0)),
            spec((rows, part), lambda j: (0, j)),
        ],
        out_specs=[spec((rows, part), lambda j: (0, j)), spec((1, part), lambda j: (0, j))],
        out_shape=[jax.ShapeDtypeStruct((rows, ff), half), jax.ShapeDtypeStruct((1, ff), single)],
        compiler_params=params(),
        cost_estimate=cost(20e9),
        name="inner_grad",
    )(token, ddown, wd, slope)


def first_norm_kernel(
    pos_ref,
    token_ref,
    dinner_ref,
    wi_ref,
    dr2_ref,
    normed1_ref,
    root1_ref,
    wo_ref,
    ctxt_ref,
    vec_ref,
    x_ref,
    dr1_ref,
    dctx_ref,
    xt_ref,
    send_ref,
    keep_ref,
    sums_ref,
):
    step = pl.program_id(0)
    g1 = vec_ref[1:2]
    normed1 = normed1_ref[...]
    dh1 = dr2_ref[...] + dot(dinner_ref[...], wi_ref[...], NT)
    dr1 = norm_back(dh1, normed1, root1_ref[:, 0:1], g1)
    dr1_ref[...] = dr1
    dattn = dr1.astype(half)
    dctx_ref[...] = dot(dattn, wo_ref[...], NT).astype(half)
    xt_ref[...] = x_ref[...].T

    @pl.when(step == 0)
    def _():
        sums_ref[...] = jnp.zeros_like(sums_ref)
        send_ref[...] = jnp.zeros_like(send_ref)
        keep_ref[...] = jnp.zeros_like(keep_ref)

    sums_ref[0:1] += column_sum(dh1 * normed1)
    sums_ref[1:2] += column_sum(dh1)
    sums_ref[2:3] += column_sum(dattn.astype(single))
    me = pos_ref[1]
    part = dot(ctxt_ref[...], dattn)
    quarter = part.shape[0] // 4
    for y in range(2):
        zero = part[2 * y * quarter : (2 * y + 1) * quarter]
        one = part[(2 * y + 1) * quarter : (2 * y + 2) * quarter]
        send_ref[y * quarter : (y + 1) * quarter] += jnp.where(me == 0, one, zero)
        keep_ref[y * quarter : (y + 1) * quarter] += jnp.where(me == 0, zero, one)


def first_norm(pos, token, dinner, wi, dr2, normed1, root1, wo, ctxt, vec, x):
    rows, width = dr2.shape
    ff = wi.shape[1]
    tile = spec((TILE, width), lambda i, p: (i, 0))

    def whole(shape):
        return spec(shape, lambda i, p: (0, 0))

    return pl.pallas_call(
        first_norm_kernel,
        grid_spec=pltpu.PrefetchScalarGridSpec(
            num_scalar_prefetch=1,
            grid=(rows // TILE,),
            in_specs=[
                ANY,
                spec((TILE, ff), lambda i, p: (i, 0)),
                whole((width, ff)),
                tile,
                tile,
                spec((TILE, 128), lambda i, p: (i, 0)),
                whole((width, width)),
                spec((width, TILE), lambda i, p: (0, i)),
                whole((8, width)),
                tile,
            ],
            out_specs=[
                tile,
                tile,
                spec((width, TILE), lambda i, p: (0, i)),
                whole((width // 2, width)),
                whole((width // 2, width)),
                whole((8, width)),
            ],
        ),
        out_shape=[
            jax.ShapeDtypeStruct((rows, width), single),
            jax.ShapeDtypeStruct((rows, width), half),
            jax.ShapeDtypeStruct((width, rows), half),
            jax.ShapeDtypeStruct((width // 2, width), single),
            jax.ShapeDtypeStruct((width // 2, width), single),
            jax.ShapeDtypeStruct((8, width), single),
        ],
        compiler_params=params(),
        cost_estimate=cost(20e9),
        name="first_norm_back",
    )(pos, token, dinner, wi, dr2, normed1, root1, wo, ctxt, vec, x)


def attention_back_kernel(
    n_ref, token_ref, q_ref, k_ref, v_ref, ctx_ref, dctx_ref, lse_ref, dq_ref, dk_ref, dv_ref, sums_ref, dqt_ref
):
    n = n_ref[pl.program_id(0)]
    q, k, v, dctx = q_ref[0], k_ref[0], v_ref[0], dctx_ref[0]
    rows, width = q.shape
    heads = width // HD
    lane = lax.broadcasted_iota(jnp.int32, (rows, 128), 1)
    kt = k.T
    prod_t = (ctx_ref[0].astype(single) * dctx.astype(single)).T
    scale = HD**-0.5
    for pair in range(heads // 2):
        cols = slice(pair * 128, pair * 128 + 128)
        q_pair, v_pair, d_pair = q[:, cols], v[:, cols], dctx[:, cols]
        dks, dvs = [], []
        for parity in range(2):
            h = pair * 2 + parity
            q_one, k_one = pair_operands(q, k, h, n, scale)
            p = jnp.exp(dot(k_one, q_one, NT) - lse_ref[0, 0, h : h + 1, :])
            inside = (lane // HD) == parity
            v_one = jnp.where(inside, v_pair.astype(single), 0.0).astype(half)
            dp = dot(v_one, d_pair, NT)
            delta = jnp.sum(prod_t[h * HD : (h + 1) * HD], axis=0, keepdims=True)
            ds = (p * (dp - delta)).astype(half)
            dvs.append(dot(p.astype(half), d_pair))
            dks.append(dot(ds, q_pair))
            dqt_ref[h * HD : (h + 1) * HD, :] = (dot(kt[h * HD : (h + 1) * HD], ds) * scale).astype(half)
        low_half = lane < HD
        dk_ref[0, :, cols] = (jnp.where(low_half, dks[0], dks[1]) * scale).astype(half)
        dv_ref[0, :, cols] = jnp.where(low_half, dvs[0], dvs[1]).astype(half)
    dq = dqt_ref[...].T
    dq_ref[0] = dq
    sums_ref[0, 0, 0:1, :] = column_sum(dq.astype(single))
    sums_ref[0, 0, 1:2, :] = column_sum(dv_ref[0].astype(single))


def attention_back(lengths, token, q, k, v, ctx, dctx, lse):
    seqs, length, width = q.shape
    quads = width // 256
    rows = spec((1, length, 256), lambda s, g, n: (s, 0, g))
    return pl.pallas_call(
        attention_back_kernel,
        grid_spec=pltpu.PrefetchScalarGridSpec(
            num_scalar_prefetch=1,
            grid=(seqs, quads),
            in_specs=[ANY, rows, rows, rows, rows, rows, spec((1, 1, 8, length), lambda s, g, n: (s, g, 0, 0))],
            out_specs=[rows, rows, rows, spec((1, 1, 8, 256), lambda s, g, n: (s, g, 0, 0))],
            scratch_shapes=[pltpu.VMEM((256, length), half)],
        ),
        out_shape=[jax.ShapeDtypeStruct(q.shape, half)] * 3 + [jax.ShapeDtypeStruct((seqs, quads, 8, 256), single)],
        compiler_params=params(),
        cost_estimate=cost(20e9),
        name="attention_back",
    )(lengths, token, q, k, v, ctx, dctx.reshape(q.shape), lse)


def outer_send_kernel(pos_ref, act_ref, ddown_ref, send_ref):
    send_ref[0] = dot(act_ref[...], ddown_ref[...], TN)


def outer_send(pos, act, ddown, other):
    rows, width = ddown.shape
    ff = act.shape[1]
    part = ff // 4
    return pl.pallas_call(
        outer_send_kernel,
        grid_spec=pltpu.PrefetchScalarGridSpec(
            num_scalar_prefetch=1,
            grid=(2,),
            in_specs=[
                spec((rows, part), lambda y, p: (0, 2 * y + (1 - p[1] if other else p[1]))),
                spec((rows, width), lambda y, p: (0, 0)),
            ],
            out_specs=spec((1, part, width), lambda y, p: (y, 0, 0)),
        ),
        out_shape=jax.ShapeDtypeStruct((2, part, width), single),
        compiler_params=params(),
        cost_estimate=cost(10e9),
        name="outer_weight_send",
    )(pos, act, ddown)


def split_x(pos, block, rows, cols, at, sx, kx, to):
    me = pos[2]
    for z in range(4):
        zero = block[(2 * z) * rows : (2 * z + 1) * rows, cols]
        one = block[(2 * z + 1) * rows : (2 * z + 2) * rows, cols]
        sx[at + (z, slice(None), to)] = jnp.where(me == 0, one, zero)
        kx[at + (z, slice(None), to)] = jnp.where(me == 0, zero, one)


def split_z(pos, block, rows, cols, at, sz, kz, to):
    side = pos[3]
    for x in range(2):
        zs = [block[(2 * z + x) * rows : (2 * z + x + 1) * rows, cols] for z in range(4)]
        for hi, (even, odd) in enumerate(((0, 1), (3, 2))):
            sz[at + (hi, x, slice(None), to)] = jnp.where(side == 0, zs[odd], zs[even])
            kz[at + (hi, x, slice(None), to)] = jnp.where(side == 0, zs[even], zs[odd])


def outer_keep_kernel(pos_ref, token_ref, act_ref, ddown_ref, got_ref, sx_ref, kx_ref, sy_ref, ky_ref, sz_ref, kz_ref, tok_ref):
    y = pl.program_id(0)
    block = dot(act_ref[...], ddown_ref[...], TN) + got_ref[0]
    rows = block.shape[0] // 8
    third = block.shape[1] // 3
    split_x(pos_ref, block, rows, slice(0, third), (0,), sx_ref, kx_ref, slice(None))
    mid = block[:, third : 2 * third].reshape(4, 2, rows, third)

    @pl.when(y == pos_ref[0])
    def _():
        ky_ref[...] = mid

    @pl.when(y != pos_ref[0])
    def _():
        sy_ref[...] = mid

    split_z(pos_ref, block, rows, slice(2 * third, 3 * third), (0,), sz_ref, kz_ref, slice(None))
    tok_ref[...] = block[0:8, 0:128]


def outer_keep(pos, token, act, ddown, got):
    rows, width = ddown.shape
    ff = act.shape[1]
    part = ff // 4
    r, third = part // 8, width // 3
    xs = spec((1, 4, r, third), lambda y, p: (y, 0, 0, 0))
    ys = spec((4, 2, r, third), lambda y, p: (0, 0, 0, 0))
    zs = spec((1, 2, 2, r, third), lambda y, p: (y, 0, 0, 0, 0))
    return pl.pallas_call(
        outer_keep_kernel,
        grid_spec=pltpu.PrefetchScalarGridSpec(
            num_scalar_prefetch=1,
            grid=(2,),
            in_specs=[
                ANY,
                spec((rows, part), lambda y, p: (0, 2 * y + p[1])),
                spec((rows, width), lambda y, p: (0, 0)),
                spec((1, part, width), lambda y, p: (y, 0, 0)),
            ],
            out_specs=[xs, xs, ys, ys, zs, zs, spec((8, 128), lambda y, p: (0, 0))],
        ),
        out_shape=[jax.ShapeDtypeStruct((2, 4, r, third), single)] * 2
        + [jax.ShapeDtypeStruct((4, 2, r, third), single)] * 2
        + [jax.ShapeDtypeStruct((2, 2, 2, r, third), single)] * 2
        + [TOKEN],
        compiler_params=params(),
        cost_estimate=cost(10e9),
        name="outer_weight_keep",
    )(pos, token, act, ddown, got)


def row_half(left_ref, me):
    return jnp.concatenate([left_ref[0, me], left_ref[1, me]], axis=0)


def rows_send_kernel(pos_ref, token_ref, left_ref, right_ref, send_ref, tok_ref, *, other):
    me = 1 - pos_ref[1] if other else pos_ref[1]
    send_ref[0] = dot(row_half(left_ref, me), right_ref[...])
    tok_ref[...] = send_ref[0, 0:8, 0:128]


def rows_send(pos, token, left_t, right, other, parts):
    width, rows = left_t.shape
    columns = right.shape[1] // parts
    return pl.pallas_call(
        functools.partial(rows_send_kernel, other=other),
        grid_spec=pltpu.PrefetchScalarGridSpec(
            num_scalar_prefetch=1,
            grid=(parts,),
            in_specs=[
                ANY,
                spec((2, 2, width // 4, rows), lambda j, p: (0, 0, 0, 0)),
                spec((rows, columns), lambda j, p: (0, j)),
            ],
            out_specs=[
                spec((1, width // 2, columns), lambda j, p: (j, 0, 0)),
                spec((8, 128), lambda j, p: (0, 0)),
            ],
        ),
        out_shape=[jax.ShapeDtypeStruct((parts, width // 2, columns), single), TOKEN],
        compiler_params=params(),
        cost_estimate=cost(10e9),
        name="weight_rows_send",
    )(pos, token, left_t.reshape(2, 2, width // 4, rows), right)


def inner_keep_kernel(
    pos_ref,
    token_ref,
    left_ref,
    right_ref,
    got_ref,
    okeep_ref,
    ogot_ref,
    sx_ref,
    kx_ref,
    sy_ref,
    ky_ref,
    sz_ref,
    kz_ref,
    tok_ref,
):
    step = pl.program_id(0)
    block = dot(row_half(left_ref, pos_ref[1]), right_ref[...]) + got_ref[0]
    count, columns = block.shape
    rows = count // 16
    tok_ref[...] = block[0:8, 0:128]
    out_half = okeep_ref.shape[1] // 2

    @pl.when(step == 0)
    def _():
        extra = okeep_ref[:, :out_half] + ogot_ref[:, :out_half]
        for y in range(2):
            sub = slice(y * 8 * rows, (y + 1) * 8 * rows)
            split_x(pos_ref, block[sub], rows, slice(None), (y,), sx_ref, kx_ref, slice(0, columns))
            split_x(pos_ref, extra[sub], rows, slice(None), (y,), sx_ref, kx_ref, slice(columns, columns + out_half))

    @pl.when(step == 1)
    def _():
        extra = okeep_ref[:, out_half:] + ogot_ref[:, out_half:]
        me = pos_ref[0]
        for data, to in ((block, slice(0, columns)), (extra, slice(columns, columns + out_half))):
            zero = data[: 8 * rows].reshape(4, 2, rows, data.shape[1])
            one = data[8 * rows :].reshape(4, 2, rows, data.shape[1])
            sy_ref[:, :, :, to] = jnp.where(me == 0, one, zero)
            ky_ref[:, :, :, to] = jnp.where(me == 0, zero, one)

    @pl.when(step == 2)
    def _():
        for y in range(2):
            sub = slice(y * 8 * rows, (y + 1) * 8 * rows)
            split_z(pos_ref, block[sub], rows, slice(None), (y,), sz_ref, kz_ref, slice(None))


def inner_keep(pos, token, left_t, right, got, out_keep, out_got):
    width, rows = left_t.shape
    columns = right.shape[1] // 3
    r = width // 32
    wide = columns + out_keep.shape[1] // 2

    def whole(shape):
        return spec(shape, lambda j, p: (0,) * len(shape))

    shapes = [(2, 4, r, wide)] * 2 + [(4, 2, r, wide)] * 2 + [(2, 2, 2, r, columns)] * 2
    return pl.pallas_call(
        inner_keep_kernel,
        grid_spec=pltpu.PrefetchScalarGridSpec(
            num_scalar_prefetch=1,
            grid=(3,),
            in_specs=[
                ANY,
                whole((2, 2, width // 4, rows)),
                spec((rows, columns), lambda j, p: (0, j)),
                spec((1, width // 2, columns), lambda j, p: (j, 0, 0)),
                whole(out_keep.shape),
                whole(out_keep.shape),
            ],
            out_specs=[whole(s) for s in shapes] + [whole((8, 128))],
        ),
        out_shape=[jax.ShapeDtypeStruct(s, single) for s in shapes] + [TOKEN],
        compiler_params=params(),
        cost_estimate=cost(10e9),
        name="inner_weight_keep",
    )(pos, token, left_t.reshape(2, 2, width // 4, rows), right, got, out_keep, out_got)


def qkv_send_kernel(pos_ref, left_ref, dq_ref, dk_ref, dv_ref, send_ref, tok_ref, *, other):
    me = 1 - pos_ref[1] if other else pos_ref[1]
    left = row_half(left_ref, me)
    for t, ref in enumerate((dq_ref, dk_ref, dv_ref)):
        send_ref[t] = dot(left, ref[...])
    tok_ref[...] = send_ref[0, 0:8, 0:128]


def qkv_send(pos, xt, dq, dk, dv, other):
    width, rows = xt.shape

    def whole(shape):
        return spec(shape, lambda j, p: (0,) * len(shape))

    return pl.pallas_call(
        functools.partial(qkv_send_kernel, other=other),
        grid_spec=pltpu.PrefetchScalarGridSpec(
            num_scalar_prefetch=1,
            grid=(1,),
            in_specs=[whole((2, 2, width // 4, rows))] + [whole((rows, width))] * 3,
            out_specs=[whole((3, width // 2, width)), whole((8, 128))],
        ),
        out_shape=[jax.ShapeDtypeStruct((3, width // 2, width), single), TOKEN],
        compiler_params=params(),
        cost_estimate=cost(10e9),
        name="qkv_weight_send",
    )(pos, xt.reshape(2, 2, width // 4, rows), dq, dk, dv)


def qkv_keep_kernel(pos_ref, token_ref, left_ref, dq_ref, dk_ref, dv_ref, got_ref, sx_ref, kx_ref, sy_ref, ky_ref, tok_ref):
    left = row_half(left_ref, pos_ref[1])
    width = dq_ref.shape[1]
    mid = width // 2
    rows = width // 32
    gq, gk, gv = [dot(left, ref[...]) + got_ref[t] for t, ref in enumerate((dq_ref, dk_ref, dv_ref))]
    tok_ref[...] = gq[0:8, 0:128]
    for y in range(2):
        sub = slice(y * 8 * rows, (y + 1) * 8 * rows)
        split_x(pos_ref, gq[sub], rows, slice(None), (y,), sx_ref, kx_ref, slice(0, width))
        split_x(pos_ref, gk[sub], rows, slice(0, mid), (y,), sx_ref, kx_ref, slice(width, width + mid))
    me = pos_ref[0]
    for data, to in ((gk[:, mid:], slice(0, mid)), (gv, slice(mid, mid + width))):
        zero = data[: 8 * rows].reshape(4, 2, rows, data.shape[1])
        one = data[8 * rows :].reshape(4, 2, rows, data.shape[1])
        sy_ref[:, :, :, to] = jnp.where(me == 0, one, zero)
        ky_ref[:, :, :, to] = jnp.where(me == 0, zero, one)


def qkv_keep(pos, token, xt, dq, dk, dv, got):
    width, rows = xt.shape
    r = width // 32
    wide = width + width // 2

    def whole(shape):
        return spec(shape, lambda j, p: (0,) * len(shape))

    shapes = [(2, 4, r, wide)] * 2 + [(4, 2, r, wide)] * 2
    return pl.pallas_call(
        qkv_keep_kernel,
        grid_spec=pltpu.PrefetchScalarGridSpec(
            num_scalar_prefetch=1,
            grid=(1,),
            in_specs=[ANY, whole((2, 2, width // 4, rows))] + [whole((rows, width))] * 3 + [whole((3, width // 2, width))],
            out_specs=[whole(s) for s in shapes] + [whole((8, 128))],
        ),
        out_shape=[jax.ShapeDtypeStruct(s, single) for s in shapes] + [TOKEN],
        compiler_params=params(),
        cost_estimate=cost(10e9),
        name="qkv_weight_keep",
    )(pos, token, xt.reshape(2, 2, width // 4, rows), dq, dk, dv, got)


def token_grad_kernel(token_ref, dr1_ref, dq_ref, dk_ref, dv_ref, wq_ref, wk_ref, wv_ref, out_ref):
    out_ref[...] = (
        dr1_ref[...]
        + dot(dq_ref[...], wq_ref[...], NT)
        + dot(dk_ref[...], wk_ref[...], NT)
        + dot(dv_ref[...], wv_ref[...], NT)
    )


def token_grads(token, dr1, dq, dk, dv, wq, wk, wv):
    rows, width = dr1.shape
    tile = spec((TILE, width), lambda i: (i, 0))
    w = spec((width, width), lambda i: (0, 0))
    return pl.pallas_call(
        token_grad_kernel,
        grid=(rows // TILE,),
        in_specs=[ANY, tile, tile, tile, tile, w, w, w],
        out_specs=tile,
        out_shape=jax.ShapeDtypeStruct((rows, width), single),
        compiler_params=params(),
        cost_estimate=cost(10e9),
        name="token_grad",
    )(token, dr1, dq, dk, dv, wq, wk, wv)


def pair_list(change):
    pairs = []
    for y in range(2):
        for c in range(2):
            for z in range(4):
                for x in range(2):
                    py, pc, pz, px = change(y, c, z, x)
                    pairs.append((((y * 2 + c) * 4 + z) * 2 + x, ((py * 2 + pc) * 4 + pz) * 2 + px))
    return pairs


PAIRS = {
    "y": pair_list(lambda y, c, z, x: (1 - y, c, z, x)),
    "c": pair_list(lambda y, c, z, x: (y, 1 - c, z, x)),
    "x": pair_list(lambda y, c, z, x: (y, c, z, 1 - x)),
    "near": pair_list(lambda y, c, z, x: (y, c, z ^ 1, x)),
    "far": pair_list(lambda y, c, z, x: (y, c, 3 - z, x)),
}


def swap(array, name):
    return lax.ppermute(array, ALL_AXES, PAIRS[name])


def take(array, axis, index):
    return lax.dynamic_index_in_dim(array, index, axis, keepdims=False)


def halves(parts, axis, me):
    return sum_of([take(p, axis, 1 - me) for p in parts]), [take(p, axis, me) for p in parts]


def sum_of(parts):
    return functools.reduce(jnp.add, parts)


def z_sides(parts, side):
    zero = [jnp.stack([p[0], p[3]]) for p in parts]
    one = [jnp.stack([p[1], p[2]]) for p in parts]
    sent = sum_of([jnp.where(side == 0, b, a) for a, b in zip(zero, one)])
    kept = [jnp.where(side == 0, a, b) for a, b in zip(zero, one)]
    return sent, kept


def small_sum(array):
    for name in ("c", "x", "y", "near", "far"):
        array = array + swap(array, name)
    return array


def per_device(
    tokens,
    out_cot,
    lengths,
    labels,
    task_ids,
    task_weights,
    query_weight,
    key_weight,
    value_weight,
    query_bias,
    value_bias,
    output_weight,
    output_bias,
    norm1_gain,
    norm1_bias,
    inner_weight,
    inner_bias,
    outer_weight,
    outer_bias,
    norm2_gain,
    norm2_bias,
    head_table,
    *,
    staged,
):
    seqs, length, width = tokens.shape
    rows = seqs * length
    ff = inner_weight.shape[1]
    group_seqs = seqs * lax.axis_size("batch")
    task_index = lax.axis_index("task")
    batch_index = lax.axis_index("batch")
    my_y, my_c, my_z, my_x = task_index // 2, task_index % 2, batch_index // 2, batch_index % 2
    my_hi = my_z // 2
    my_side = (my_z // 2) ^ (my_z % 2)
    pos = jnp.stack([my_y, my_c, my_x, my_side, my_hi]).astype(jnp.int32)
    vec = jnp.stack(
        [output_bias, norm1_gain, norm1_bias, outer_bias, norm2_gain, norm2_bias, norm2_bias, norm2_bias]
    ).astype(single)

    q, k, v, ctx, ctxt, lse = attention(
        tokens, lengths, query_weight, key_weight, value_weight, query_bias, value_bias
    )
    block_out, normed1, root1, h1t, act, slope, dr2, ddown, sums2 = middle(
        tokens,
        ctx,
        out_cot,
        labels,
        task_ids,
        task_weights,
        output_weight,
        inner_weight,
        outer_weight,
        vec,
        inner_bias,
        head_table,
        group_seqs,
    )
    block_out = block_out.reshape(tokens.shape)
    x_rows = tokens.reshape(rows, width)

    o_send = outer_send(pos, act, ddown, True)
    if staged:
        o_got = swap(o_send, "c")
    dinner, inner_bias_sum = inner_grad(o_send, ddown, outer_weight, slope)
    if staged:
        osx, okx, osy, oky, osz, okz, token = outer_keep(pos, dinner, act, ddown, o_got)
        orx, ory, orz = swap(osx, "x"), swap(osy, "y"), swap(osz, "near")
    else:
        o_keep = outer_send(pos, act, ddown, False)
        token = o_keep
    i_send, token = rows_send(pos, token, h1t, dinner, True, 3)
    if staged:
        i_got = swap(i_send, "c")
    dr1, dctx, xt, out_send, out_keep, sums1 = first_norm(
        pos, token, dinner, inner_weight, dr2, normed1, root1, output_weight, ctxt, vec, x_rows
    )
    if staged:
        out_got = swap(out_send, "c")
        isx, ikx, isy, iky, isz, ikz, token = inner_keep(pos, dr1, h1t, dinner, i_got, out_keep, out_got)
        irx, iry, irz = swap(isx, "x"), swap(isy, "y"), swap(isz, "near")
    else:
        i_keep, token = rows_send(pos, token, h1t, dinner, False, 3)
    dq, dk, dv, sums0 = attention_back(lengths, token, q, k, v, ctx, dctx, lse)
    dq, dk, dv = [a.reshape(rows, width) for a in (dq, dk, dv)]
    qkv_s, token = qkv_send(pos, xt, dq, dk, dv, True)

    if staged:
        qkv_got = swap(qkv_s, "c")

        def second(kx, rx, ky, ry, kz, rz):
            xs, xk = halves([kx, rx], 0, my_y)
            ys, yk = halves([ky, ry], 1, my_x)
            xk.append(swap(xs, "y"))
            yk.append(swap(ys, "x"))
            if kz is None:
                return xk, yk, None
            zs, zk = halves([kz, rz], 1, my_hi)
            zk.append(swap(zs, "far"))
            return xk, yk, zk

        def third(xk, yk, zk):
            xs, xk = z_sides(xk, my_side)
            ys, yk = z_sides(yk, my_side)
            got = swap(jnp.concatenate([xs, ys], axis=-1), "near")
            split = xs.shape[-1]
            xk.append(got[..., :split])
            yk.append(got[..., split:])
            if zk is None:
                return xk, yk, None
            zs, zk = halves(zk, 1, my_x)
            zk.append(swap(zs, "x"))
            return xk, yk, zk

        def fourth(xk, yk, zk):
            xs, xk = halves(xk, 0, my_hi)
            ys, yk = halves(yk, 0, my_hi)
            got = swap(jnp.concatenate([xs, ys], axis=-1), "far")
            split = xs.shape[-1]
            x_sum = sum_of(xk + [got[..., :split]])
            y_sum = sum_of(yk + [got[..., split:]])
            if zk is None:
                return x_sum, y_sum, None
            zs, zk = halves(zk, 0, my_y)
            return x_sum, y_sum, sum_of(zk + [swap(zs, "y")])

        o_parts = fourth(*third(*second(okx, orx, oky, ory, okz, orz)))
        i_parts = fourth(*third(*second(ikx, irx, iky, iry, ikz, irz)))
    token_grad = token_grads(token, dr1, dq, dk, dv, query_weight, key_weight, value_weight)
    token_grad = token_grad.reshape(tokens.shape)

    classes = head_table.shape[1]
    chooser = (jnp.arange(head_table.shape[0], dtype=jnp.int32) == task_ids[0]).astype(single)
    head_local = (chooser[:, None, None] * sums2[None, 3 : 3 + classes, :]).reshape(-1, width)
    loss_row = jnp.where(jnp.arange(width)[None, :] == task_index, sums2[7:8], 0.0)
    bias0 = sums0.sum(axis=0).transpose(1, 0, 2).reshape(8, width)
    small = jnp.concatenate(
        [bias0[:2], sums1[:3], inner_bias_sum.reshape(-1, width), sums2[:3], loss_row, head_local], axis=0
    )

    if staged:
        small = small_sum(small)
        qsx, qkx, qsy, qky, token = qkv_keep(pos, token_grad, xt, dq, dk, dv, qkv_got)
        qrx, qry = swap(qsx, "x"), swap(qsy, "y")
        q_x, q_y, _ = fourth(*third(*second(qkx, qrx, qky, qry, None, None)))
        mid = width // 2
        wide = i_parts[2].shape[-1]
        outer_s = jnp.concatenate(o_parts, axis=-1)
        inner_s = jnp.concatenate([i_parts[0][:, :wide], i_parts[1][:, :wide], i_parts[2]], axis=-1)
        output_s = jnp.concatenate([i_parts[0][:, wide:], i_parts[1][:, wide:]], axis=-1)
        query_s = q_x[:, :width]
        key_s = jnp.concatenate([q_x[:, width:], q_y[:, :mid]], axis=-1)
        value_s = q_y[:, mid:]
    else:
        small = lax.psum(small, ALL_AXES)
        qkv_k, _ = qkv_send(pos, xt, dq, dk, dv, False)

        def whole_rows(sent, kept):
            both = jnp.stack([jnp.where(my_c == 0, kept, sent), jnp.where(my_c == 0, sent, kept)], axis=1)
            return both.reshape(-1, both.shape[-1])

        def scatter(grad):
            return lax.psum_scatter(grad, ALL_AXES, scatter_dimension=0, tiled=True)

        def by_rows(array):
            return array.reshape(2, -1, array.shape[-1])

        outer_s = scatter(whole_rows(o_send, o_keep))
        inner_s = scatter(
            jnp.concatenate([whole_rows(by_rows(i_send[j]), by_rows(i_keep[j])) for j in range(3)], axis=-1)
        )
        output_s = scatter(whole_rows(by_rows(out_send), by_rows(out_keep)))
        query_s, key_s, value_s = [scatter(whole_rows(by_rows(qkv_s[t]), by_rows(qkv_k[t]))) for t in range(3)]

    where = task_index * lax.axis_size("batch") + batch_index
    devices = lax.axis_size("task") * lax.axis_size("batch")

    def mine(array):
        flat = array.reshape(-1)
        count = flat.shape[0] // devices
        return lax.dynamic_slice(flat, (where * count,), (count,))

    bias_rows = ff // width
    at = 5 + bias_rows
    loss = lax.dynamic_slice(small, (at + 3, task_index), (1, 1)).reshape(1)
    head_grad = small[at + 4 :].reshape(head_table.shape)
    return (
        block_out,
        token_grad,
        loss,
        query_s,
        key_s,
        value_s,
        mine(small[0]),
        mine(small[1]),
        output_s,
        mine(small[4]),
        mine(small[2]),
        mine(small[3]),
        inner_s,
        mine(small[5:at]),
        outer_s,
        mine(small[at + 2]),
        mine(small[at]),
        mine(small[at + 1]),
        head_grad,
    )


def solution(mesh):
    rows = P(ALL_AXES)
    plain = P()
    task = P("task")
    staged = mesh.shape["task"] == 4 and mesh.shape["batch"] == 8
    return jax.shard_map(
        functools.partial(per_device, staged=staged),
        mesh=mesh,
        in_specs=(rows, rows, rows, rows, task, task) + (plain,) * 16,
        out_specs=(rows, rows, task) + (rows,) * 15 + (plain,),
        check_vma=False,
    )
```

```python
import functools

import jax
import jax.numpy as jnp
from jax import lax
from jax.experimental import pallas as pl
from jax.experimental.pallas import tpu as pltpu
from jax.sharding import PartitionSpec as P

HD = 64
TILE = 256
ALL_AXES = ("task", "batch")
NN = (((1,), (0,)), ((), ()))
NT = (((1,), (1,)), ((), ()))
TN = (((0,), (0,)), ((), ()))
half = jnp.bfloat16
single = jnp.float32
eps_norm = 1e-12


def dot(left, right, dims=NN):
    return lax.dot_general(left, right, dims, preferred_element_type=single)


ANY = pl.BlockSpec(memory_space=pl.ANY)
SMEM = pl.BlockSpec(memory_space=pltpu.SMEM)
VMEM = pl.BlockSpec(memory_space=pltpu.VMEM)
HBM = pl.BlockSpec(memory_space=pltpu.HBM)


def near(shape, dtype=single):
    return pltpu.VMEM(shape, dtype)


def far(shape, dtype=single):
    return jax.ShapeDtypeStruct(shape, dtype)


def call(kernel, name, inputs, outputs, scratch=(), megabytes=7, aliases=None, us=1):
    specs = {"v": VMEM, "s": SMEM, "a": ANY, "h": HBM}
    spaces = {"v": pltpu.VMEM, "h": pltpu.HBM}
    arrays = [
        pltpu.with_memory_space_constraint(x, spaces[p]) if p in spaces and (x.ndim > 1 or p == "h") else x for x, p in inputs
    ]
    return pl.pallas_call(
        kernel,
        in_specs=[specs[p] for _, p in inputs],
        out_specs=[specs[p] for _, p in outputs],
        out_shape=[o for o, _ in outputs],
        scratch_shapes=list(scratch),
        input_output_aliases=aliases or {},
        compiler_params=pltpu.CompilerParams(vmem_limit_bytes=megabytes << 20),
        cost_estimate=pl.CostEstimate(flops=us * 10**9, bytes_accessed=1024, transcendentals=0),
        name=name,
    )(*arrays)


def at(index, size):
    return pl.ds(pl.multiple_of(index * size, size), size)


def as_row(ref):
    return ref[...].astype(single).reshape(1, -1)


def pair_operands(q, k, parity, dead, scale):
    rows = q.shape[0]
    lane = lax.broadcasted_iota(jnp.int32, (rows, 128), 1)
    inside = (lane // HD) == parity
    spare = lane == HD * (1 - parity)
    q_one = jnp.where(inside, q.astype(single) * scale, jnp.where(spare, 1.0, 0.0)).astype(half)
    k_one = jnp.where(inside, k.astype(single), jnp.where(spare & dead, -1e30, 0.0)).astype(half)
    return q_one, k_one


def attention_kernel(
    n_ref, x_hbm, wq_hbm, wk_hbm, wv_hbm, bq_hbm, bv_hbm, wo_hbm, wi_hbm, wd_hbm, cot_hbm,
    x_ref, q_hbm, k_hbm, v_hbm, ctx_ref, ctxt_ref, lse_ref, wo_ref, wi_ref, wd_ref, cot_ref,
    q_ref, k_ref, v_ref, wq_ref, wk_ref, wv_ref, bq_vmem, bv_vmem, sems, out_sems,
    *, length,
):
    rows, width = x_ref.shape
    pairs = (
        (x_hbm, x_ref), (bq_hbm, bq_vmem), (bv_hbm, bv_vmem),
        (wq_hbm, wq_ref), (wk_hbm, wk_ref), (wv_hbm, wv_ref),
        (wo_hbm, wo_ref), (wi_hbm, wi_ref), (wd_hbm, wd_ref), (cot_hbm, cot_ref),
    )
    copies = [pltpu.make_async_copy(src, dst, sems.at[i]) for i, (src, dst) in enumerate(pairs)]
    for copy in copies:
        copy.start()
    for copy in copies[:3]:
        copy.wait()
    zero = jnp.zeros((1, width), single)
    leaving = []
    for i, (copy, w_ref, bias, out, out_hbm) in enumerate((
        (copies[3], wq_ref, as_row(bq_vmem), q_ref, q_hbm),
        (copies[4], wk_ref, zero, k_ref, k_hbm),
        (copies[5], wv_ref, as_row(bv_vmem), v_ref, v_hbm),
    )):
        copy.wait()

        @pl.loop(0, rows // TILE)
        def _(i):
            tile = at(i, TILE)
            out[tile, :] = (dot(x_ref[tile, :], w_ref[...]) + bias).astype(half)

        leaving.append(pltpu.make_async_copy(out, out_hbm, out_sems.at[i]))
        leaving[-1].start()

    quads = width // 256

    @pl.loop(0, (rows // length) * quads)
    def _(step):
        seq, quad = step // quads, step % quads
        tokens, cols = at(seq, length), at(quad, 256)
        dead = lax.broadcasted_iota(jnp.int32, (length, 128), 0) >= n_ref[seq]
        q, k, v = q_ref[tokens, cols], k_ref[tokens, cols], v_ref[tokens, cols]
        vt = v.T
        scores = []
        for h in range(4):
            pair = slice(h // 2 * 128, h // 2 * 128 + 128)
            q_one, k_one = pair_operands(q[:, pair], k[:, pair], h % 2, dead, HD**-0.5)
            scores.append(dot(k_one, q_one, NT))
        weights = []
        for s in scores:
            top = jnp.max(s, axis=0, keepdims=True)
            e = jnp.exp(s - top)
            weights.append((e.astype(half), top, jnp.sum(e, axis=0, keepdims=True)))
        parts = []
        for h, (e, top, total) in enumerate(weights):
            parts.append((dot(vt[h * HD : (h + 1) * HD], e) * (1.0 / total)).astype(half))
            lse_ref[step, h : h + 1, :] = top + jnp.log(total)
        ctxt = jnp.concatenate(parts, axis=0)
        ctxt_ref[cols, tokens] = ctxt
        ctx_ref[tokens, cols] = ctxt.T

    for copy in copies[6:] + leaving:
        copy.wait()


def attention(tokens, lengths, wq, wk, wv, bq, bv, wo, wi, wd, cot):
    seqs, length, width = tokens.shape
    rows = seqs * length
    flat = (rows, width)
    quads = width // 256
    return call(
        functools.partial(attention_kernel, length=length),
        "attention_forward",
        [(lengths, "s"), (tokens.reshape(flat), "h"), (wq, "h"), (wk, "h"), (wv, "h"), (bq, "h"), (bv, "h")]
        + [(wo, "h"), (wi, "h"), (wd, "h"), (cot.reshape(flat), "h")],
        [(near(flat, half), "v")]
        + [(far(flat, half), "a")] * 3
        + [(near(flat, half), "v"), (near((width, rows), half), "v"), (near((seqs * quads, 8, length)), "v")]
        + [(near(w.shape, half), "v") for w in (wo, wi, wd)]
        + [(near(flat, half), "v")],
        [pltpu.VMEM(flat, half)] * 3
        + [pltpu.VMEM(w.shape, half) for w in (wq, wk, wv, bq, bv)]
        + [pltpu.SemaphoreType.DMA((10,)), pltpu.SemaphoreType.DMA((3,))],
        18,
    )


def norm_parts(resid):
    center = resid - jnp.mean(resid, axis=-1, keepdims=True)
    inv_root = lax.rsqrt(jnp.mean(center * center, axis=-1, keepdims=True) + eps_norm)
    return center * inv_root, inv_root


def norm_back(grad_out, normed, inv_root, gain):
    scaled = grad_out * gain
    return inv_root * (
        scaled
        - jnp.mean(scaled, axis=-1, keepdims=True)
        - normed * jnp.mean(scaled * normed, axis=-1, keepdims=True)
    )


def gelu_parts(u):
    bell = jnp.exp(u * u * -0.5)
    t = 1.0 / (1.0 + jnp.abs(u) * (0.3275911 * 0.7071067811865476))
    series = 0.5 * 1.061405429
    for c in (-1.453152027, 1.421413741, -0.284496736, 0.254829592):
        series = series * t + 0.5 * c
    below = series * t * bell
    cdf = jnp.where(u < 0.0, below, 1.0 - below)
    return u * cdf, cdf + u * bell * 0.3989422804014327


def column_sum(array):
    return jnp.sum(array, axis=0, keepdims=True)


def middle_kernel(
    task_ref, label_ref, weight_ref, x_ref, ctx_ref, cot_ref, wo_ref, wi_ref, wd_ref,
    bo_ref, g1_ref, b1_ref, bi_ref, bd_ref, g2_ref, b2_ref, head_ref,
    out_hbm, normed1_ref, root1_ref, h1t_ref, act_ref, slope_ref, ddown_ref, sums_ref,
    out_ref, sems,
    *, length, group_seqs,
):
    rows, width = x_ref.shape
    ff = wi_ref.shape[1]
    part = 768
    bo, g1, b1, bd, g2, b2 = [as_row(r) for r in (bo_ref, g1_ref, b1_ref, bd_ref, g2_ref, b2_ref)]
    bi = as_row(bi_ref)
    w = weight_ref[0]
    table = head_ref[...].astype(single)
    chosen = lax.broadcasted_iota(jnp.int32, table.shape, 1) == task_ref[0]
    head = jnp.sum(jnp.where(chosen, table, 0.0), axis=1)
    classes = head.shape[0]
    sums_ref[...] = jnp.zeros_like(sums_ref)

    @pl.loop(0, rows // TILE)
    def _(step):
        tile = at(step, TILE)
        x = x_ref[tile, :].astype(single)
        normed1, root1 = norm_parts(x + dot(ctx_ref[tile, :], wo_ref[...]) + bo)
        normed1_ref[tile, :] = normed1.astype(half)
        root1_ref[tile, :] = jnp.broadcast_to(root1, (TILE, 128))
        hidden1 = normed1 * g1 + b1
        h1 = hidden1.astype(half)
        h1t_ref[:, tile] = h1.T

        def inner_part(j):
            return dot(h1, wi_ref[:, j : j + part]) + bi[:, j : j + part]

        down = None
        following = inner_part(0)
        for j in range(0, ff, part):
            inner = following
            if j + part < ff:
                following = inner_part(j + part)
            value, slope = gelu_parts(inner)
            act = value.astype(half)
            act_ref[tile, j : j + part] = act
            slope_ref[tile, j : j + part] = slope.astype(half)
            term = dot(act, wd_ref[j : j + part, :])
            down = term if down is None else down + term
        normed2, root2 = norm_parts(hidden1 + down + bd)
        final = normed2 * g2 + b2
        low = final.astype(half)
        out_ref[tile, :] = low
        pltpu.make_async_copy(out_ref.at[tile, :], out_hbm.at[tile, :], sems.at[step]).start()
        cls = low[0:1].astype(single)
        logits = [jnp.sum(cls * head[c : c + 1], axis=1, keepdims=True) for c in range(classes)]
        top = functools.reduce(jnp.maximum, logits)
        lse = top + jnp.log(sum(jnp.exp(v - top) for v in logits))
        per_seq = length // TILE
        label = label_ref[step // per_seq]
        first = jnp.where(step % per_seq == 0, 1.0, 0.0)
        picked = sum(jnp.where(label == c, v, 0.0) for c, v in enumerate(logits))
        slopes = [
            (jnp.exp(v - lse) - jnp.where(label == c, 1.0, 0.0)) * (w / group_seqs * first)
            for c, v in enumerate(logits)
        ]
        d_cls = sum(s * head[c : c + 1] for c, s in enumerate(slopes))
        row = lax.broadcasted_iota(jnp.int32, final.shape, 0)
        d_final = cot_ref[tile, :].astype(single) * w + jnp.where(row == 0, d_cls, 0.0)
        dr2 = norm_back(d_final, normed2, root2, g2)
        ddown = dr2.astype(half)
        ddown_ref[tile, :] = ddown
        sums_ref[0:1] += column_sum(d_final * normed2)
        sums_ref[1:2] += column_sum(d_final)
        sums_ref[2:3] += column_sum(ddown.astype(single))
        for c in range(classes):
            sums_ref[3 + c : 4 + c] += slopes[c] * cls
        sums_ref[7:8] += jnp.broadcast_to((lse - picked) * (w / group_seqs * first), cls.shape)

    for i in range(rows // TILE):
        tile = pl.ds(i * TILE, TILE)
        pltpu.make_async_copy(out_ref.at[tile, :], out_hbm.at[tile, :], sems.at[i]).wait()


def middle(x, ctx, cot, length, labels, task_ids, task_weights, wo, wi, wd, vectors, head_table, group_seqs):
    rows, width = x.shape
    ff = wi.shape[1]
    assert head_table.shape[0] <= 4
    flat = (rows, width)
    return call(
        functools.partial(middle_kernel, length=length, group_seqs=group_seqs),
        "middle_forward",
        [(task_ids, "s"), (labels, "s"), (task_weights, "s")]
        + [(a, "v") for a in (x, ctx, cot, wo, wi, wd, *vectors, head_table)],
        [(far(flat, half), "a")]
        + [
            (near(flat, half), "v"),
            (near((rows, 128)), "v"),
            (near((width, rows), half), "v"),
            (near((rows, ff), half), "v"),
            (near((rows, ff), half), "v"),
            (near(flat, half), "v"),
            (near((8, width)), "v"),
        ],
        [pltpu.VMEM(flat, half), pltpu.SemaphoreType.DMA((rows // TILE,))],
        8,
    )


def inner_grad_kernel(after_ref, ddown_ref, wd_ref, slope_ref, dinner_ref, bias_ref):
    part = 768

    @pl.loop(0, wd_ref.shape[0] // part)
    def _(j):
        cols = at(j, part)
        d = dot(ddown_ref[...], wd_ref[cols, :], NT) * slope_ref[:, cols].astype(single)
        low = d.astype(half)
        dinner_ref[:, cols] = low
        bias_ref[pl.ds(j, 1), :] = column_sum(low.astype(single))


def inner_grad(after, ddown, wd, slope):
    ff, width = wd.shape
    return call(
        inner_grad_kernel,
        "inner_grad",
        [(after, "a"), (ddown, "v"), (wd, "v"), (slope, "v")],
        [(near(slope.shape, half), "v"), (near((ff // width, width)), "v")],
        aliases={3: 0},
        us=6,
    )


def first_norm_kernel(
    pos_ref, after_ref, dinner_ref, wi_ref, ddown_ref, normed1_ref, root1_ref, wo_ref, ctxt_ref, g1_ref, x_ref,
    dr1_ref, dctx_ref, xt_ref, send_ref, keep_ref, sums_ref, dattn_ref,
):
    rows, width = dr1_ref.shape
    g1 = as_row(g1_ref)
    sums_ref[...] = jnp.zeros_like(sums_ref)

    @pl.loop(0, rows // TILE)
    def _(step):
        tile = at(step, TILE)
        normed1 = normed1_ref[tile, :].astype(single)
        dh1 = ddown_ref[tile, :].astype(single) + dot(dinner_ref[tile, :], wi_ref[...], NT)
        dr1 = norm_back(dh1, normed1, root1_ref[tile, 0:1], g1)
        dr1_ref[tile, :] = dr1
        dattn = dr1.astype(half)
        dattn_ref[tile, :] = dattn
        dctx_ref[tile, :] = dot(dattn, wo_ref[...], NT).astype(half)
        xt_ref[:, tile] = x_ref[tile, :].T
        sums_ref[0:1] += column_sum(dh1 * normed1)
        sums_ref[1:2] += column_sum(dh1)
        sums_ref[2:3] += column_sum(dattn.astype(single))

    me = pos_ref[1]
    quarter = width // 4
    for y in range(2):
        to = slice(y * quarter, (y + 1) * quarter)
        send_ref[to, :] = dot(ctxt_ref[at(2 * y + 1 - me, quarter), :], dattn_ref[...])
        keep_ref[to, :] = dot(ctxt_ref[at(2 * y + me, quarter), :], dattn_ref[...])


def first_norm(pos, after, dinner, wi, ddown, normed1, root1, wo, ctxt, g1, x):
    rows, width = ddown.shape
    flat = (rows, width)
    part = (width // 2, width)
    return call(
        first_norm_kernel,
        "first_norm_back",
        [(pos, "s"), (after, "a")]
        + [(a, "v") for a in (dinner, wi, ddown, normed1, root1, wo, ctxt, g1, x)],
        [(near(flat), "v"), (near(flat, half), "v"), (near((width, rows), half), "v")]
        + [(near(part), "v"), (near(part), "v"), (near((8, width)), "v")],
        [pltpu.VMEM(flat, half)],
        us=12,
    )


def attention_back_kernel(
    n_ref, after_ref, q_ref, k_ref, v_ref, ctx_ref, dctx_ref, lse_ref, dq_ref, dk_ref, dv_ref, sums_ref,
    *, length, quad,
):
    scale = HD**-0.5
    quads = q_ref.shape[1] // 256
    cols = slice(quad * 256, quad * 256 + 256)
    sums_ref[...] = jnp.zeros_like(sums_ref)

    @pl.loop(0, q_ref.shape[0] // length)
    def _(seq):
        tokens = at(seq, length)
        dead = lax.broadcasted_iota(jnp.int32, (length, 128), 0) >= n_ref[seq]
        low_half = lax.broadcasted_iota(jnp.int32, (length, 128), 1) < HD
        q, k, v, dctx = [r[tokens, cols] for r in (q_ref, k_ref, v_ref, dctx_ref)]
        kt = k.T
        prod_t = (ctx_ref[tokens, cols].astype(single) * dctx.astype(single)).T
        dqt = []
        for pair in range(2):
            side = slice(pair * 128, pair * 128 + 128)
            q_pair, k_pair, v_pair, d_pair = q[:, side], k[:, side], v[:, side], dctx[:, side]
            first = []
            for parity in range(2):
                q_one, k_one = pair_operands(q_pair, k_pair, parity, dead, scale)
                inside = low_half if parity == 0 else ~low_half
                v_one = jnp.where(inside, v_pair.astype(single), 0.0).astype(half)
                first.append((dot(k_one, q_one, NT), dot(v_one, d_pair, NT)))
            dks, dvs = [], []
            for parity, (s, dp) in enumerate(first):
                h = pair * 2 + parity
                p = jnp.exp(s - lse_ref[seq * quads + quad, h : h + 1, :])
                delta = jnp.sum(prod_t[h * HD : (h + 1) * HD], axis=0, keepdims=True)
                ds = (p * (dp - delta)).astype(half)
                dvs.append(dot(p.astype(half), d_pair))
                dks.append(dot(ds, q_pair))
                dqt.append((dot(kt[h * HD : (h + 1) * HD], ds) * scale).astype(half))
            dk_ref[tokens, side] = (jnp.where(low_half, dks[0], dks[1]) * scale).astype(half)
            dv = jnp.where(low_half, dvs[0], dvs[1]).astype(half)
            dv_ref[tokens, side] = dv
            sums_ref[1:2, side] += column_sum(dv.astype(single))
        dq = jnp.concatenate(dqt, axis=0).T
        dq_ref[tokens, :] = dq
        sums_ref[0:1, :] += column_sum(dq.astype(single))


def attention_back(lengths, after, q, k, v, ctx, dctx, lse, length, quad):
    rows = q.shape[0]
    return call(
        functools.partial(attention_back_kernel, length=length, quad=quad),
        f"attention_back_{quad}",
        [(lengths, "s"), (after, "a")] + [(a, "v") for a in (q, k, v, ctx, dctx, lse)],
        [(near((rows, 256), half), "v")] * 3 + [(near((8, 256)), "v")],
        us=6,
    )


def outer_half(me, act_ref, ddown_ref, y):
    part = act_ref.shape[1] // 4
    return dot(act_ref[:, at(2 * y + me, part)], ddown_ref[...], TN)


def outer_send_kernel(pos_ref, act_ref, ddown_ref, send_ref, *, other):
    me = 1 - pos_ref[1] if other else pos_ref[1]
    for y in range(2):
        send_ref[y] = outer_half(me, act_ref, ddown_ref, y)


def outer_send(pos, act, ddown, other):
    width = ddown.shape[1]
    return call(
        functools.partial(outer_send_kernel, other=other),
        "outer_weight_send",
        [(pos, "s"), (act, "v"), (ddown, "v")],
        [(near((2, act.shape[1] // 4, width)), "v")],
        us=3,
    )[0]


def split_x(pos, block, rows, cols, lead, sx, kx, to):
    me = pos[2]
    for z in range(4):
        zero = block[(2 * z) * rows : (2 * z + 1) * rows, cols]
        one = block[(2 * z + 1) * rows : (2 * z + 2) * rows, cols]
        sx[lead + (z, slice(None), to)] = jnp.where(me == 0, one, zero)
        kx[lead + (z, slice(None), to)] = jnp.where(me == 0, zero, one)


def split_z(pos, block, rows, cols, lead, sz, kz, to):
    side = pos[3]
    for x in range(2):
        zs = [block[(2 * z + x) * rows : (2 * z + x + 1) * rows, cols] for z in range(4)]
        for hi, (even, odd) in enumerate(((0, 1), (3, 2))):
            sz[lead + (hi, x, slice(None), to)] = jnp.where(side == 0, zs[odd], zs[even])
            kz[lead + (hi, x, slice(None), to)] = jnp.where(side == 0, zs[even], zs[odd])


def split_y(pos, data, rows, sy, ky, to):
    me = pos[0]
    zero = data[: 8 * rows].reshape(4, 2, rows, data.shape[1])
    one = data[8 * rows :].reshape(4, 2, rows, data.shape[1])
    sy[:, :, :, to] = jnp.where(me == 0, one, zero)
    ky[:, :, :, to] = jnp.where(me == 0, zero, one)


def outer_keep_kernel(
    pos_ref, after_ref, act_ref, ddown_ref, got_ref, sx_ref, kx_ref, sy_ref, ky_ref, sz_ref, kz_ref
):
    third = ddown_ref.shape[1] // 3
    mids = []
    for y in range(2):
        block = outer_half(pos_ref[1], act_ref, ddown_ref, y) + got_ref[y]
        rows = block.shape[0] // 8
        split_x(pos_ref, block, rows, slice(0, third), (y,), sx_ref, kx_ref, slice(None))
        split_z(pos_ref, block, rows, slice(2 * third, 3 * third), (y,), sz_ref, kz_ref, slice(None))
        mids.append(block[:, third : 2 * third])
    split_y(pos_ref, jnp.concatenate(mids, axis=0), rows, sy_ref, ky_ref, slice(None))


def outer_keep(pos, after, act, ddown, got):
    width = ddown.shape[1]
    r, third = act.shape[1] // 32, width // 3
    shapes = [(2, 4, r, third)] * 2 + [(4, 2, r, third)] * 2 + [(2, 2, 2, r, third)] * 2
    return call(
        outer_keep_kernel,
        "outer_weight_keep",
        [(pos, "s"), (after, "a"), (act, "v"), (ddown, "v"), (got, "v")],
        [(near(s), "v") for s in shapes],
    )


def row_half(left_ref, me):
    quarter = left_ref.shape[0] // 4
    return jnp.concatenate([left_ref[at(me, quarter), :], left_ref[at(2 + me, quarter), :]], axis=0)


def inner_send_kernel(pos_ref, after_ref, left_ref, right_ref, send_ref, *, other):
    me = 1 - pos_ref[1] if other else pos_ref[1]
    left = row_half(left_ref, me)
    parts, _, columns = send_ref.shape
    for j in range(parts):
        send_ref[j] = dot(left, right_ref[:, j * columns : (j + 1) * columns])


def inner_send(pos, after, left_t, right, other):
    width = left_t.shape[0]
    return call(
        functools.partial(inner_send_kernel, other=other),
        "inner_weight_send",
        [(pos, "s"), (after, "a"), (left_t, "v"), (right, "v")],
        [(near((2, width // 2, right.shape[1] // 2)), "v")],
        us=3,
    )[0]


def inner_keep_kernel(
    pos_ref, after_ref, left_ref, right_ref, got_ref, okeep_ref, ogot_ref, sx_ref, kx_ref, sy_ref, ky_ref
):
    left = row_half(left_ref, pos_ref[1])
    count, columns = got_ref.shape[1:]
    rows = count // 16
    out_half = okeep_ref.shape[1] // 2
    most, rest = slice(0, columns), slice(columns, columns + out_half)

    def block(j):
        return dot(left, right_ref[:, j * columns : (j + 1) * columns]) + got_ref[j]

    def both_x(data, to):
        for y in range(2):
            sub = slice(y * 8 * rows, (y + 1) * 8 * rows)
            split_x(pos_ref, data[sub], rows, slice(None), (y,), sx_ref, kx_ref, to)

    both_x(block(0), most)
    both_x(okeep_ref[:, :out_half] + ogot_ref[:, :out_half], rest)
    split_y(pos_ref, block(1), rows, sy_ref, ky_ref, most)
    split_y(pos_ref, okeep_ref[:, out_half:] + ogot_ref[:, out_half:], rows, sy_ref, ky_ref, rest)


def inner_keep(pos, after, left_t, right, got, out_keep, out_got):
    width = left_t.shape[0]
    r = width // 32
    wide = right.shape[1] // 2 + out_keep.shape[1] // 2
    shapes = [(2, 4, r, wide)] * 2 + [(4, 2, r, wide)] * 2
    return call(
        inner_keep_kernel,
        "inner_weight_keep",
        [(pos, "s"), (after, "a")] + [(a, "v") for a in (left_t, right, got, out_keep, out_got)],
        [(near(s), "v") for s in shapes],
        us=3,
    )


SMALL = 40


def small_rows(pos_ref, task_ref, sums0, sums1, inner_bias, sums2, classes, tables, out, base):
    quads = len(sums0)
    width = out.shape[1]
    out[base : base + SMALL, :] = jnp.zeros((SMALL, width), single)
    for g in range(quads):
        out[base : base + 2, g * 256 : (g + 1) * 256] = sums0[g][0:2]
    out[base + 2 : base + 5, :] = sums1[0:3]
    at_row = base + 5 + inner_bias.shape[0]
    out[base + 5 : at_row, :] = inner_bias[...]
    out[at_row : at_row + 3, :] = sums2[0:3]
    lane = lax.broadcasted_iota(jnp.int32, (1, width), 1)
    out[at_row + 3 : at_row + 4, :] = jnp.where(lane == pos_ref[6], sums2[7:8], 0.0)
    for t in range(tables):
        mine = jnp.where(task_ref[0] == t, 1.0, 0.0)
        first = at_row + 4 + t * classes
        out[first : first + classes, :] = sums2[3 : 3 + classes] * mine


def qkv_send_kernel(pos_ref, task_ref, after_ref, left_ref, *refs, other, classes, tables, quads):
    parts, refs = refs[: 3 * quads], refs[3 * quads :]
    sums0, refs = refs[:quads], refs[quads:]
    sums1, inner_bias, sums2, send_ref = refs
    me = 1 - pos_ref[1] if other else pos_ref[1]
    left = row_half(left_ref, me)
    count = left.shape[0]
    for t in range(3):
        for g in range(quads):
            send_ref[t * count : (t + 1) * count, g * 256 : (g + 1) * 256] = dot(left, parts[g * 3 + t][...])
    small_rows(pos_ref, task_ref, sums0, sums1, inner_bias, sums2, classes, tables, send_ref, 3 * count)


def qkv_send(pos, task_ids, after, xt, parts, sums0, sums1, inner_bias, sums2, classes, tables, other):
    width = xt.shape[0]
    assert 5 + inner_bias.shape[0] + 4 + classes * tables <= SMALL
    return call(
        functools.partial(qkv_send_kernel, other=other, classes=classes, tables=tables, quads=len(sums0)),
        "qkv_weight_send",
        [(pos, "s"), (task_ids, "s"), (after, "a"), (xt, "v")]
        + [(p, "v") for p in (*parts, *sums0, sums1, inner_bias, sums2)],
        [(near((3 * (width // 2) + SMALL, width)), "v")],
        us=3,
    )[0]


def rows24(index, r):
    return pl.ds(pl.multiple_of(index * r, 8), r)


def qkv_keep_kernel(pos_ref, after_ref, left_ref, own_ref, got_ref, *refs):
    *parts, sx, kx, sy, ky, sz, kz, small = refs
    left = row_half(left_ref, pos_ref[1])
    quads = len(parts) // 3
    count, width = left.shape[0], got_ref.shape[1]
    r = width // 32
    me_y, me_x, side = pos_ref[0], pos_ref[2], pos_ref[3]

    def grad(t):
        mine = jnp.concatenate([dot(left, parts[g * 3 + t][...]) for g in range(quads)], axis=1)
        return mine + got_ref[t * count : (t + 1) * count, :]

    total = own_ref[3 * count :, :] + got_ref[3 * count :, :]
    small[...] = total
    sx[8 * r :, :] = total
    g = grad(0)
    for y in range(2):
        for z in range(4):
            begin = (y * 8 + z * 2) * r
            zero, one = g[begin : begin + r], g[begin + r : begin + 2 * r]
            to = slice((y * 4 + z) * r, (y * 4 + z + 1) * r)
            sx[to, :] = jnp.where(me_x == 0, one, zero)
            kx[to, :] = jnp.where(me_x == 0, zero, one)
    g = grad(1)
    sy[...] = jnp.where(me_y == 0, g[8 * r :], g[: 8 * r])
    ky[...] = jnp.where(me_y == 0, g[: 8 * r], g[8 * r :])
    g = grad(2)
    for y in range(2):
        for x in range(2):
            zs = [g[(y * 8 + z * 2 + x) * r : (y * 8 + z * 2 + x + 1) * r] for z in range(4)]
            for hi, (even, odd) in enumerate(((0, 1), (3, 2))):
                begin = ((y * 2 + hi) * 2 + x) * r
                sz[begin : begin + r, :] = jnp.where(side == 0, zs[odd], zs[even])
                kz[begin : begin + r, :] = jnp.where(side == 0, zs[even], zs[odd])


def qkv_keep(pos, after, xt, own, got, parts):
    width = xt.shape[0]
    r = width // 32
    shapes = [8 * r + SMALL] + [8 * r] * 5 + [SMALL]
    return call(
        qkv_keep_kernel,
        "qkv_weight_keep",
        [(pos, "s"), (after, "a"), (xt, "v"), (own, "v"), (got, "v")] + [(p, "v") for p in parts],
        [(near((n, width)), "v") for n in shapes],
        us=3,
    )


def second_qkv_kernel(pos_ref, after_ref, kx, rx, ky, ry, kz, rz, small, xs, xk, ys, yk, zs, zk, small_out):
    me_y, me_x, me_hi = pos_ref[0], pos_ref[2], pos_ref[4]
    r = kx.shape[0] // 8
    total = small[...] + rx[8 * r :, :]
    small_out[...] = total
    xs[4 * r :, :] = total
    there, here = rows24(1 - me_y, 4 * r), rows24(me_y, 4 * r)
    xs[: 4 * r, :] = kx[there, :] + rx[there, :]
    xk[...] = kx[here, :] + rx[here, :]
    for z in range(4):
        there, here = rows24(2 * z + 1 - me_x, r), rows24(2 * z + me_x, r)
        to = slice(z * r, (z + 1) * r)
        ys[to, :] = ky[there, :] + ry[there, :]
        yk[to, :] = ky[here, :] + ry[here, :]
    for y in range(2):
        there, here = rows24(2 * y + 1 - me_hi, 2 * r), rows24(2 * y + me_hi, 2 * r)
        to = slice(y * 2 * r, (y + 1) * 2 * r)
        zs[to, :] = kz[there, :] + rz[there, :]
        zk[to, :] = kz[here, :] + rz[here, :]


def third_qkv_kernel(pos_ref, after_ref, xk, xr, yk, yr, zk, zr, small, sent, kept, zs, zn, small_out):
    me_x, side = pos_ref[2], pos_ref[3]
    r = xk.shape[0] // 4
    total = small[...] + xr[4 * r :, :]
    small_out[...] = total
    sent[4 * r :, :] = total
    for i, (k, got) in enumerate(((xk, xr), (yk, yr))):
        for hi, (keep, send) in enumerate(((side, 1 - side), (3 - side, 2 + side))):
            there, here = rows24(send, r), rows24(keep, r)
            to = slice((2 * i + hi) * r, (2 * i + hi + 1) * r)
            sent[to, :] = k[there, :] + got[there, :]
            kept[to, :] = k[here, :] + got[here, :]
    for y in range(2):
        there, here = rows24(2 * y + 1 - me_x, r), rows24(2 * y + me_x, r)
        to = slice(y * r, (y + 1) * r)
        zs[to, :] = zk[there, :] + zr[there, :]
        zn[to, :] = zk[here, :] + zr[here, :]


def fourth_qkv_kernel(pos_ref, after_ref, k, got, zk, zr, small, sent, kept, zs, zn, small_out):
    me_y, me_hi = pos_ref[0], pos_ref[4]
    r = k.shape[0] // 4
    total = small[...] + got[4 * r :, :]
    small_out[...] = total
    sent[2 * r :, :] = total
    for i in range(2):
        there, here = rows24(2 * i + 1 - me_hi, r), rows24(2 * i + me_hi, r)
        to = slice(i * r, (i + 1) * r)
        sent[to, :] = k[there, :] + got[there, :]
        kept[to, :] = k[here, :] + got[here, :]
    there, here = rows24(1 - me_y, r), rows24(me_y, r)
    zs[...] = zk[there, :] + zr[there, :]
    zn[...] = zk[here, :] + zr[here, :]


def qkv_stage(kernel, name, pos, after, arrays, counts):
    width = arrays[0].shape[1]
    return call(
        kernel,
        name,
        [(pos, "s"), (after, "a")] + [(a, "v") for a in arrays],
        [(near((n, width)), "v") for n in counts],
    )


def last_qkv_kernel(pos_ref, k, got, zk, zr, small, q_out, k_out, v_out, *outs, classes, bias_rows):
    *vectors, inner_out, loss_out, head_out = outs
    r = zk.shape[0]
    width = small.shape[1]
    q_out[...] = k[:r, :] + got[:r, :]
    k_out[...] = k[r:, :] + got[r : 2 * r, :]
    v_out[...] = zk[...] + zr[...]
    total = small[...] + got[2 * r :, :]
    me = pos_ref[5]
    rolled = pltpu.roll(total, lax.rem(width - me * r, width), 1)
    after = 5 + bias_rows
    for out, row in zip(vectors, (0, 1, 2, 3, 4, after, after + 1, after + 2)):
        out[...] = rolled[row : row + 1, :r]
    part = inner_out.shape[1]
    per_row = width // part
    row = lax.broadcasted_iota(jnp.int32, total.shape, 0)
    one = jnp.sum(jnp.where(row == 5 + me // per_row, total, 0.0), axis=0, keepdims=True)
    one = jnp.broadcast_to(one, (8, width))
    inner_out[...] = pltpu.roll(one, lax.rem(width - (me % per_row) * part, width), 1)[0:1, :part]
    lane = lax.broadcasted_iota(jnp.int32, (1, width), 1)
    loss_row = total[after + 3 : after + 4]
    loss_out[...] = jnp.sum(jnp.where(lane == pos_ref[6], loss_row, 0.0), axis=1, keepdims=True)
    for t in range(head_out.shape[0]):
        first = after + 4 + t * classes
        head_out[t] = total[first : first + classes]


def last_qkv(pos, k, got, zk, zr, small, classes, tables, bias_rows):
    r, width = zk.shape
    shapes = [(r, width)] * 3 + [(1, r)] * 8 + [(1, r * bias_rows), (1, 1), (tables, classes, width)]
    return call(
        functools.partial(last_qkv_kernel, classes=classes, bias_rows=bias_rows),
        "last_qkv_stage",
        [(pos, "s")] + [(a, "v") for a in (k, got, zk, zr, small)],
        [(far(s), "v") for s in shapes],
    )


def token_grad_kernel(after_ref, dr1_ref, wq_ref, wk_ref, wv_ref, *refs):
    *parts, out_hbm, done_ref, out_ref, sems = refs
    done_ref[...] = jnp.zeros_like(done_ref)
    rows = out_ref.shape[0]
    quads = len(parts) // 3

    @pl.loop(0, rows // TILE)
    def _(step):
        tile = at(step, TILE)
        total = dr1_ref[tile, :]
        for t, w_ref in enumerate((wq_ref, wk_ref, wv_ref)):
            d = jnp.concatenate([parts[g * 3 + t][tile, :] for g in range(quads)], axis=1)
            total = total + dot(d, w_ref[...], NT)
        out_ref[tile, :] = total
        pltpu.make_async_copy(out_ref.at[tile, :], out_hbm.at[tile, :], sems.at[step]).start()

    for i in range(rows // TILE):
        tile = pl.ds(i * TILE, TILE)
        pltpu.make_async_copy(out_ref.at[tile, :], out_hbm.at[tile, :], sems.at[i]).wait()


def token_grads(after, dr1, wq, wk, wv, parts):
    rows, width = dr1.shape
    return call(
        token_grad_kernel,
        "token_grad",
        [(after, "a")] + [(a, "v") for a in (dr1, wq, wk, wv, *parts)],
        [(far((rows, width)), "a"), (near((8, 128)), "v")],
        [pltpu.VMEM((rows, width), single), pltpu.SemaphoreType.DMA((rows // TILE,))],
        us=5,
    )


def second_kernel(pos_ref, after_ref, kx, rx, ky, ry, *refs):
    me_y, me_x, me_hi = pos_ref[0], pos_ref[2], pos_ref[4]
    outs = refs[len(refs) % 4 :] if len(refs) == 4 else refs[2:]
    xs, xk, ys, yk = outs[:4]
    xs[...] = kx[1 - me_y] + rx[1 - me_y]
    xk[...] = kx[me_y] + rx[me_y]
    ys[...] = ky[:, 1 - me_x] + ry[:, 1 - me_x]
    yk[...] = ky[:, me_x] + ry[:, me_x]
    if len(refs) > 4:
        kz, rz = refs[:2]
        zs, zk = outs[4:]
        zs[...] = kz[:, 1 - me_hi] + rz[:, 1 - me_hi]
        zk[...] = kz[:, me_hi] + rz[:, me_hi]


def second(pos, after, kx, rx, ky, ry, kz=None, rz=None):
    flat = (4,) + kx.shape[2:]
    inputs = [kx, rx, ky, ry]
    shapes = [flat] * 4
    if kz is not None:
        inputs += [kz, rz]
        shapes += [(2, 2) + kz.shape[3:]] * 2
    return call(
        second_kernel,
        "second_stage",
        [(pos, "s"), (after, "a")] + [(a, "v") for a in inputs],
        [(near(s), "v") for s in shapes],
    )


def third_kernel(pos_ref, after_ref, xk, xr, yk, yr, *refs):
    me_x, side = pos_ref[2], pos_ref[3]
    wide = xk.shape[2]
    if len(refs) == 2:
        sent, kept = refs
    else:
        zk, zr, sent, kept, zs, zn = refs
        zs[...] = zk[:, 1 - me_x] + zr[:, 1 - me_x]
        zn[...] = zk[:, me_x] + zr[:, me_x]
    for hi, (keep, send) in enumerate(((side, 1 - side), (3 - side, 2 + side))):
        sent[hi, :, :wide] = xk[send] + xr[send]
        sent[hi, :, wide:] = yk[send] + yr[send]
        kept[hi, :, :wide] = xk[keep] + xr[keep]
        kept[hi, :, wide:] = yk[keep] + yr[keep]


def third(pos, after, xk, xr, yk, yr, zk=None, zr=None):
    r, wide = xk.shape[1:]
    inputs = [xk, xr, yk, yr]
    shapes = [(2, r, 2 * wide)] * 2
    if zk is not None:
        inputs += [zk, zr]
        shapes += [(2,) + zk.shape[2:]] * 2
    return call(
        third_kernel,
        "third_stage",
        [(pos, "s"), (after, "a")] + [(a, "v") for a in inputs],
        [(near(s), "v") for s in shapes],
    )


def fourth_kernel(pos_ref, after_ref, xyk, xyr, *refs):
    me_y, me_hi = pos_ref[0], pos_ref[4]
    if len(refs) == 2:
        sent, kept = refs
    else:
        zk, zr, sent, kept, zs, zn = refs
        zs[...] = zk[1 - me_y] + zr[1 - me_y]
        zn[...] = zk[me_y] + zr[me_y]
    sent[...] = xyk[1 - me_hi] + xyr[1 - me_hi]
    kept[...] = xyk[me_hi] + xyr[me_hi]


def fourth(pos, after, xyk, xyr, zk=None, zr=None):
    inputs = [xyk, xyr]
    shapes = [xyk.shape[1:]] * 2
    if zk is not None:
        inputs += [zk, zr]
        shapes += [zk.shape[1:]] * 2
    return call(
        fourth_kernel,
        "fourth_stage",
        [(pos, "s"), (after, "a")] + [(a, "v") for a in inputs],
        [(near(s), "v") for s in shapes],
    )


def last_kernel(after_ref, xyk, xyr, *refs, layout):
    count = len(layout)
    outs = refs[-count - 1 : -1]
    refs[-1][...] = jnp.zeros_like(refs[-1])
    sources = [(xyk, xyr), refs[:2]]
    for out, pieces in zip(outs, layout):
        to = 0
        for source, begin, end in pieces:
            a, b = sources[source]
            out[:, to : to + end - begin] = a[:, begin:end] + b[:, begin:end]
            to += end - begin


def last(after, xyk, xyr, zk, zr, layout):
    inputs = [xyk, xyr] + ([] if zk is None else [zk, zr])
    shapes = [(xyk.shape[0], sum(e - b for _, b, e in pieces)) for pieces in layout]
    return call(
        functools.partial(last_kernel, layout=layout),
        "last_stage",
        [(after, "a")] + [(a, "v") for a in inputs],
        [(far(s), "v") for s in shapes] + [(near((8, 128)), "v")],
    )


def pair_list(change):
    pairs = []
    for y in range(2):
        for c in range(2):
            for z in range(4):
                for x in range(2):
                    py, pc, pz, px = change(y, c, z, x)
                    pairs.append((((y * 2 + c) * 4 + z) * 2 + x, ((py * 2 + pc) * 4 + pz) * 2 + px))
    return pairs


PAIRS = {
    "y": pair_list(lambda y, c, z, x: (1 - y, c, z, x)),
    "c": pair_list(lambda y, c, z, x: (y, 1 - c, z, x)),
    "x": pair_list(lambda y, c, z, x: (y, c, z, 1 - x)),
    "near": pair_list(lambda y, c, z, x: (y, c, z ^ 1, x)),
    "far": pair_list(lambda y, c, z, x: (y, c, 3 - z, x)),
}


def swap(array, name):
    return lax.ppermute(array, ALL_AXES, PAIRS[name])


def per_device(
    tokens,
    out_cot,
    lengths,
    labels,
    task_ids,
    task_weights,
    query_weight,
    key_weight,
    value_weight,
    query_bias,
    value_bias,
    output_weight,
    output_bias,
    norm1_gain,
    norm1_bias,
    inner_weight,
    inner_bias,
    outer_weight,
    outer_bias,
    norm2_gain,
    norm2_bias,
    head_table,
    *,
    staged,
):
    seqs, length, width = tokens.shape
    rows = seqs * length
    ff = inner_weight.shape[1]
    group_seqs = seqs * lax.axis_size("batch")
    task_index = lax.axis_index("task")
    batch_index = lax.axis_index("batch")
    my_y, my_c, my_z, my_x = task_index // 2, task_index % 2, batch_index // 2, batch_index % 2
    my_hi = my_z // 2
    my_side = (my_z // 2) ^ (my_z % 2)
    where = task_index * lax.axis_size("batch") + batch_index
    pos = jnp.stack([my_y, my_c, my_x, my_side, my_hi, where, task_index]).astype(jnp.int32)
    vectors = (output_bias, norm1_gain, norm1_bias, inner_bias, outer_bias, norm2_gain, norm2_bias)

    x, q, k, v, ctx, ctxt, lse, wo, wi, wd, cot = attention(
        tokens,
        lengths,
        query_weight,
        key_weight,
        value_weight,
        query_bias,
        value_bias,
        output_weight,
        inner_weight,
        outer_weight,
        out_cot,
    )
    block_out, normed1, root1, h1t, act, slope, ddown, sums2 = middle(
        x, ctx, cot, length, labels, task_ids, task_weights, wo, wi, wd, vectors, head_table.transpose(1, 0, 2), group_seqs
    )
    block_out = block_out.reshape(tokens.shape)

    classes, tables = head_table.shape[1], head_table.shape[0]
    parts, sums0 = [], []

    def back(quad, after):
        *grads, sums = attention_back(lengths, after, q, k, v, ctx, dctx, lse, length, quad)
        parts.extend(grads)
        sums0.append(sums)
        return sums

    o_send = outer_send(pos, act, ddown, True)
    if staged:
        o_got = swap(o_send, "c")
    dinner, inner_bias_sum = inner_grad(o_send, ddown, wd, slope)
    i_send = inner_send(pos, inner_bias_sum, h1t, dinner, True)
    if staged:
        i_got = swap(i_send, "c")
        osx, okx, osy, oky, osz, okz = outer_keep(pos, i_send, act, ddown, o_got)
        orx, ory, orz = swap(osx, "x"), swap(osy, "y"), swap(osz, "near")
        after = okx
    else:
        o_keep = outer_send(pos, act, ddown, False)
        after = o_keep
    dr1, dctx, xt, out_send, out_keep, sums1 = first_norm(
        pos,
        after,
        dinner,
        inner_weight,
        ddown,
        normed1,
        root1,
        output_weight,
        ctxt,
        norm1_gain,
        tokens.reshape(rows, width),
    )
    f2, mid, third_w = ff // 2, width // 2, width // 3
    if staged:
        out_got = swap(out_send, "c")
        oxs, oxk, oys, oyk, ozs, ozk = second(pos, sums1, okx, orx, oky, ory, okz, orz)
        oxr, oyr, ozr = swap(oxs, "y"), swap(oys, "x"), swap(ozs, "far")
        after = back(0, oxk)
        isx, ikx, isy, iky = inner_keep(pos, after, h1t, dinner, i_got, out_keep, out_got)
        irx, iry = swap(isx, "x"), swap(isy, "y")
        after = ikx
        osent, okept, ozs, ozk = third(pos, after, oxk, oxr, oyk, oyr, ozk, ozr)
        ogot, ozr = swap(osent, "near"), swap(ozs, "x")
        after = back(1, okept)
        osent, okept, ozs, ozk = fourth(pos, after, okept, ogot, ozk, ozr)
        ogot, ozr = swap(osent, "far"), swap(ozs, "y")
        after = back(2, okept)
        ixs, ixk, iys, iyk = second(pos, after, ikx, irx, iky, iry)
        ixr, iyr = swap(ixs, "y"), swap(iys, "x")
        qkv_s = qkv_send(
            pos, task_ids, ixk, xt, parts, sums0, sums1, inner_bias_sum, sums2, classes, tables, True
        )
        qkv_got = swap(qkv_s, "c")
        outer_s, after = last(qkv_s, okept, ogot, ozk, ozr, (((0, 0, 2 * third_w), (1, 0, third_w)),))
        token_grad, after = token_grads(after, dr1, query_weight, key_weight, value_weight, parts)
        qsx, qkx, qsy, qky, qsz, qkz, small = qkv_keep(pos, after, xt, qkv_s, qkv_got, parts)
        qrx, qry, qrz = swap(qsx, "x"), swap(qsy, "y"), swap(qsz, "near")
        isent, ikept = third(pos, small, ixk, ixr, iyk, iyr)
        igot = swap(isent, "near")
        r = width // 32
        qxs, qxk, qys, qyk, qzs, qzk, small = qkv_stage(
            second_qkv_kernel,
            "second_qkv_stage",
            pos,
            ikept,
            (qkx, qrx, qky, qry, qkz, qrz, small),
            [4 * r + SMALL] + [4 * r] * 5 + [SMALL],
        )
        qxr, qyr, qzr = swap(qxs, "y"), swap(qys, "x"), swap(qzs, "far")
        isent, ikept = fourth(pos, small, ikept, igot)
        igot = swap(isent, "far")
        qsent, qkept, qzs, qzk, small = qkv_stage(
            third_qkv_kernel,
            "third_qkv_stage",
            pos,
            ikept,
            (qxk, qxr, qyk, qyr, qzk, qzr, small),
            [4 * r + SMALL, 4 * r, 2 * r, 2 * r, SMALL],
        )
        qgot, qzr = swap(qsent, "near"), swap(qzs, "x")
        one = f2 + mid
        inner_s, output_s, after = last(
            qkept,
            ikept,
            igot,
            None,
            None,
            (((0, 0, f2), (0, one, one + f2)), ((0, f2, one), (0, one + f2, 2 * one))),
        )
        qsent, qkept, qzs, qzk, small = qkv_stage(
            fourth_qkv_kernel,
            "fourth_qkv_stage",
            pos,
            after,
            (qkept, qgot, qzk, qzr, small),
            [2 * r + SMALL, 2 * r, r, r, SMALL],
        )
        qgot, qzr = swap(qsent, "far"), swap(qzs, "y")
        query_s, key_s, value_s, *rest = last_qkv(
            pos, qkept, qgot, qzk, qzr, small, classes, tables, ff // width
        )
        vector_s = [v.reshape(-1) for v in rest[:-1]]
        head_grad = rest[-1]
    else:
        i_keep = inner_send(pos, sums1, h1t, dinner, False)
        after = i_keep
        for quad in range(width // 256):
            after = back(quad, after)
        small_of = (parts, sums0, sums1, inner_bias_sum, sums2, classes, tables)
        qkv_s = qkv_send(pos, task_ids, after, xt, *small_of, True)
        token_grad, after = token_grads(qkv_s, dr1, query_weight, key_weight, value_weight, parts)
        qkv_k = qkv_send(pos, task_ids, after, xt, *small_of, False)

        def whole_rows(sent, kept):
            both = jnp.stack([jnp.where(my_c == 0, kept, sent), jnp.where(my_c == 0, sent, kept)], axis=1)
            return both.reshape(-1, both.shape[-1])

        def scatter(grad):
            return lax.psum_scatter(grad, ALL_AXES, scatter_dimension=0, tiled=True)

        def by_rows(array):
            return array.reshape(2, -1, array.shape[-1])

        outer_s = scatter(whole_rows(o_send, o_keep))
        inner_s = scatter(
            jnp.concatenate([whole_rows(by_rows(i_send[j]), by_rows(i_keep[j])) for j in range(2)], axis=-1)
        )
        output_s = scatter(whole_rows(by_rows(out_send), by_rows(out_keep)))
        count = width // 2
        query_s, key_s, value_s = [
            scatter(whole_rows(*[by_rows(a[t * count : (t + 1) * count]) for a in (qkv_s, qkv_k)])) for t in range(3)
        ]
        small = lax.psum(qkv_s[3 * count :], ALL_AXES)
        devices = lax.axis_size("task") * lax.axis_size("batch")

        def mine(array):
            flat = array.reshape(-1)
            size = flat.shape[0] // devices
            return lax.dynamic_slice(flat, (where * size,), (size,))

        last_row = 5 + ff // width
        vector_s = [mine(small[i]) for i in (0, 1, 2, 3, 4, last_row, last_row + 1, last_row + 2)]
        vector_s.append(mine(small[5:last_row]))
        vector_s.append(lax.dynamic_slice(small, (last_row + 3, task_index), (1, 1)).reshape(1))
        head_grad = small[last_row + 4 : last_row + 4 + classes * tables].reshape(head_table.shape)
    token_grad = token_grad.reshape(tokens.shape)
    bias_q, bias_v, gain1, bias1, bias_o, gain2, bias2, bias_d, bias_i, loss = vector_s
    return (
        block_out,
        token_grad,
        loss,
        query_s,
        key_s,
        value_s,
        bias_q,
        bias_v,
        output_s,
        bias_o,
        gain1,
        bias1,
        inner_s,
        bias_i,
        outer_s,
        bias_d,
        gain2,
        bias2,
        head_grad,
    )


def solution(mesh):
    rows = P(ALL_AXES)
    plain = P()
    task = P("task")
    staged = mesh.shape["task"] == 4 and mesh.shape["batch"] == 8
    return jax.shard_map(
        functools.partial(per_device, staged=staged),
        mesh=mesh,
        in_specs=(rows, rows, rows, rows, task, task) + (plain,) * 16,
        out_specs=(rows, rows, task) + (rows,) * 15 + (plain,),
        check_vma=False,
    )
```

```python
import functools

import jax
import jax.numpy as jnp
from jax import lax
from jax.experimental import pallas as pl
from jax.experimental.pallas import tpu as pltpu
from jax.sharding import PartitionSpec as P

HD = 64
TILE = 256
ALL_AXES = ("task", "batch")
NN = (((1,), (0,)), ((), ()))
NT = (((1,), (1,)), ((), ()))
TN = (((0,), (0,)), ((), ()))
half = jnp.bfloat16
single = jnp.float32
eps_norm = 1e-12


def dot(left, right, dims=NN):
    return lax.dot_general(left, right, dims, preferred_element_type=single)


ANY = pl.BlockSpec(memory_space=pl.ANY)
SMEM = pl.BlockSpec(memory_space=pltpu.SMEM)
VMEM = pl.BlockSpec(memory_space=pltpu.VMEM)
HBM = pl.BlockSpec(memory_space=pltpu.HBM)


def near(shape, dtype=single):
    return pltpu.VMEM(shape, dtype)


def off(shape, dtype=single):
    return pltpu.HBM(shape, dtype)


def far(shape, dtype=single):
    return jax.ShapeDtypeStruct(shape, dtype)


COSTS = {
    "attention_back_0": 3000,
    "attention_back_1": 10000,
    "attention_back_2": 30,
    "first_norm_back": 3000,
    "fourth_qkv_stage": 100,
    "fourth_stage_inner": 3000,
    "fourth_stage_outer": 1000,
    "inner_grad": 3000,
    "inner_weight_keep": 1000,
    "inner_weight_send": 10000,
    "last_outer_stage": 3000,
    "last_stage": 300,
    "outer_weight_keep": 3000,
    "outer_weight_send": 1000,
    "qkv_weight_keep": 1000,
    "qkv_weight_send": 1000,
    "second_qkv_stage": 100,
    "second_stage_inner": 10000,
    "second_stage_outer": 3000,
    "sum": 10000,
    "third_outer_stage": 10000,
    "third_qkv_stage": 3000,
    "third_stage": 10000,
    "token_grad": 3000,
}
ORDER = [
    "send_outer",
    "rest_outer",
    "inner_grad",
    "send_inner",
    "keep_outer",
    "first_norm",
    "keep_inner",
    "back_0",
    "second_outer",
    "back_1",
    "second_inner",
    "back_2",
    "third_outer",
    "send_qkv",
    "keep_qkv",
    "third_inner",
    "tokens",
    "fourth_outer",
    "second_qkv",
    "sum_outer",
    "third_qkv",
    "fourth_inner",
    "fourth_qkv",
    "last_inner",
    "last_outer",
    "last_qkv",
]


def call(kernel, name, inputs, outputs, scratch=(), megabytes=7, aliases=None):
    specs = {"v": VMEM, "s": SMEM, "a": ANY, "h": HBM}
    spaces = {"v": pltpu.VMEM, "h": pltpu.HBM}
    arrays = [
        pltpu.with_memory_space_constraint(x, spaces[p]) if p in spaces and (x.ndim > 1 or p == "h") else x for x, p in inputs
    ]
    return pl.pallas_call(
        kernel,
        in_specs=[specs[p] for _, p in inputs],
        out_specs=[specs[p] for _, p in outputs],
        out_shape=[o for o, _ in outputs],
        scratch_shapes=list(scratch),
        input_output_aliases=aliases or {},
        compiler_params=pltpu.CompilerParams(vmem_limit_bytes=megabytes << 20),
        cost_estimate=pl.CostEstimate(flops=COSTS.get(name, 1) * 10**6, bytes_accessed=1024, transcendentals=0),
        name=name,
    )(*arrays)


def at(index, size):
    return pl.ds(pl.multiple_of(index * size, size), size)


def as_row(ref):
    return ref[...].astype(single).reshape(1, -1)


def pair_operands(q, k, parity, dead, scale):
    rows = q.shape[0]
    lane = lax.broadcasted_iota(jnp.int32, (rows, 128), 1)
    inside = (lane // HD) == parity
    spare = lane == HD * (1 - parity)
    q_one = jnp.where(inside, q.astype(single) * scale, jnp.where(spare, 1.0, 0.0)).astype(half)
    k_one = jnp.where(inside, k.astype(single), jnp.where(spare & dead, -1e30, 0.0)).astype(half)
    return q_one, k_one


def attention_kernel(
    n_ref, x_hbm, wq_hbm, wk_hbm, wv_hbm, bq_hbm, bv_hbm, wo_hbm, wi_hbm, wd_hbm, cot_hbm,
    x_ref, q_hbm, k_hbm, v_hbm, ctx_ref, ctxt_hbm, lse_ref, wo_ref, wi_ref, wd_ref, cot_ref,
    ctxt_ref, q_ref, k_ref, v_ref, wq_ref, wk_ref, wv_ref, bq_vmem, bv_vmem, sems, out_sems, ctxt_sems,
    *, length,
):
    rows, width = x_ref.shape
    sides = [pl.ds(i * (rows // 2), rows // 2) for i in range(2)]
    pairs = (
        (x_hbm.at[sides[0], :], x_ref.at[sides[0], :]), (bq_hbm, bq_vmem), (wq_hbm, wq_ref),
        (x_hbm.at[sides[1], :], x_ref.at[sides[1], :]), (bv_hbm, bv_vmem), (wk_hbm, wk_ref), (wv_hbm, wv_ref),
        (wo_hbm, wo_ref), (wi_hbm, wi_ref), (wd_hbm, wd_ref), (cot_hbm, cot_ref),
    )
    copies = [pltpu.make_async_copy(src, dst, sems.at[i]) for i, (src, dst) in enumerate(pairs)]
    for copy in copies[:7]:
        copy.start()
    zero = jnp.zeros((1, width), single)
    leaving = []
    for i, (waits, w_ref, bias, out, out_hbm) in enumerate((
        ((0, 1, 2), wq_ref, bq_vmem, q_ref, q_hbm),
        ((4, 5), wk_ref, None, k_ref, k_hbm),
        ((6,), wv_ref, bv_vmem, v_ref, v_hbm),
    )):
        for wait in waits:
            copies[wait].wait()
        shift = zero if bias is None else as_row(bias)
        for part, side in enumerate(sides):
            if i == 0 and part == 1:
                copies[3].wait()
            out[side, :] = (dot(x_ref[side, :], w_ref[...]) + shift).astype(half)
        if i == 0:
            for copy in copies[7:]:
                copy.start()
        leaving.append(pltpu.make_async_copy(out, out_hbm, out_sems.at[i]))
        leaving[-1].start()

    quads = width // 256

    @pl.loop(0, (rows // length) * quads)
    def _(step):
        seq, quad = step // quads, step % quads
        tokens, cols = at(seq, length), at(quad, 256)
        dead = lax.broadcasted_iota(jnp.int32, (length, 128), 0) >= n_ref[seq]
        q, k, v = q_ref[tokens, cols], k_ref[tokens, cols], v_ref[tokens, cols]
        vt = v.T
        scores = []
        for h in range(4):
            pair = slice(h // 2 * 128, h // 2 * 128 + 128)
            q_one, k_one = pair_operands(q[:, pair], k[:, pair], h % 2, dead, HD**-0.5)
            scores.append(dot(k_one, q_one, NT))
        weights = []
        for s in scores:
            top = jnp.max(s, axis=0, keepdims=True)
            e = jnp.exp(s - top)
            weights.append((e.astype(half), top, jnp.sum(e, axis=0, keepdims=True)))
        parts = []
        for h, (e, top, total) in enumerate(weights):
            parts.append((dot(vt[h * HD : (h + 1) * HD], e) * (1.0 / total)).astype(half))
            lse_ref[step, h : h + 1, :] = top + jnp.log(total)
        ctxt = jnp.concatenate(parts, axis=0)
        ctxt_ref[cols, tokens] = ctxt
        ctx_ref[tokens, cols] = ctxt.T
        pltpu.make_async_copy(ctxt_ref.at[cols, tokens], ctxt_hbm.at[cols, tokens], ctxt_sems.at[step]).start()

    for step in range((rows // length) * quads):
        seq, quad = step // quads, step % quads
        tokens, cols = pl.ds(seq * length, length), pl.ds(quad * 256, 256)
        pltpu.make_async_copy(ctxt_ref.at[cols, tokens], ctxt_hbm.at[cols, tokens], ctxt_sems.at[step]).wait()
    for copy in copies[7:] + leaving:
        copy.wait()


def attention(tokens, lengths, wq, wk, wv, bq, bv, wo, wi, wd, cot):
    seqs, length, width = tokens.shape
    rows = seqs * length
    flat = (rows, width)
    quads = width // 256
    return call(
        functools.partial(attention_kernel, length=length),
        "attention_forward",
        [(lengths, "s"), (tokens.reshape(flat), "h"), (wq, "h"), (wk, "h"), (wv, "h"), (bq, "h"), (bv, "h")]
        + [(wo, "h"), (wi, "h"), (wd, "h"), (cot.reshape(flat), "h")],
        [(near(flat, half), "v")]
        + [(off(flat, half), "h")] * 3
        + [(near(flat, half), "v"), (off((width, rows), half), "h"), (near((seqs * quads, 8, length)), "v")]
        + [(near(w.shape, half), "v") for w in (wo, wi, wd)]
        + [(near(flat, half), "v")],
        [pltpu.VMEM((width, rows), half)]
        + [pltpu.VMEM(flat, half)] * 3
        + [pltpu.VMEM(w.shape, half) for w in (wq, wk, wv, bq, bv)]
        + [pltpu.SemaphoreType.DMA((11,)), pltpu.SemaphoreType.DMA((3,))]
        + [pltpu.SemaphoreType.DMA((seqs * quads,))],
        20,
    )


def norm_parts(resid):
    center = resid - jnp.mean(resid, axis=-1, keepdims=True)
    inv_root = lax.rsqrt(jnp.mean(center * center, axis=-1, keepdims=True) + eps_norm)
    return center * inv_root, inv_root


def norm_back(grad_out, normed, inv_root, gain):
    scaled = grad_out * gain
    return inv_root * (
        scaled
        - jnp.mean(scaled, axis=-1, keepdims=True)
        - normed * jnp.mean(scaled * normed, axis=-1, keepdims=True)
    )


def gelu_parts(u):
    u = u.astype(half)
    w = u * u
    v = jnp.minimum(w, jnp.asarray(36.0, half))
    p = (v * jnp.asarray(-0.00031594874, half) + jnp.asarray(0.0367987, half)) * v + jnp.asarray(0.79771759, half)
    h = jnp.asarray(0.5, half)
    cdf = h + h * jnp.tanh(u * p)
    bell = jnp.exp2(w * jnp.asarray(-0.72134752, half) - jnp.asarray(1.32574806, half))
    return u * cdf, cdf + u * bell


def column_sum(array):
    return jnp.sum(array, axis=0, keepdims=True)


def middle_kernel(
    task_ref, label_ref, weight_ref, x_ref, ctx_ref, cot_ref, wo_ref, wi_ref, wd_ref,
    bo_ref, g1_ref, b1_ref, bi_ref, bd_ref, g2_ref, b2_ref, head_ref,
    out_hbm, normed1_ref, root1_ref, h1t_ref, act_ref, slope_ref, ddown_ref, sums_ref,
    out_ref, h1_s, hid_s, res_s, sems,
    *, length, group_seqs,
):
    rows, width = x_ref.shape
    ff = wi_ref.shape[1]
    part = 768
    bo, g1, b1, bd, g2, b2 = [as_row(r) for r in (bo_ref, g1_ref, b1_ref, bd_ref, g2_ref, b2_ref)]
    bi = as_row(bi_ref)
    w = weight_ref[0]
    table = head_ref[...].astype(single)
    chosen = lax.broadcasted_iota(jnp.int32, table.shape, 1) == task_ref[0]
    head = jnp.sum(jnp.where(chosen, table, 0.0), axis=1)
    classes = head.shape[0]
    sums_ref[...] = jnp.zeros_like(sums_ref)
    res_s[...] = jnp.zeros_like(res_s)
    tiles = rows // TILE
    per_seq = length // TILE
    pieces = ff // part
    piece = TILE // pieces

    def rows_of(step, k):
        return pl.ds(pl.multiple_of(step * TILE + k * piece, piece), piece)

    def project(step, slot):
        tile = at(step, TILE)
        hid_s[slot] = x_ref[tile, :].astype(single) + dot(ctx_ref[tile, :], wo_ref[...]) + bo

    def norm_first(step, slot, k):
        here, to = slice(k * piece, (k + 1) * piece), rows_of(step, k)
        normed1, root1 = norm_parts(hid_s[slot, here, :])
        normed1_ref[to, :] = normed1.astype(half)
        root1_ref[to, :] = jnp.broadcast_to(root1, (piece, 128))
        hidden1 = normed1 * g1 + b1
        hid_s[slot, here, :] = hidden1
        h1_s[slot, here, :] = hidden1.astype(half)

    def norm_second(step, slot, k, valid):
        here, to = slice(k * piece, (k + 1) * piece), rows_of(step, k)
        normed2, root2 = norm_parts(res_s[slot, here, :])
        final = normed2 * g2 + b2
        low = final.astype(half)
        out_ref[to, :] = low
        d_final = cot_ref[to, :].astype(single) * w
        if k == 0:
            cls = low[0:1].astype(single)
            logits = [jnp.sum(cls * head[c : c + 1], axis=1, keepdims=True) for c in range(classes)]
            top = functools.reduce(jnp.maximum, logits)
            lse = top + jnp.log(sum(jnp.exp(v - top) for v in logits))
            label = label_ref[step // per_seq]
            weight = jnp.where(step % per_seq == 0, w / group_seqs, 0.0)
            picked = sum(jnp.where(label == c, v, 0.0) for c, v in enumerate(logits))
            slopes = [
                (jnp.exp(v - lse) - jnp.where(label == c, 1.0, 0.0)) * weight for c, v in enumerate(logits)
            ]
            d_cls = sum(s * head[c : c + 1] for c, s in enumerate(slopes))
            row = lax.broadcasted_iota(jnp.int32, d_final.shape, 0)
            d_final = d_final + jnp.where(row == 0, d_cls, 0.0)
            for c in range(classes):
                sums_ref[3 + c : 4 + c] += slopes[c] * cls * valid
            sums_ref[7:8] += jnp.broadcast_to((lse - picked) * (weight * valid), cls.shape)
        ddown = norm_back(d_final, normed2, root2, g2).astype(half)
        ddown_ref[to, :] = ddown
        sums_ref[0:1] += column_sum(d_final * normed2) * valid
        sums_ref[1:2] += column_sum(d_final) * valid
        sums_ref[2:3] += column_sum(ddown.astype(single)) * valid

    def leave(step):
        tile = at(step, TILE)
        return pltpu.make_async_copy(out_ref.at[tile, :], out_hbm.at[tile, :], sems.at[step])

    project(0, 0)
    for k in range(pieces):
        norm_first(0, 0, k)
    h1t_ref[:, :TILE] = h1_s[0].T

    @pl.loop(0, tiles)
    def _(step):
        slot = lax.rem(step, 2)
        tile = at(step, TILE)
        later, earlier = jnp.minimum(step + 1, tiles - 1), jnp.maximum(step - 1, 0)
        valid = jnp.where(step > 0, 1.0, 0.0)
        project(later, 1 - slot)
        h1 = h1_s[slot]

        def inner_part(j):
            return dot(h1, wi_ref[:, j : j + part]) + bi[:, j : j + part]

        down = None
        following = inner_part(0)
        for k in range(pieces):
            j = k * part
            inner = following
            if k + 1 < pieces:
                following = inner_part(j + part)
            norm_first(later, 1 - slot, k)
            value, slope = gelu_parts(inner)
            act = value.astype(half)
            act_ref[tile, j : j + part] = act
            slope_ref[tile, j : j + part] = slope.astype(half)
            norm_second(earlier, 1 - slot, k, valid)
            term = dot(act, wd_ref[j : j + part, :])
            down = term if down is None else down + term
        res_s[slot] = hid_s[slot] + down + bd
        h1t_ref[:, at(later, TILE)] = h1_s[1 - slot].T

        @pl.when(step > 0)
        def _():
            leave(earlier).start()

    for k in range(pieces):
        norm_second(tiles - 1, (tiles - 1) % 2, k, 1.0)
    leave(tiles - 1).start()
    for step in range(tiles):
        leave(step).wait()


def middle(x, ctx, cot, length, labels, task_ids, task_weights, wo, wi, wd, vectors, head_table, group_seqs):
    rows, width = x.shape
    ff = wi.shape[1]
    assert head_table.shape[0] <= 4
    flat = (rows, width)
    return call(
        functools.partial(middle_kernel, length=length, group_seqs=group_seqs),
        "middle_forward",
        [(task_ids, "s"), (labels, "s"), (task_weights, "s")]
        + [(a, "v") for a in (x, ctx, cot, wo, wi, wd, *vectors, head_table)],
        [(far(flat, half), "a")]
        + [
            (near(flat, half), "v"),
            (near((rows, 128)), "v"),
            (near((width, rows), half), "v"),
            (near((rows, ff), half), "v"),
            (near((rows, ff), half), "v"),
            (near(flat, half), "v"),
            (near((8, width)), "v"),
        ],
        [pltpu.VMEM(flat, half), pltpu.VMEM((2, TILE, width), half)]
        + [pltpu.VMEM((2, TILE, width), single)] * 2
        + [pltpu.SemaphoreType.DMA((rows // TILE,))],
        14,
    )


def inner_grad_kernel(after_ref, ddown_ref, wd_ref, slope_ref, dinner_ref, bias_ref):
    part = 768

    @pl.loop(0, wd_ref.shape[0] // part)
    def _(j):
        cols = at(j, part)
        d = dot(ddown_ref[...], wd_ref[cols, :], NT) * slope_ref[:, cols].astype(single)
        low = d.astype(half)
        dinner_ref[:, cols] = low
        bias_ref[pl.ds(j, 1), :] = column_sum(low.astype(single))


def inner_grad(after, ddown, wd, slope):
    ff, width = wd.shape
    return call(
        inner_grad_kernel,
        "inner_grad",
        [(after, "a"), (ddown, "v"), (wd, "v"), (slope, "v")],
        [(near(slope.shape, half), "v"), (near((ff // width, width)), "v")],
        aliases={3: 0},
    )


def first_norm_kernel(
    after_ref, dinner_ref, wi_ref, ddown_ref, normed1_ref, root1_ref, wo_ref, g1_ref, x_ref,
    dr1_ref, dattn_ref, dctx_ref, xt_ref, sums_ref,
):
    rows, width = dr1_ref.shape
    g1 = as_row(g1_ref)
    sums_ref[...] = jnp.zeros_like(sums_ref)

    @pl.loop(0, rows // TILE)
    def _(step):
        tile = at(step, TILE)
        normed1 = normed1_ref[tile, :].astype(single)
        dh1 = ddown_ref[tile, :].astype(single) + dot(dinner_ref[tile, :], wi_ref[...], NT)
        dr1 = norm_back(dh1, normed1, root1_ref[tile, 0:1], g1)
        dr1_ref[tile, :] = dr1
        dattn = dr1.astype(half)
        dattn_ref[tile, :] = dattn
        dctx_ref[tile, :] = dot(dattn, wo_ref[...], NT).astype(half)
        xt_ref[:, tile] = x_ref[tile, :].T
        sums_ref[0:1] += column_sum(dh1 * normed1)
        sums_ref[1:2] += column_sum(dh1)
        sums_ref[2:3] += column_sum(dattn.astype(single))


def first_norm(after, dinner, wi, ddown, normed1, root1, wo, g1, x):
    rows, width = ddown.shape
    flat = (rows, width)
    return call(
        first_norm_kernel,
        "first_norm_back",
        [(after, "a")] + [(a, "v") for a in (dinner, wi, ddown, normed1, root1, wo, g1, x)],
        [(near(flat), "v"), (near(flat, half), "v"), (near(flat, half), "v")]
        + [(near((width, rows), half), "v"), (near((8, width)), "v")],
    )


def attention_back_kernel(
    n_ref, after_ref, q_ref, k_ref, v_ref, ctx_ref, dctx_ref, lse_ref, dq_ref, dk_ref, dv_ref, sums_ref,
    *, length, quad,
):
    scale = HD**-0.5
    quads = q_ref.shape[1] // 256
    cols = slice(quad * 256, quad * 256 + 256)
    sums_ref[...] = jnp.zeros_like(sums_ref)

    @pl.loop(0, q_ref.shape[0] // length)
    def _(seq):
        tokens = at(seq, length)
        dead = lax.broadcasted_iota(jnp.int32, (length, 128), 0) >= n_ref[seq]
        low_half = lax.broadcasted_iota(jnp.int32, (length, 128), 1) < HD
        q, k, v, dctx = [r[tokens, cols] for r in (q_ref, k_ref, v_ref, dctx_ref)]
        kt = k.T
        prod_t = (ctx_ref[tokens, cols].astype(single) * dctx.astype(single)).T
        dqt = []
        for pair in range(2):
            side = slice(pair * 128, pair * 128 + 128)
            q_pair, k_pair, v_pair, d_pair = q[:, side], k[:, side], v[:, side], dctx[:, side]
            first = []
            for parity in range(2):
                q_one, k_one = pair_operands(q_pair, k_pair, parity, dead, scale)
                inside = low_half if parity == 0 else ~low_half
                v_one = jnp.where(inside, v_pair.astype(single), 0.0).astype(half)
                first.append((dot(k_one, q_one, NT), dot(v_one, d_pair, NT)))
            dks, dvs = [], []
            for parity, (s, dp) in enumerate(first):
                h = pair * 2 + parity
                p = jnp.exp(s - lse_ref[seq * quads + quad, h : h + 1, :])
                delta = jnp.sum(prod_t[h * HD : (h + 1) * HD], axis=0, keepdims=True)
                ds = (p * (dp - delta)).astype(half)
                dvs.append(dot(p.astype(half), d_pair))
                dks.append(dot(ds, q_pair))
                dqt.append((dot(kt[h * HD : (h + 1) * HD], ds) * scale).astype(half))
            dk_ref[tokens, side] = (jnp.where(low_half, dks[0], dks[1]) * scale).astype(half)
            dv = jnp.where(low_half, dvs[0], dvs[1]).astype(half)
            dv_ref[tokens, side] = dv
            sums_ref[1:2, side] += column_sum(dv.astype(single))
        dq = jnp.concatenate(dqt, axis=0).T
        dq_ref[tokens, :] = dq
        sums_ref[0:1, :] += column_sum(dq.astype(single))


def attention_back(lengths, after, q, k, v, ctx, dctx, lse, length, quad):
    rows = q.shape[0]
    return call(
        functools.partial(attention_back_kernel, length=length, quad=quad),
        f"attention_back_{quad}",
        [(lengths, "s"), (after, "a")] + [(a, "v") for a in (q, k, v, ctx, dctx, lse)],
        [(near((rows, 256), half), "v")] * 3 + [(near((8, 256)), "v")],
    )


def outer_half(me, act_ref, ddown_ref, y):
    part = act_ref.shape[1] // 4
    return dot(act_ref[:, at(2 * y + me, part)], ddown_ref[...], TN)


def outer_send_kernel(pos_ref, after_ref, act_ref, ddown_ref, send_ref, *, other):
    me = 1 - pos_ref[1] if other else pos_ref[1]
    for y in range(2):
        send_ref[y] = outer_half(me, act_ref, ddown_ref, y)


def outer_send(pos, after, act, ddown, other):
    width = ddown.shape[1]
    return call(
        functools.partial(outer_send_kernel, other=other),
        "outer_weight_send" if other else "outer_weight_rest",
        [(pos, "s"), (after, "a"), (act, "v"), (ddown, "v")],
        [(near((2, act.shape[1] // 4, width)), "v")],
    )[0]


def split_x(pos, block, rows, cols, lead, sx, kx, to):
    me = pos[2]
    for z in range(4):
        zero = block[(2 * z) * rows : (2 * z + 1) * rows, cols]
        one = block[(2 * z + 1) * rows : (2 * z + 2) * rows, cols]
        sx[lead + (z, slice(None), to)] = jnp.where(me == 0, one, zero)
        kx[lead + (z, slice(None), to)] = jnp.where(me == 0, zero, one)


def split_z(pos, block, rows, cols, lead, sz, kz, to):
    side = pos[3]
    for x in range(2):
        zs = [block[(2 * z + x) * rows : (2 * z + x + 1) * rows, cols] for z in range(4)]
        for hi, (even, odd) in enumerate(((0, 1), (3, 2))):
            sz[lead + (hi, x, slice(None), to)] = jnp.where(side == 0, zs[odd], zs[even])
            kz[lead + (hi, x, slice(None), to)] = jnp.where(side == 0, zs[even], zs[odd])


def split_y(pos, data, rows, sy, ky, to):
    me = pos[0]
    zero = data[: 8 * rows].reshape(4, 2, rows, data.shape[1])
    one = data[8 * rows :].reshape(4, 2, rows, data.shape[1])
    sy[:, :, :, to] = jnp.where(me == 0, one, zero)
    ky[:, :, :, to] = jnp.where(me == 0, zero, one)


def outer_keep_kernel(
    pos_ref, after_ref, own_ref, got_ref, sx_ref, kx_ref, sy_ref, ky_ref, sz_ref, kz_ref
):
    third = own_ref.shape[2] // 3
    rows = own_ref.shape[1] // 8
    me_y, me_x, side = pos_ref[0], pos_ref[2], pos_ref[3]
    xs, ys, zs = [slice(i * third, (i + 1) * third) for i in range(3)]

    def at_rows(y, z, x, cols):
        begin = (2 * z + x) * rows
        return own_ref[y, begin : begin + rows, cols] + got_ref[y, begin : begin + rows, cols]

    for y in range(2):
        for z in range(4):
            zero, one = at_rows(y, z, 0, xs), at_rows(y, z, 1, xs)
            sx_ref[y, z] = jnp.where(me_x == 0, one, zero)
            kx_ref[y, z] = jnp.where(me_x == 0, zero, one)
        for x in range(2):
            for hi, (even, odd) in enumerate(((0, 1), (3, 2))):
                zero, one = at_rows(y, even, x, zs), at_rows(y, odd, x, zs)
                sz_ref[y, hi, x] = jnp.where(side == 0, one, zero)
                kz_ref[y, hi, x] = jnp.where(side == 0, zero, one)
    for z in range(4):
        for x in range(2):
            zero, one = at_rows(0, z, x, ys), at_rows(1, z, x, ys)
            sy_ref[z, x] = jnp.where(me_y == 0, one, zero)
            ky_ref[z, x] = jnp.where(me_y == 0, zero, one)


def outer_keep(pos, after, own, got):
    width = own.shape[2]
    r, third = own.shape[1] // 8, width // 3
    shapes = [(2, 4, r, third)] * 2 + [(4, 2, r, third)] * 2 + [(2, 2, 2, r, third)] * 2
    return call(
        outer_keep_kernel,
        "outer_weight_keep",
        [(pos, "s"), (after, "a"), (own, "v"), (got, "v")],
        [(near(s), "v") for s in shapes],
    )


def row_half(left_ref, me):
    quarter = left_ref.shape[0] // 4
    return jnp.concatenate([left_ref[at(me, quarter), :], left_ref[at(2 + me, quarter), :]], axis=0)


def inner_send_kernel(pos_ref, after_ref, left_ref, right_ref, send_ref, *, other):
    me = 1 - pos_ref[1] if other else pos_ref[1]
    left = row_half(left_ref, me)
    parts, _, columns = send_ref.shape
    for j in range(parts):
        send_ref[j] = dot(left, right_ref[:, j * columns : (j + 1) * columns])


def inner_send(pos, after, left_t, right, other):
    width = left_t.shape[0]
    return call(
        functools.partial(inner_send_kernel, other=other),
        "inner_weight_send",
        [(pos, "s"), (after, "a"), (left_t, "v"), (right, "v")],
        [(near((2, width // 2, right.shape[1] // 2)), "v")],
    )[0]


def inner_keep_kernel(pos_ref, after_ref, left_ref, right_ref, got_ref, sx_ref, kx_ref, sy_ref, ky_ref):
    left = row_half(left_ref, pos_ref[1])
    count, columns = got_ref.shape[1:]
    rows = count // 16

    def block(j):
        return dot(left, right_ref[:, j * columns : (j + 1) * columns]) + got_ref[j]

    data = block(0)
    for y in range(2):
        sub = slice(y * 8 * rows, (y + 1) * 8 * rows)
        split_x(pos_ref, data[sub], rows, slice(None), (y,), sx_ref, kx_ref, slice(None))
    split_y(pos_ref, block(1), rows, sy_ref, ky_ref, slice(None))


def inner_keep(pos, after, left_t, right, got):
    r = left_t.shape[0] // 32
    wide = right.shape[1] // 2
    shapes = [(2, 4, r, wide)] * 2 + [(4, 2, r, wide)] * 2
    return call(
        inner_keep_kernel,
        "inner_weight_keep",
        [(pos, "s"), (after, "a")] + [(a, "v") for a in (left_t, right, got)],
        [(near(s), "v") for s in shapes],
    )


SMALL = 40


def small_rows(pos_ref, task_ref, sums0, sums1, inner_bias, sums2, classes, tables, out, base):
    quads = len(sums0)
    width = sums1.shape[1]
    lanes = slice(0, width)
    out[base : base + SMALL, :] = jnp.zeros((SMALL, out.shape[1]), single)
    for g in range(quads):
        out[base : base + 2, g * 256 : (g + 1) * 256] = sums0[g][0:2]
    out[base + 2 : base + 5, lanes] = sums1[0:3]
    at_row = base + 5 + inner_bias.shape[0]
    out[base + 5 : at_row, lanes] = inner_bias[...]
    out[at_row : at_row + 3, lanes] = sums2[0:3]
    lane = lax.broadcasted_iota(jnp.int32, (1, width), 1)
    out[at_row + 3 : at_row + 4, lanes] = jnp.where(lane == pos_ref[6], sums2[7:8], 0.0)
    for t in range(tables):
        mine = jnp.where(task_ref[0] == t, 1.0, 0.0)
        first = at_row + 4 + t * classes
        out[first : first + classes, lanes] = sums2[3 : 3 + classes] * mine


def quad_grads(me, left_ref, ctxt_ref, dattn_ref, parts, g):
    left = row_half(left_ref, me)
    pieces = [dot(left, part[...]) for part in parts[3 * g : 3 * g + 3]]
    pieces.append(dot(row_half(ctxt_ref, me), dattn_ref[:, g * 256 : (g + 1) * 256]))
    return pieces


def qkv_send_kernel(pos_ref, task_ref, after_ref, left_ref, ctxt_ref, dattn_ref, *refs, other, classes, tables, quads):
    parts, refs = refs[: 3 * quads], refs[3 * quads :]
    sums0, refs = refs[:quads], refs[quads:]
    sums1, inner_bias, sums2, send_ref = refs
    me = 1 - pos_ref[1] if other else pos_ref[1]
    count = left_ref.shape[0] // 2
    for g in range(quads):
        for t, piece in enumerate(quad_grads(me, left_ref, ctxt_ref, dattn_ref, parts, g)):
            send_ref[g * count : (g + 1) * count, t * 256 : (t + 1) * 256] = piece
    small_rows(pos_ref, task_ref, sums0, sums1, inner_bias, sums2, classes, tables, send_ref, quads * count)


def qkv_send(pos, task_ids, after, xt, ctxt, dattn, parts, sums0, sums1, inner_bias, sums2, classes, tables, other):
    width = xt.shape[0]
    assert 5 + inner_bias.shape[0] + 4 + classes * tables <= SMALL
    return call(
        functools.partial(qkv_send_kernel, other=other, classes=classes, tables=tables, quads=len(sums0)),
        "qkv_weight_send",
        [(pos, "s"), (task_ids, "s"), (after, "a"), (xt, "v"), (ctxt, "v"), (dattn, "v")]
        + [(p, "v") for p in (*parts, *sums0, sums1, inner_bias, sums2)],
        [(near((len(sums0) * (width // 2) + SMALL, 1024)), "v")],
    )[0]


def rows24_from(base, index, r):
    return pl.ds(pl.multiple_of(base + index * r, 8), r)


def rows24(index, r):
    return pl.ds(pl.multiple_of(index * r, 8), r)


def pack(out, row, block):
    r, w = block.shape[0] // 4, block.shape[1]
    for j in range(4):
        out[row : row + r, j * w : (j + 1) * w] = block[j * r : (j + 1) * r]


def third_outer_kernel(pos_ref, after_ref, xk, xr, yk, yr, zk, zr, sent, kept, zs, zn):
    me_x, side = pos_ref[2], pos_ref[3]
    wide = xk.shape[2]
    for hi, (keep, send) in enumerate(((side, 1 - side), (3 - side, 2 + side))):
        sent[hi, :, :wide] = xk[send] + xr[send]
        sent[hi, :, wide:] = yk[send] + yr[send]
        kept[hi, :, :wide] = xk[keep] + xr[keep]
        kept[hi, :, wide:] = yk[keep] + yr[keep]
    r = xk.shape[1] // 4
    for y in range(2):
        pack(zs, y * r, zk[y, 1 - me_x] + zr[y, 1 - me_x])
        pack(zn, y * r, zk[y, me_x] + zr[y, me_x])


def third_outer(pos, after, xk, xr, yk, yr, zk, zr):
    r, wide = xk.shape[1:]
    shapes = [(2, r, 2 * wide)] * 2 + [(r // 2, 4 * wide)] * 2
    return call(
        third_outer_kernel,
        "third_outer_stage",
        [(pos, "s"), (after, "a")] + [(a, "v") for a in (xk, xr, yk, yr, zk, zr)],
        [(near(s), "v") for s in shapes],
    )


def qkv_keep_kernel(pos_ref, after_ref, left_ref, ctxt_ref, dattn_ref, own_ref, got_ref, ozs, *refs):
    *parts, sx, kx, sy, ky, sz, kz, small = refs
    count, width = left_ref.shape[0] // 2, left_ref.shape[0]
    r = width // 32
    me_y, me_c, me_x, side = pos_ref[0], pos_ref[1], pos_ref[2], pos_ref[3]
    total = own_ref[3 * count :, :width] + got_ref[3 * count :, :width]
    small[...] = total
    sx[8 * r : 8 * r + SMALL, :width] = total
    sx[8 * r + SMALL :, :] = ozs[...]

    def grads(g):
        for t, piece in enumerate(quad_grads(me_c, left_ref, ctxt_ref, dattn_ref, parts, g)):
            cols = slice(t * 256, (t + 1) * 256)
            yield cols, piece + got_ref[g * count : (g + 1) * count, cols]

    for cols, g in grads(0):
        for y in range(2):
            for x in range(2):
                zs = [g[(y * 8 + z * 2 + x) * r : (y * 8 + z * 2 + x + 1) * r] for z in range(4)]
                for hi, (even, odd) in enumerate(((0, 1), (3, 2))):
                    begin = ((y * 2 + hi) * 2 + x) * r
                    sz[begin : begin + r, cols] = jnp.where(side == 0, zs[odd], zs[even])
                    kz[begin : begin + r, cols] = jnp.where(side == 0, zs[even], zs[odd])
    for cols, g in grads(1):
        for y in range(2):
            for z in range(4):
                begin = (y * 8 + z * 2) * r
                zero, one = g[begin : begin + r], g[begin + r : begin + 2 * r]
                to = slice((y * 4 + z) * r, (y * 4 + z + 1) * r)
                sx[to, cols] = jnp.where(me_x == 0, one, zero)
                kx[to, cols] = jnp.where(me_x == 0, zero, one)
    for cols, g in grads(2):
        sy[:, cols] = jnp.where(me_y == 0, g[8 * r :], g[: 8 * r])
        ky[:, cols] = jnp.where(me_y == 0, g[: 8 * r], g[8 * r :])


def qkv_keep(pos, after, xt, ctxt, dattn, own, got, ozs, parts):
    width = xt.shape[0]
    r = width // 32
    wide = own.shape[1]
    shapes = [(8 * r + SMALL + 2 * r, wide)] + [(8 * r, wide)] * 5 + [(SMALL, width)]
    return call(
        qkv_keep_kernel,
        "qkv_weight_keep",
        [(pos, "s"), (after, "a")]
        + [(a, "v") for a in (xt, ctxt, dattn, own, got, ozs, *parts)],
        [(near(n), "v") for n in shapes],
    )


def second_qkv_kernel(pos_ref, after_ref, kx, rx, ky, ry, kz, rz, small, oz, xs, xk, ys, yk, zs, zk, small_out, oz_out):
    me_y, me_x, me_hi = pos_ref[0], pos_ref[2], pos_ref[4]
    r, width = kx.shape[0] // 8, small.shape[1]
    total = small[...] + rx[8 * r : 8 * r + SMALL, :width]
    small_out[...] = total
    xs[4 * r : 4 * r + SMALL, :width] = total
    base = 8 * r + SMALL
    xs[4 * r + SMALL :, :] = oz[rows24(1 - me_y, r), :] + rx[rows24_from(base, 1 - me_y, r), :]
    oz_out[...] = oz[rows24(me_y, r), :] + rx[rows24_from(base, me_y, r), :]
    there, here = rows24(1 - me_y, 4 * r), rows24(me_y, 4 * r)
    xs[: 4 * r, :] = kx[there, :] + rx[there, :]
    xk[...] = kx[here, :] + rx[here, :]
    for z in range(4):
        there, here = rows24(2 * z + 1 - me_x, r), rows24(2 * z + me_x, r)
        to = slice(z * r, (z + 1) * r)
        ys[to, :] = ky[there, :] + ry[there, :]
        yk[to, :] = ky[here, :] + ry[here, :]
    for y in range(2):
        there, here = rows24(2 * y + 1 - me_hi, 2 * r), rows24(2 * y + me_hi, 2 * r)
        to = slice(y * 2 * r, (y + 1) * 2 * r)
        zs[to, :] = kz[there, :] + rz[there, :]
        zk[to, :] = kz[here, :] + rz[here, :]


def third_qkv_kernel(pos_ref, after_ref, xk, xr, yk, yr, zk, zr, small, sent, kept, zs, zn, small_out):
    me_x, side = pos_ref[2], pos_ref[3]
    r, width = xk.shape[0] // 4, small.shape[1]
    total = small[...] + xr[4 * r : 4 * r + SMALL, :width]
    small_out[...] = total
    sent[4 * r :, :width] = total
    for i, (k, got) in enumerate(((xk, xr), (yk, yr))):
        for hi, (keep, send) in enumerate(((side, 1 - side), (3 - side, 2 + side))):
            there, here = rows24(send, r), rows24(keep, r)
            to = slice((2 * i + hi) * r, (2 * i + hi + 1) * r)
            sent[to, :] = k[there, :] + got[there, :]
            kept[to, :] = k[here, :] + got[here, :]
    for y in range(2):
        there, here = rows24(2 * y + 1 - me_x, r), rows24(2 * y + me_x, r)
        to = slice(y * r, (y + 1) * r)
        zs[to, :] = zk[there, :] + zr[there, :]
        zn[to, :] = zk[here, :] + zr[here, :]


def fourth_qkv_kernel(pos_ref, after_ref, k, got, zk, zr, small, sent, kept, zs, zn, small_out):
    me_y, me_hi = pos_ref[0], pos_ref[4]
    r, width = k.shape[0] // 4, small.shape[1]
    total = small[...] + got[4 * r :, :width]
    small_out[...] = total
    sent[2 * r :, :width] = total
    for i in range(2):
        there, here = rows24(2 * i + 1 - me_hi, r), rows24(2 * i + me_hi, r)
        to = slice(i * r, (i + 1) * r)
        sent[to, :] = k[there, :] + got[there, :]
        kept[to, :] = k[here, :] + got[here, :]
    there, here = rows24(1 - me_y, r), rows24(me_y, r)
    zs[...] = zk[there, :] + zr[there, :]
    zn[...] = zk[here, :] + zr[here, :]


def qkv_stage(kernel, name, pos, after, arrays, counts, width):
    wide = arrays[0].shape[1]
    return call(
        kernel,
        name,
        [(pos, "s"), (after, "a")] + [(a, "v") for a in arrays],
        [(near((n, width if n == SMALL else wide)), "v") for n in counts],
    )


def add_kernel(after_ref, a, b, out):
    out[...] = a[...] + b[...]


def sum_kernel(after, a, b):
    return call(add_kernel, "sum", [(after, "a"), (a, "v"), (b, "v")], [(near(a.shape), "v")])[0]


def last_outer_kernel(after_ref, xy, zk, zr, out, done):
    done[...] = jnp.zeros_like(done)
    wide = xy.shape[1]
    out[:, :wide] = xy[...]
    r = zk.shape[0]
    z = zk[...] + zr[4 * r + SMALL :, :]
    w = z.shape[1] // 4
    for j in range(4):
        out[j * r : (j + 1) * r, wide:] = z[:, j * w : (j + 1) * w]


def last_outer(after, xy, zk, zr):
    shape = (xy.shape[0], xy.shape[1] + zk.shape[1] // 4)
    return call(
        last_outer_kernel,
        "last_outer_stage",
        [(after, "a")] + [(a, "v") for a in (xy, zk, zr)],
        [(far(shape), "v"), (near((8, 128)), "v")],
    )


def last_qkv_kernel(pos_ref, k, got, zk, zr, small, q_out, k_out, v_out, o_out, *outs, classes, bias_rows):
    *vectors, inner_out, loss_out, head_out = outs
    r = zk.shape[0]
    width = small.shape[1]
    xs = k[:r, :] + got[:r, :]
    ys = k[r:, :] + got[r : 2 * r, :]
    zs = zk[...] + zr[...]
    for t, out in enumerate((q_out, k_out, v_out, o_out)):
        for g, data in enumerate((zs, xs, ys)):
            out[:, g * 256 : (g + 1) * 256] = data[:, t * 256 : (t + 1) * 256]
    total = small[...] + got[2 * r :, :width]
    me = pos_ref[5]
    rolled = pltpu.roll(total, lax.rem(width - me * r, width), 1)
    after = 5 + bias_rows
    for out, row in zip(vectors, (0, 1, 2, 3, 4, after, after + 1, after + 2)):
        out[...] = rolled[row : row + 1, :r]
    part = inner_out.shape[1]
    per_row = width // part
    row = lax.broadcasted_iota(jnp.int32, total.shape, 0)
    one = jnp.sum(jnp.where(row == 5 + me // per_row, total, 0.0), axis=0, keepdims=True)
    one = jnp.broadcast_to(one, (8, width))
    inner_out[...] = pltpu.roll(one, lax.rem(width - (me % per_row) * part, width), 1)[0:1, :part]
    lane = lax.broadcasted_iota(jnp.int32, (1, width), 1)
    loss_row = total[after + 3 : after + 4]
    loss_out[...] = jnp.sum(jnp.where(lane == pos_ref[6], loss_row, 0.0), axis=1, keepdims=True)
    for t in range(head_out.shape[0]):
        first = after + 4 + t * classes
        head_out[t] = total[first : first + classes]


def last_qkv(pos, k, got, zk, zr, small, classes, tables, bias_rows):
    r, width = zk.shape[0], small.shape[1]
    shapes = [(r, width)] * 4 + [(1, r)] * 8 + [(1, r * bias_rows), (1, 1), (tables, classes, width)]
    return call(
        functools.partial(last_qkv_kernel, classes=classes, bias_rows=bias_rows),
        "last_qkv_stage",
        [(pos, "s")] + [(a, "v") for a in (k, got, zk, zr, small)],
        [(far(s), "v") for s in shapes],
    )


def token_grad_kernel(after_ref, dr1_ref, wq_ref, wk_ref, wv_ref, *refs):
    *parts, out_hbm, done_ref, out_ref, sems = refs
    done_ref[...] = jnp.zeros_like(done_ref)
    rows = out_ref.shape[0]
    quads = len(parts) // 3

    @pl.loop(0, rows // TILE)
    def _(step):
        tile = at(step, TILE)
        total = dr1_ref[tile, :]
        for t, w_ref in enumerate((wq_ref, wk_ref, wv_ref)):
            d = jnp.concatenate([parts[g * 3 + t][tile, :] for g in range(quads)], axis=1)
            total = total + dot(d, w_ref[...], NT)
        out_ref[tile, :] = total
        pltpu.make_async_copy(out_ref.at[tile, :], out_hbm.at[tile, :], sems.at[step]).start()

    for i in range(rows // TILE):
        tile = pl.ds(i * TILE, TILE)
        pltpu.make_async_copy(out_ref.at[tile, :], out_hbm.at[tile, :], sems.at[i]).wait()


def token_grads(after, dr1, wq, wk, wv, parts):
    rows, width = dr1.shape
    return call(
        token_grad_kernel,
        "token_grad",
        [(after, "a")] + [(a, "v") for a in (dr1, wq, wk, wv, *parts)],
        [(far((rows, width)), "a"), (near((8, 128)), "v")],
        [pltpu.VMEM((rows, width), single), pltpu.SemaphoreType.DMA((rows // TILE,))],
    )


def second_kernel(pos_ref, after_ref, kx, rx, ky, ry, *refs):
    me_y, me_x, me_hi = pos_ref[0], pos_ref[2], pos_ref[4]
    outs = refs[len(refs) % 4 :] if len(refs) == 4 else refs[2:]
    xs, xk, ys, yk = outs[:4]
    xs[...] = kx[1 - me_y] + rx[1 - me_y]
    xk[...] = kx[me_y] + rx[me_y]
    ys[...] = ky[:, 1 - me_x] + ry[:, 1 - me_x]
    yk[...] = ky[:, me_x] + ry[:, me_x]
    if len(refs) > 4:
        kz, rz = refs[:2]
        zs, zk = outs[4:]
        zs[...] = kz[:, 1 - me_hi] + rz[:, 1 - me_hi]
        zk[...] = kz[:, me_hi] + rz[:, me_hi]


def second(tag, pos, after, kx, rx, ky, ry, kz=None, rz=None):
    flat = (4,) + kx.shape[2:]
    inputs = [kx, rx, ky, ry]
    shapes = [flat] * 4
    if kz is not None:
        inputs += [kz, rz]
        shapes += [(2, 2) + kz.shape[3:]] * 2
    return call(
        second_kernel,
        f"second_stage_{tag}",
        [(pos, "s"), (after, "a")] + [(a, "v") for a in inputs],
        [(near(s), "v") for s in shapes],
    )


def third_kernel(pos_ref, after_ref, xk, xr, yk, yr, *refs):
    me_x, side = pos_ref[2], pos_ref[3]
    wide = xk.shape[2]
    if len(refs) == 2:
        sent, kept = refs
    else:
        zk, zr, sent, kept, zs, zn = refs
        zs[...] = zk[:, 1 - me_x] + zr[:, 1 - me_x]
        zn[...] = zk[:, me_x] + zr[:, me_x]
    for hi, (keep, send) in enumerate(((side, 1 - side), (3 - side, 2 + side))):
        sent[hi, :, :wide] = xk[send] + xr[send]
        sent[hi, :, wide:] = yk[send] + yr[send]
        kept[hi, :, :wide] = xk[keep] + xr[keep]
        kept[hi, :, wide:] = yk[keep] + yr[keep]


def third(pos, after, xk, xr, yk, yr, zk=None, zr=None):
    r, wide = xk.shape[1:]
    inputs = [xk, xr, yk, yr]
    shapes = [(2, r, 2 * wide)] * 2
    if zk is not None:
        inputs += [zk, zr]
        shapes += [(2,) + zk.shape[2:]] * 2
    return call(
        third_kernel,
        "third_stage",
        [(pos, "s"), (after, "a")] + [(a, "v") for a in inputs],
        [(near(s), "v") for s in shapes],
    )


def fourth_kernel(pos_ref, after_ref, xyk, xyr, *refs):
    me_y, me_hi = pos_ref[0], pos_ref[4]
    if len(refs) == 2:
        sent, kept = refs
    else:
        zk, zr, sent, kept, zs, zn = refs
        zs[...] = zk[1 - me_y] + zr[1 - me_y]
        zn[...] = zk[me_y] + zr[me_y]
    sent[...] = xyk[1 - me_hi] + xyr[1 - me_hi]
    kept[...] = xyk[me_hi] + xyr[me_hi]


def fourth(tag, pos, after, xyk, xyr):
    return call(
        fourth_kernel,
        f"fourth_stage_{tag}",
        [(pos, "s"), (after, "a"), (xyk, "v"), (xyr, "v")],
        [(near(xyk.shape[1:]), "v")] * 2,
    )


def last_kernel(after_ref, xyk, xyr, *refs, layout):
    count = len(layout)
    outs = refs[-count - 1 : -1]
    refs[-1][...] = jnp.zeros_like(refs[-1])
    sources = [(xyk, xyr), refs[:2]]
    for out, pieces in zip(outs, layout):
        to = 0
        for source, begin, end in pieces:
            a, b = sources[source]
            out[:, to : to + end - begin] = a[:, begin:end] + b[:, begin:end]
            to += end - begin


def last(after, xyk, xyr, zk, zr, layout):
    inputs = [xyk, xyr] + ([] if zk is None else [zk, zr])
    shapes = [(xyk.shape[0], sum(e - b for _, b, e in pieces)) for pieces in layout]
    return call(
        functools.partial(last_kernel, layout=layout),
        "last_stage",
        [(after, "a")] + [(a, "v") for a in inputs],
        [(far(s), "v") for s in shapes] + [(near((8, 128)), "v")],
    )


def pair_list(change):
    pairs = []
    for y in range(2):
        for c in range(2):
            for z in range(4):
                for x in range(2):
                    py, pc, pz, px = change(y, c, z, x)
                    pairs.append((((y * 2 + c) * 4 + z) * 2 + x, ((py * 2 + pc) * 4 + pz) * 2 + px))
    return pairs


PAIRS = {
    "y": pair_list(lambda y, c, z, x: (1 - y, c, z, x)),
    "c": pair_list(lambda y, c, z, x: (y, 1 - c, z, x)),
    "x": pair_list(lambda y, c, z, x: (y, c, z, 1 - x)),
    "near": pair_list(lambda y, c, z, x: (y, c, z ^ 1, x)),
    "far": pair_list(lambda y, c, z, x: (y, c, 3 - z, x)),
}


def swap(array, name):
    return lax.ppermute(array, ALL_AXES, PAIRS[name])


def per_device(
    tokens,
    out_cot,
    lengths,
    labels,
    task_ids,
    task_weights,
    query_weight,
    key_weight,
    value_weight,
    query_bias,
    value_bias,
    output_weight,
    output_bias,
    norm1_gain,
    norm1_bias,
    inner_weight,
    inner_bias,
    outer_weight,
    outer_bias,
    norm2_gain,
    norm2_bias,
    head_table,
    *,
    staged,
):
    seqs, length, width = tokens.shape
    rows = seqs * length
    ff = inner_weight.shape[1]
    group_seqs = seqs * lax.axis_size("batch")
    task_index = lax.axis_index("task")
    batch_index = lax.axis_index("batch")
    my_y, my_c, my_z, my_x = task_index // 2, task_index % 2, batch_index // 2, batch_index % 2
    my_hi = my_z // 2
    my_side = (my_z // 2) ^ (my_z % 2)
    where = task_index * lax.axis_size("batch") + batch_index
    pos = jnp.stack([my_y, my_c, my_x, my_side, my_hi, where, task_index]).astype(jnp.int32)
    vectors = (output_bias, norm1_gain, norm1_bias, inner_bias, outer_bias, norm2_gain, norm2_bias)

    x, q, k, v, ctx, ctxt, lse, wo, wi, wd, cot = attention(
        tokens,
        lengths,
        query_weight,
        key_weight,
        value_weight,
        query_bias,
        value_bias,
        output_weight,
        inner_weight,
        outer_weight,
        out_cot,
    )
    block_out, normed1, root1, h1t, act, slope, ddown, sums2 = middle(
        x, ctx, cot, length, labels, task_ids, task_weights, wo, wi, wd, vectors, head_table.transpose(1, 0, 2), group_seqs
    )
    block_out = block_out.reshape(tokens.shape)

    classes, tables = head_table.shape[1], head_table.shape[0]
    f2, r, quads = ff // 2, width // 32, width // 256
    parts, sums0 = [None] * (3 * quads), [None] * quads

    def back(quad, after):
        *grads, sums = attention_back(lengths, after, q, k, v, ctx, e["dctx"], lse, length, quad)
        parts[3 * quad : 3 * quad + 3] = grads
        sums0[quad] = sums
        return sums

    def small_args():
        return (ctxt, e["dattn"], parts, sums0, e["sums1"], e["inner_bias"], sums2, classes, tables)

    e = {}

    def send_outer(after):
        e["o_send"] = outer_send(pos, after, act, ddown, True)
        return e["o_send"]

    def rest_outer(after):
        e["o_rest"] = outer_send(pos, after, act, ddown, False)
        return e["o_rest"]

    def do_inner_grad(after):
        e["dinner"], e["inner_bias"] = inner_grad(after, ddown, wd, slope)
        return e["inner_bias"]

    def send_inner(after):
        e["i_send"] = inner_send(pos, after, h1t, e["dinner"], True)
        return e["i_send"]

    def do_first_norm(after):
        e["dr1"], e["dattn"], e["dctx"], e["xt"], e["sums1"] = first_norm(
            after,
            e["dinner"],
            inner_weight,
            ddown,
            normed1,
            root1,
            output_weight,
            norm1_gain,
            tokens.reshape(rows, width),
        )
        return e["sums1"]

    def do_tokens(after):
        e["token_grad"], after = token_grads(after, e["dr1"], query_weight, key_weight, value_weight, parts)
        return after

    def send_qkv(after):
        e["qkv_s"] = qkv_send(pos, task_ids, after, e["xt"], *small_args(), True)
        return e["qkv_s"]

    def keep_outer(after):
        osx, okx, osy, oky, osz, okz = outer_keep(pos, after, e["o_rest"], swap(e["o_send"], "c"))
        e["o1"] = (okx, swap(osx, "x"), oky, swap(osy, "y"), okz, swap(osz, "near"))
        return okx

    def keep_inner(after):
        isx, ikx, isy, iky = inner_keep(pos, after, h1t, e["dinner"], swap(e["i_send"], "c"))
        e["i1"] = (ikx, swap(isx, "x"), iky, swap(isy, "y"))
        return ikx

    def second_outer(after):
        xs, xk, ys, yk, zs, zk = second("outer", pos, after, *e["o1"])
        e["o2"] = (xk, swap(xs, "y"), yk, swap(ys, "x"), zk, swap(zs, "far"))
        return xk

    def second_inner(after):
        xs, xk, ys, yk = second("inner", pos, after, *e["i1"])
        e["i2"] = (xk, swap(xs, "y"), yk, swap(ys, "x"))
        return xk

    def do_third_outer(after):
        sent, kept, e["ozs"], e["oz"] = third_outer(pos, after, *e["o2"])
        e["o3"] = (kept, swap(sent, "near"))
        return kept

    def third_inner(after):
        sent, kept = third(pos, after, *e["i2"])
        e["i3"] = (kept, swap(sent, "near"))
        return kept

    def fourth_outer(after):
        sent, kept = fourth("outer", pos, after, *e["o3"])
        e["o4"] = (kept, swap(sent, "far"))
        return kept

    def fourth_inner(after):
        sent, kept = fourth("inner", pos, after, *e["i3"])
        e["i4"] = (kept, swap(sent, "far"))
        return kept

    def sum_outer(after):
        e["outer_xy"] = sum_kernel(after, *e["o4"])
        return e["outer_xy"]

    def last_inner(after):
        e["inner_s"], after = last(after, *e["i4"], None, None, (((0, 0, 2 * f2),),))
        return after

    def do_last_outer(after):
        e["outer_s"], after = last_outer(after, e["outer_xy"], e["oz2"], e["q2"][1])
        return after

    def keep_qkv(after):
        sx, kx, sy, ky, sz, kz, small = qkv_keep(
            pos, after, e["xt"], ctxt, e["dattn"], e["qkv_s"], swap(e["qkv_s"], "c"), e["ozs"], parts
        )
        e["q1"] = (kx, swap(sx, "x"), ky, swap(sy, "y"), kz, swap(sz, "near"), small, e["oz"])
        return small

    def stage(kernel, name, after, arrays, counts):
        return qkv_stage(kernel, name, pos, after, arrays, counts, width)

    def second_qkv(after):
        xs, xk, ys, yk, zs, zk, small, e["oz2"] = stage(
            second_qkv_kernel,
            "second_qkv_stage",
            after,
            e["q1"],
            [5 * r + SMALL, 4 * r, 4 * r, 4 * r, 4 * r, 4 * r, SMALL, r],
        )
        e["q2"] = (xk, swap(xs, "y"), yk, swap(ys, "x"), zk, swap(zs, "far"), small)
        return small

    def third_qkv(after):
        sent, kept, zs, zk, small = stage(
            third_qkv_kernel, "third_qkv_stage", after, e["q2"], [4 * r + SMALL, 4 * r, 2 * r, 2 * r, SMALL]
        )
        e["q3"] = (kept, swap(sent, "near"), zk, swap(zs, "x"), small)
        return small

    def fourth_qkv(after):
        sent, kept, zs, zk, small = stage(
            fourth_qkv_kernel, "fourth_qkv_stage", after, e["q3"], [2 * r + SMALL, 2 * r, r, r, SMALL]
        )
        e["q4"] = (kept, swap(sent, "far"), zk, swap(zs, "y"), small)
        return small

    def do_last_qkv(after):
        e["last"] = last_qkv(pos, *e["q4"], classes, tables, ff // width)
        return after

    steps = {
        "send_outer": send_outer,
        "rest_outer": rest_outer,
        "inner_grad": do_inner_grad,
        "send_inner": send_inner,
        "keep_outer": keep_outer,
        "first_norm": do_first_norm,
        "keep_inner": keep_inner,
        "second_outer": second_outer,
        "send_qkv": send_qkv,
        "second_inner": second_inner,
        "third_outer": do_third_outer,
        "keep_qkv": keep_qkv,
        "third_inner": third_inner,
        "tokens": do_tokens,
        "fourth_outer": fourth_outer,
        "second_qkv": second_qkv,
        "sum_outer": sum_outer,
        "third_qkv": third_qkv,
        "fourth_inner": fourth_inner,
        "fourth_qkv": fourth_qkv,
        "last_inner": last_inner,
        "last_outer": do_last_outer,
        "last_qkv": do_last_qkv,
    }
    for quad in range(quads):
        steps[f"back_{quad}"] = functools.partial(back, quad)
    if staged:
        after = sums2
        for name in ORDER:
            after = steps[name](after)
        query_s, key_s, value_s, output_s, *rest = e["last"]
        inner_s, outer_s = e["inner_s"], e["outer_s"]
        vector_s = [v.reshape(-1) for v in rest[:-1]]
        head_grad = rest[-1]
    else:
        after = do_first_norm(send_inner(do_inner_grad(send_outer(sums2))))
        o_keep = rest_outer(after)
        i_keep = inner_send(pos, after, h1t, e["dinner"], False)
        for quad in range(quads):
            after = back(quad, after)
        after = do_tokens(send_qkv(after))
        qkv_k = qkv_send(pos, task_ids, after, e["xt"], *small_args(), False)
        o_send, i_send, qkv_s = e["o_send"], e["i_send"], e["qkv_s"]

        def whole_rows(sent, kept):
            both = jnp.stack([jnp.where(my_c == 0, kept, sent), jnp.where(my_c == 0, sent, kept)], axis=1)
            return both.reshape(-1, both.shape[-1])

        def scatter(grad):
            return lax.psum_scatter(grad, ALL_AXES, scatter_dimension=0, tiled=True)

        def by_rows(array):
            return array.reshape(2, -1, array.shape[-1])

        outer_s = scatter(whole_rows(o_send, o_keep))
        inner_s = scatter(
            jnp.concatenate([whole_rows(by_rows(i_send[j]), by_rows(i_keep[j])) for j in range(2)], axis=-1)
        )
        count = width // 2

        def tensor(array, t):
            cols = slice(t * 256, (t + 1) * 256)
            return by_rows(jnp.concatenate([array[g * count : (g + 1) * count, cols] for g in range(quads)], axis=1))

        query_s, key_s, value_s, output_s = [
            scatter(whole_rows(tensor(qkv_s, t), tensor(qkv_k, t))) for t in range(4)
        ]
        small = lax.psum(qkv_s[quads * count :, :width], ALL_AXES)
        devices = lax.axis_size("task") * lax.axis_size("batch")

        def mine(array):
            flat = array.reshape(-1)
            size = flat.shape[0] // devices
            return lax.dynamic_slice(flat, (where * size,), (size,))

        last_row = 5 + ff // width
        vector_s = [mine(small[i]) for i in (0, 1, 2, 3, 4, last_row, last_row + 1, last_row + 2)]
        vector_s.append(mine(small[5:last_row]))
        vector_s.append(lax.dynamic_slice(small, (last_row + 3, task_index), (1, 1)).reshape(1))
        head_grad = small[last_row + 4 : last_row + 4 + classes * tables].reshape(head_table.shape)
    token_grad = e["token_grad"].reshape(tokens.shape)
    bias_q, bias_v, gain1, bias1, bias_o, gain2, bias2, bias_d, bias_i, loss = vector_s
    return (
        block_out,
        token_grad,
        loss,
        query_s,
        key_s,
        value_s,
        bias_q,
        bias_v,
        output_s,
        bias_o,
        gain1,
        bias1,
        inner_s,
        bias_i,
        outer_s,
        bias_d,
        gain2,
        bias2,
        head_grad,
    )


def solution(mesh):
    rows = P(ALL_AXES)
    plain = P()
    task = P("task")
    staged = mesh.shape["task"] == 4 and mesh.shape["batch"] == 8
    return jax.shard_map(
        functools.partial(per_device, staged=staged),
        mesh=mesh,
        in_specs=(rows, rows, rows, rows, task, task) + (plain,) * 16,
        out_specs=(rows, rows, task) + (rows,) * 15 + (plain,),
        check_vma=False,
    )
```

```python
import functools

import jax
import jax.numpy as jnp
from jax import lax
from jax.experimental import pallas as pl
from jax.experimental.pallas import tpu as pltpu
from jax.sharding import PartitionSpec as P

HD = 64
TILE = 256
ALL_AXES = ("task", "batch")
NN = (((1,), (0,)), ((), ()))
NT = (((1,), (1,)), ((), ()))
TN = (((0,), (0,)), ((), ()))
half = jnp.bfloat16
single = jnp.float32
eps_norm = 1e-12


def dot(left, right, dims=NN):
    return lax.dot_general(left, right, dims, preferred_element_type=single)


ANY = pl.BlockSpec(memory_space=pl.ANY)
SMEM = pl.BlockSpec(memory_space=pltpu.SMEM)
VMEM = pl.BlockSpec(memory_space=pltpu.VMEM)
HBM = pl.BlockSpec(memory_space=pltpu.HBM)


def near(shape, dtype=single):
    return pltpu.VMEM(shape, dtype)


def off(shape, dtype=single):
    return pltpu.HBM(shape, dtype)


def far(shape, dtype=single):
    return jax.ShapeDtypeStruct(shape, dtype)


COSTS = {
    "attention_back_0": 1,
    "attention_back_1": 10000,
    "attention_back_2": 10000,
    "first_norm_back": 1,
    "fourth_qkv_stage": 100,
    "fourth_stage_inner": 1,
    "fourth_stage_outer": 1000,
    "inner_grad": 3000,
    "inner_weight_keep": 1000,
    "inner_weight_send": 10000,
    "last_outer_stage": 3000,
    "last_stage": 300,
    "outer_weight_keep": 3000,
    "outer_weight_rest": 1,
    "outer_weight_send": 3000,
    "qkv_weight_keep": 100,
    "qkv_weight_send": 3000,
    "second_qkv_stage": 100,
    "second_stage_inner": 10000,
    "second_stage_outer": 3000,
    "sum": 10000,
    "third_outer_stage": 10000,
    "third_qkv_stage": 3000,
    "third_stage": 10000,
    "token_grad": 3000,
}
ORDER = [
    "send_outer",
    "inner_grad",
    "send_inner",
    "rest_outer",
    "keep_outer",
    "keep_inner",
    "first_norm",
    "back_0",
    "second_outer",
    "back_1",
    "second_inner",
    "back_2",
    "third_outer",
    "send_qkv",
    "keep_qkv",
    "third_inner",
    "tokens",
    "fourth_outer",
    "second_qkv",
    "sum_outer",
    "third_qkv",
    "fourth_inner",
    "last_outer",
    "fourth_qkv",
    "last_inner",
    "last_qkv",
]


def call(kernel, name, inputs, outputs, scratch=(), megabytes=7, aliases=None):
    specs = {"v": VMEM, "s": SMEM, "a": ANY, "h": HBM}
    spaces = {"v": pltpu.VMEM, "h": pltpu.HBM}
    arrays = [
        pltpu.with_memory_space_constraint(x, spaces[p]) if p in spaces and (x.ndim > 1 or p == "h") else x for x, p in inputs
    ]
    return pl.pallas_call(
        kernel,
        in_specs=[specs[p] for _, p in inputs],
        out_specs=[specs[p] for _, p in outputs],
        out_shape=[o for o, _ in outputs],
        scratch_shapes=list(scratch),
        input_output_aliases=aliases or {},
        compiler_params=pltpu.CompilerParams(vmem_limit_bytes=megabytes << 20),
        cost_estimate=pl.CostEstimate(flops=COSTS.get(name, 1) * 10**6, bytes_accessed=1024, transcendentals=0),
        name=name,
    )(*arrays)


def at(index, size):
    return pl.ds(pl.multiple_of(index * size, size), size)


def as_row(ref):
    return ref[...].astype(single).reshape(1, -1)


def pair_operands(q, k, parity, dead, scale):
    rows = q.shape[0]
    lane = lax.broadcasted_iota(jnp.int32, (rows, 128), 1)
    inside = (lane // HD) == parity
    spare = lane == HD * (1 - parity)
    q_one = jnp.where(inside, q.astype(single) * scale, jnp.where(spare, 1.0, 0.0)).astype(half)
    k_one = jnp.where(inside, k.astype(single), jnp.where(spare & dead, -1e30, 0.0)).astype(half)
    return q_one, k_one


def attention_kernel(
    n_ref, x_hbm, wq_hbm, wk_hbm, wv_hbm, bq_hbm, bv_hbm, wo_hbm, wi_hbm, wd_hbm, cot_hbm,
    x_ref, q_hbm, k_hbm, v_hbm, ctx_ref, ctxt_hbm, lse_ref, wo_ref, wi_ref, wd_ref, cot_ref,
    ctxt_ref, q_ref, k_ref, v_ref, wq_ref, wk_ref, wv_ref, bq_vmem, bv_vmem, sems, out_sems, ctxt_sems,
    *, length,
):
    rows, width = x_ref.shape
    sides = [pl.ds(i * (rows // 2), rows // 2) for i in range(2)]
    pairs = (
        (x_hbm.at[sides[0], :], x_ref.at[sides[0], :]), (bq_hbm, bq_vmem), (wq_hbm, wq_ref),
        (x_hbm.at[sides[1], :], x_ref.at[sides[1], :]), (bv_hbm, bv_vmem), (wk_hbm, wk_ref), (wv_hbm, wv_ref),
        (wo_hbm, wo_ref), (wi_hbm, wi_ref), (wd_hbm, wd_ref), (cot_hbm, cot_ref),
    )
    copies = [pltpu.make_async_copy(src, dst, sems.at[i]) for i, (src, dst) in enumerate(pairs)]
    for copy in copies[:7]:
        copy.start()
    zero = jnp.zeros((1, width), single)
    leaving = []
    for i, (waits, w_ref, bias, out, out_hbm) in enumerate((
        ((0, 1, 2), wq_ref, bq_vmem, q_ref, q_hbm),
        ((4, 5), wk_ref, None, k_ref, k_hbm),
        ((6,), wv_ref, bv_vmem, v_ref, v_hbm),
    )):
        for wait in waits:
            copies[wait].wait()
        shift = zero if bias is None else as_row(bias)
        for part, side in enumerate(sides):
            if i == 0 and part == 1:
                copies[3].wait()
            out[side, :] = (dot(x_ref[side, :], w_ref[...]) + shift).astype(half)
        if i == 0:
            for copy in copies[7:]:
                copy.start()
        leaving.append(pltpu.make_async_copy(out, out_hbm, out_sems.at[i]))
        leaving[-1].start()

    quads = width // 256

    @pl.loop(0, (rows // length) * quads)
    def _(step):
        seq, quad = step // quads, step % quads
        tokens, cols = at(seq, length), at(quad, 256)
        dead = lax.broadcasted_iota(jnp.int32, (length, 128), 0) >= n_ref[seq]
        q, k, v = q_ref[tokens, cols], k_ref[tokens, cols], v_ref[tokens, cols]
        vt = v.T
        scores = []
        for h in range(4):
            pair = slice(h // 2 * 128, h // 2 * 128 + 128)
            q_one, k_one = pair_operands(q[:, pair], k[:, pair], h % 2, dead, HD**-0.5)
            scores.append(dot(k_one, q_one, NT))
        weights = []
        for s in scores:
            top = jnp.max(s, axis=0, keepdims=True)
            e = jnp.exp(s - top)
            weights.append((e.astype(half), top, jnp.sum(e, axis=0, keepdims=True)))
        parts = []
        for h, (e, top, total) in enumerate(weights):
            parts.append((dot(vt[h * HD : (h + 1) * HD], e) * (1.0 / total)).astype(half))
            lse_ref[step, h : h + 1, :] = top + jnp.log(total)
        ctxt = jnp.concatenate(parts, axis=0)
        ctxt_ref[cols, tokens] = ctxt
        ctx_ref[tokens, cols] = ctxt.T
        pltpu.make_async_copy(ctxt_ref.at[cols, tokens], ctxt_hbm.at[cols, tokens], ctxt_sems.at[step]).start()

    for step in range((rows // length) * quads):
        seq, quad = step // quads, step % quads
        tokens, cols = pl.ds(seq * length, length), pl.ds(quad * 256, 256)
        pltpu.make_async_copy(ctxt_ref.at[cols, tokens], ctxt_hbm.at[cols, tokens], ctxt_sems.at[step]).wait()
    for copy in copies[7:] + leaving:
        copy.wait()


def attention(tokens, lengths, wq, wk, wv, bq, bv, wo, wi, wd, cot):
    seqs, length, width = tokens.shape
    rows = seqs * length
    flat = (rows, width)
    quads = width // 256
    return call(
        functools.partial(attention_kernel, length=length),
        "attention_forward",
        [(lengths, "s"), (tokens.reshape(flat), "h"), (wq, "h"), (wk, "h"), (wv, "h"), (bq, "h"), (bv, "h")]
        + [(wo, "h"), (wi, "h"), (wd, "h"), (cot.reshape(flat), "h")],
        [(near(flat, half), "v")]
        + [(off(flat, half), "h")] * 3
        + [(near(flat, half), "v"), (off((width, rows), half), "h"), (near((seqs * quads, 8, length)), "v")]
        + [(near(w.shape, half), "v") for w in (wo, wi, wd)]
        + [(near(flat, half), "v")],
        [pltpu.VMEM((width, rows), half)]
        + [pltpu.VMEM(flat, half)] * 3
        + [pltpu.VMEM(w.shape, half) for w in (wq, wk, wv, bq, bv)]
        + [pltpu.SemaphoreType.DMA((11,)), pltpu.SemaphoreType.DMA((3,))]
        + [pltpu.SemaphoreType.DMA((seqs * quads,))],
        20,
    )


def norm_parts(resid):
    center = resid - jnp.mean(resid, axis=-1, keepdims=True)
    inv_root = lax.rsqrt(jnp.mean(center * center, axis=-1, keepdims=True) + eps_norm)
    return center * inv_root, inv_root


def norm_back(grad_out, normed, inv_root, gain):
    scaled = grad_out * gain
    return inv_root * (
        scaled
        - jnp.mean(scaled, axis=-1, keepdims=True)
        - normed * jnp.mean(scaled * normed, axis=-1, keepdims=True)
    )


def gelu_parts(u):
    u = u.astype(half)
    w = u * u
    v = jnp.minimum(w, jnp.asarray(36.0, half))
    p = (v * jnp.asarray(-0.00031594874, half) + jnp.asarray(0.0367987, half)) * v + jnp.asarray(0.79771759, half)
    h = jnp.asarray(0.5, half)
    cdf = h + h * jnp.tanh(u * p)
    bell = jnp.exp2(w * jnp.asarray(-0.72134752, half) - jnp.asarray(1.32574806, half))
    return u * cdf, cdf + u * bell


def column_sum(array):
    return jnp.sum(array, axis=0, keepdims=True)


def middle_kernel(
    task_ref, label_ref, weight_ref, x_ref, ctx_ref, cot_ref, wo_ref, wi_ref, wd_ref,
    bo_ref, g1_ref, b1_ref, bi_ref, bd_ref, g2_ref, b2_ref, head_ref,
    out_hbm, normed1_ref, root1_ref, h1t_ref, act_ref, slope_ref, ddown_ref, sums_ref,
    out_ref, sems,
    *, length, group_seqs,
):
    rows, width = x_ref.shape
    ff = wi_ref.shape[1]
    part = 768
    bo, g1, b1, bd, g2, b2 = [as_row(r) for r in (bo_ref, g1_ref, b1_ref, bd_ref, g2_ref, b2_ref)]
    bi = as_row(bi_ref)
    w = weight_ref[0]
    table = head_ref[...].astype(single)
    chosen = lax.broadcasted_iota(jnp.int32, table.shape, 1) == task_ref[0]
    head = jnp.sum(jnp.where(chosen, table, 0.0), axis=1)
    classes = head.shape[0]
    sums_ref[...] = jnp.zeros_like(sums_ref)

    @pl.loop(0, rows // (2 * TILE))
    def _(step):
        tile = at(step, (2 * TILE))
        x = x_ref[tile, :].astype(single)
        normed1, root1 = norm_parts(x + dot(ctx_ref[tile, :], wo_ref[...]) + bo)
        normed1_ref[tile, :] = normed1.astype(half)
        root1_ref[tile, :] = jnp.broadcast_to(root1, ((2 * TILE), 128))
        hidden1 = normed1 * g1 + b1
        h1 = hidden1.astype(half)
        h1t_ref[:, tile] = h1.T

        def inner_part(j):
            return dot(h1, wi_ref[:, j : j + part]) + bi[:, j : j + part]

        down = None
        following = inner_part(0)
        for j in range(0, ff, part):
            inner = following
            if j + part < ff:
                following = inner_part(j + part)
            value, slope = gelu_parts(inner)
            act = value.astype(half)
            act_ref[tile, j : j + part] = act
            slope_ref[tile, j : j + part] = slope.astype(half)
            term = dot(act, wd_ref[j : j + part, :])
            down = term if down is None else down + term
        normed2, root2 = norm_parts(hidden1 + down + bd)
        final = normed2 * g2 + b2
        low = final.astype(half)
        out_ref[tile, :] = low
        pltpu.make_async_copy(out_ref.at[tile, :], out_hbm.at[tile, :], sems.at[step]).start()
        cls = low[0:1].astype(single)
        logits = [jnp.sum(cls * head[c : c + 1], axis=1, keepdims=True) for c in range(classes)]
        top = functools.reduce(jnp.maximum, logits)
        lse = top + jnp.log(sum(jnp.exp(v - top) for v in logits))
        per_seq = length // (2 * TILE)
        label = label_ref[step // per_seq]
        first = jnp.where(step % per_seq == 0, 1.0, 0.0)
        picked = sum(jnp.where(label == c, v, 0.0) for c, v in enumerate(logits))
        slopes = [
            (jnp.exp(v - lse) - jnp.where(label == c, 1.0, 0.0)) * (w / group_seqs * first)
            for c, v in enumerate(logits)
        ]
        d_cls = sum(s * head[c : c + 1] for c, s in enumerate(slopes))
        row = lax.broadcasted_iota(jnp.int32, final.shape, 0)
        d_final = cot_ref[tile, :].astype(single) * w + jnp.where(row == 0, d_cls, 0.0)
        dr2 = norm_back(d_final, normed2, root2, g2)
        ddown = dr2.astype(half)
        ddown_ref[tile, :] = ddown
        sums_ref[0:1] += column_sum(d_final * normed2)
        sums_ref[1:2] += column_sum(d_final)
        sums_ref[2:3] += column_sum(ddown.astype(single))
        for c in range(classes):
            sums_ref[3 + c : 4 + c] += slopes[c] * cls
        sums_ref[7:8] += jnp.broadcast_to((lse - picked) * (w / group_seqs * first), cls.shape)

    for i in range(rows // (2 * TILE)):
        tile = pl.ds(i * (2 * TILE), (2 * TILE))
        pltpu.make_async_copy(out_ref.at[tile, :], out_hbm.at[tile, :], sems.at[i]).wait()


def middle(x, ctx, cot, length, labels, task_ids, task_weights, wo, wi, wd, vectors, head_table, group_seqs):
    rows, width = x.shape
    ff = wi.shape[1]
    assert head_table.shape[0] <= 4
    flat = (rows, width)
    return call(
        functools.partial(middle_kernel, length=length, group_seqs=group_seqs),
        "middle_forward",
        [(task_ids, "s"), (labels, "s"), (task_weights, "s")]
        + [(a, "v") for a in (x, ctx, cot, wo, wi, wd, *vectors, head_table)],
        [(far(flat, half), "a")]
        + [
            (near(flat, half), "v"),
            (near((rows, 128)), "v"),
            (near((width, rows), half), "v"),
            (near((rows, ff), half), "v"),
            (near((rows, ff), half), "v"),
            (near(flat, half), "v"),
            (near((8, width)), "v"),
        ],
        [pltpu.VMEM(flat, half), pltpu.SemaphoreType.DMA((rows // (2 * TILE),))],
        20,
    )


def inner_grad_kernel(after_ref, ddown_ref, wd_ref, slope_ref, dinner_ref, bias_ref):
    part = 768

    @pl.loop(0, wd_ref.shape[0] // part)
    def _(j):
        cols = at(j, part)
        d = dot(ddown_ref[...], wd_ref[cols, :], NT) * slope_ref[:, cols].astype(single)
        low = d.astype(half)
        dinner_ref[:, cols] = low
        bias_ref[pl.ds(j, 1), :] = column_sum(low.astype(single))


def inner_grad(after, ddown, wd, slope):
    ff, width = wd.shape
    return call(
        inner_grad_kernel,
        "inner_grad",
        [(after, "a"), (ddown, "v"), (wd, "v"), (slope, "v")],
        [(near(slope.shape, half), "v"), (near((ff // width, width)), "v")],
        aliases={3: 0},
    )


def first_norm_kernel(
    after_ref, dinner_ref, wi_ref, ddown_ref, normed1_ref, root1_ref, wo_ref, g1_ref, x_ref,
    dr1_ref, dattn_ref, dctx_ref, xt_ref, sums_ref,
):
    rows, width = dr1_ref.shape
    g1 = as_row(g1_ref)
    sums_ref[...] = jnp.zeros_like(sums_ref)

    @pl.loop(0, rows // TILE)
    def _(step):
        tile = at(step, TILE)
        normed1 = normed1_ref[tile, :].astype(single)
        dh1 = ddown_ref[tile, :].astype(single) + dot(dinner_ref[tile, :], wi_ref[...], NT)
        dr1 = norm_back(dh1, normed1, root1_ref[tile, 0:1], g1)
        dr1_ref[tile, :] = dr1
        dattn = dr1.astype(half)
        dattn_ref[tile, :] = dattn
        dctx_ref[tile, :] = dot(dattn, wo_ref[...], NT).astype(half)
        xt_ref[:, tile] = x_ref[tile, :].T
        sums_ref[0:1] += column_sum(dh1 * normed1)
        sums_ref[1:2] += column_sum(dh1)
        sums_ref[2:3] += column_sum(dattn.astype(single))


def first_norm(after, dinner, wi, ddown, normed1, root1, wo, g1, x):
    rows, width = ddown.shape
    flat = (rows, width)
    return call(
        first_norm_kernel,
        "first_norm_back",
        [(after, "a")] + [(a, "v") for a in (dinner, wi, ddown, normed1, root1, wo, g1, x)],
        [(near(flat), "v"), (near(flat, half), "v"), (near(flat, half), "v")]
        + [(near((width, rows), half), "v"), (near((8, width)), "v")],
    )


def attention_back_kernel(
    n_ref, after_ref, q_ref, k_ref, v_ref, ctx_ref, dctx_ref, lse_ref, dq_ref, dk_ref, dv_ref, sums_ref,
    *, length, quad,
):
    scale = HD**-0.5
    quads = q_ref.shape[1] // 256
    cols = slice(quad * 256, quad * 256 + 256)
    sums_ref[...] = jnp.zeros_like(sums_ref)

    @pl.loop(0, q_ref.shape[0] // length)
    def _(seq):
        tokens = at(seq, length)
        dead = lax.broadcasted_iota(jnp.int32, (length, 128), 0) >= n_ref[seq]
        low_half = lax.broadcasted_iota(jnp.int32, (length, 128), 1) < HD
        q, k, v, dctx = [r[tokens, cols] for r in (q_ref, k_ref, v_ref, dctx_ref)]
        kt = k.T
        prod_t = (ctx_ref[tokens, cols].astype(single) * dctx.astype(single)).T
        dqt = []
        for pair in range(2):
            side = slice(pair * 128, pair * 128 + 128)
            q_pair, k_pair, v_pair, d_pair = q[:, side], k[:, side], v[:, side], dctx[:, side]
            first = []
            for parity in range(2):
                q_one, k_one = pair_operands(q_pair, k_pair, parity, dead, scale)
                inside = low_half if parity == 0 else ~low_half
                v_one = jnp.where(inside, v_pair.astype(single), 0.0).astype(half)
                first.append((dot(k_one, q_one, NT), dot(v_one, d_pair, NT)))
            dks, dvs = [], []
            for parity, (s, dp) in enumerate(first):
                h = pair * 2 + parity
                p = jnp.exp(s - lse_ref[seq * quads + quad, h : h + 1, :])
                delta = jnp.sum(prod_t[h * HD : (h + 1) * HD], axis=0, keepdims=True)
                ds = (p * (dp - delta)).astype(half)
                dvs.append(dot(p.astype(half), d_pair))
                dks.append(dot(ds, q_pair))
                dqt.append((dot(kt[h * HD : (h + 1) * HD], ds) * scale).astype(half))
            dk_ref[tokens, side] = (jnp.where(low_half, dks[0], dks[1]) * scale).astype(half)
            dv = jnp.where(low_half, dvs[0], dvs[1]).astype(half)
            dv_ref[tokens, side] = dv
            sums_ref[1:2, side] += column_sum(dv.astype(single))
        dq = jnp.concatenate(dqt, axis=0).T
        dq_ref[tokens, :] = dq
        sums_ref[0:1, :] += column_sum(dq.astype(single))


def attention_back(lengths, after, q, k, v, ctx, dctx, lse, length, quad):
    rows = q.shape[0]
    return call(
        functools.partial(attention_back_kernel, length=length, quad=quad),
        f"attention_back_{quad}",
        [(lengths, "s"), (after, "a")] + [(a, "v") for a in (q, k, v, ctx, dctx, lse)],
        [(near((rows, 256), half), "v")] * 3 + [(near((8, 256)), "v")],
    )


def outer_half(me, act_ref, ddown_ref, y):
    part = act_ref.shape[1] // 4
    return dot(act_ref[:, at(2 * y + me, part)], ddown_ref[...], TN)


TABLE = 32


def table_rows(pos_ref, task_ref, sums2, out, classes, tables):
    width = out.shape[1]
    out[...] = jnp.zeros_like(out)
    out[0:3, :] = sums2[0:3]
    lane = lax.broadcasted_iota(jnp.int32, (1, width), 1)
    out[3:4, :] = jnp.where(lane == pos_ref[6], sums2[7:8], 0.0)
    for t in range(tables):
        mine = jnp.where(task_ref[0] == t, 1.0, 0.0)
        out[4 + t * classes : 4 + (t + 1) * classes, :] = sums2[3 : 3 + classes] * mine


def outer_send_kernel(pos_ref, task_ref, after_ref, act_ref, ddown_ref, sums2, send_ref, table_ref, *, classes, tables):
    part = act_ref.shape[1] // 4
    for y in range(2):
        send_ref[y * part : (y + 1) * part, :] = outer_half(1 - pos_ref[1], act_ref, ddown_ref, y)
    table_rows(pos_ref, task_ref, sums2, table_ref, classes, tables)
    send_ref[2 * part :, :] = table_ref[...]


def outer_rest_kernel(pos_ref, after_ref, act_ref, ddown_ref, rest_ref):
    for y in range(2):
        rest_ref[y] = outer_half(pos_ref[1], act_ref, ddown_ref, y)


def outer_send(pos, task_ids, after, act, ddown, sums2, classes, tables):
    width = ddown.shape[1]
    assert 4 + classes * tables <= TABLE
    return call(
        functools.partial(outer_send_kernel, classes=classes, tables=tables),
        "outer_weight_send",
        [(pos, "s"), (task_ids, "s"), (after, "a"), (act, "v"), (ddown, "v"), (sums2, "v")],
        [(near((act.shape[1] // 2 + TABLE, width)), "v"), (near((TABLE, width)), "v")],
    )


def outer_rest(pos, after, act, ddown):
    return call(
        outer_rest_kernel,
        "outer_weight_rest",
        [(pos, "s"), (after, "a"), (act, "v"), (ddown, "v")],
        [(near((2, act.shape[1] // 4, ddown.shape[1])), "v")],
    )[0]


def split_x(pos, block, rows, cols, lead, sx, kx, to):
    me = pos[2]
    for z in range(4):
        zero = block[(2 * z) * rows : (2 * z + 1) * rows, cols]
        one = block[(2 * z + 1) * rows : (2 * z + 2) * rows, cols]
        sx[lead + (z, slice(None), to)] = jnp.where(me == 0, one, zero)
        kx[lead + (z, slice(None), to)] = jnp.where(me == 0, zero, one)


def split_z(pos, block, rows, cols, lead, sz, kz, to):
    side = pos[3]
    for x in range(2):
        zs = [block[(2 * z + x) * rows : (2 * z + x + 1) * rows, cols] for z in range(4)]
        for hi, (even, odd) in enumerate(((0, 1), (3, 2))):
            sz[lead + (hi, x, slice(None), to)] = jnp.where(side == 0, zs[odd], zs[even])
            kz[lead + (hi, x, slice(None), to)] = jnp.where(side == 0, zs[even], zs[odd])


def split_y(pos, data, rows, sy, ky, to):
    me = pos[0]
    zero = data[: 8 * rows].reshape(4, 2, rows, data.shape[1])
    one = data[8 * rows :].reshape(4, 2, rows, data.shape[1])
    sy[:, :, :, to] = jnp.where(me == 0, one, zero)
    ky[:, :, :, to] = jnp.where(me == 0, zero, one)


def outer_keep_kernel(
    pos_ref, after_ref, own_ref, got_ref, table_ref, sx_ref, kx_ref, sy_ref, ky_ref, sz_ref, kz_ref, block_ref
):
    third, part = own_ref.shape[2] // 3, own_ref.shape[1]
    rows = own_ref.shape[1] // 8
    me_y, me_x, side = pos_ref[0], pos_ref[2], pos_ref[3]
    xs, ys, zs = [slice(i * third, (i + 1) * third) for i in range(3)]

    def at_rows(y, z, x, cols):
        begin = (2 * z + x) * rows
        there = y * part + begin
        return own_ref[y, begin : begin + rows, cols] + got_ref[there : there + rows, cols]

    table = table_ref[...] + got_ref[2 * part :, :]
    block_ref[...] = jnp.concatenate([table[:, i * third : (i + 1) * third] for i in range(3)], axis=0)
    sx_ref[8] = block_ref[...]

    for y in range(2):
        for z in range(4):
            zero, one = at_rows(y, z, 0, xs), at_rows(y, z, 1, xs)
            sx_ref[4 * y + z] = jnp.where(me_x == 0, one, zero)
            kx_ref[4 * y + z] = jnp.where(me_x == 0, zero, one)
        for x in range(2):
            for hi, (even, odd) in enumerate(((0, 1), (3, 2))):
                zero, one = at_rows(y, even, x, zs), at_rows(y, odd, x, zs)
                sz_ref[y, hi, x] = jnp.where(side == 0, one, zero)
                kz_ref[y, hi, x] = jnp.where(side == 0, zero, one)
    for z in range(4):
        for x in range(2):
            zero, one = at_rows(0, z, x, ys), at_rows(1, z, x, ys)
            sy_ref[z, x] = jnp.where(me_y == 0, one, zero)
            ky_ref[z, x] = jnp.where(me_y == 0, zero, one)


def outer_keep(pos, after, own, got, table):
    width = own.shape[2]
    r, third = own.shape[1] // 8, width // 3
    assert 3 * TABLE == r and third == 256
    shapes = [(9, r, third), (8, r, third)] + [(4, 2, r, third)] * 2 + [(2, 2, 2, r, third)] * 2 + [(r, third)]
    return call(
        outer_keep_kernel,
        "outer_weight_keep",
        [(pos, "s"), (after, "a"), (own, "v"), (got, "v"), (table, "v")],
        [(near(s), "v") for s in shapes],
    )


def row_half(left_ref, me):
    quarter = left_ref.shape[0] // 4
    return jnp.concatenate([left_ref[at(me, quarter), :], left_ref[at(2 + me, quarter), :]], axis=0)


def inner_send_kernel(pos_ref, after_ref, left_ref, right_ref, send_ref, *, other):
    me = 1 - pos_ref[1] if other else pos_ref[1]
    left = row_half(left_ref, me)
    parts, _, columns = send_ref.shape
    for j in range(parts):
        send_ref[j] = dot(left, right_ref[:, j * columns : (j + 1) * columns])


def inner_send(pos, after, left_t, right, other):
    width = left_t.shape[0]
    return call(
        functools.partial(inner_send_kernel, other=other),
        "inner_weight_send",
        [(pos, "s"), (after, "a"), (left_t, "v"), (right, "v")],
        [(near((2, width // 2, right.shape[1] // 2)), "v")],
    )[0]


def inner_keep_kernel(pos_ref, after_ref, left_ref, right_ref, got_ref, sx_ref, kx_ref, sy_ref, ky_ref):
    left = row_half(left_ref, pos_ref[1])
    count, columns = got_ref.shape[1:]
    rows = count // 16

    def block(j):
        return dot(left, right_ref[:, j * columns : (j + 1) * columns]) + got_ref[j]

    data = block(0)
    for y in range(2):
        sub = slice(y * 8 * rows, (y + 1) * 8 * rows)
        split_x(pos_ref, data[sub], rows, slice(None), (y,), sx_ref, kx_ref, slice(None))
    split_y(pos_ref, block(1), rows, sy_ref, ky_ref, slice(None))


def inner_keep(pos, after, left_t, right, got):
    r = left_t.shape[0] // 32
    wide = right.shape[1] // 2
    shapes = [(2, 4, r, wide)] * 2 + [(4, 2, r, wide)] * 2
    return call(
        inner_keep_kernel,
        "inner_weight_keep",
        [(pos, "s"), (after, "a")] + [(a, "v") for a in (left_t, right, got)],
        [(near(s), "v") for s in shapes],
    )


SMALL = 8


def small_rows(sums0, sums1, inner_bias, out, base):
    width = sums1.shape[1]
    count = inner_bias.shape[0]
    lanes = slice(0, width)
    out[base : base + SMALL, :] = jnp.zeros((SMALL, out.shape[1]), single)
    for g, sums in enumerate(sums0):
        out[base : base + 2, g * 256 : (g + 1) * 256] = sums[0:2]
    out[base + 2 : base + 5, lanes] = sums1[0:3]
    out[base + 5 : base + 4 + count, lanes] = inner_bias[: count - 1, :]
    for i in range(3):
        out[base + i : base + i + 1, width:] = inner_bias[count - 1 : count, i * 256 : (i + 1) * 256]


def quad_grads(me, left_ref, ctxt_ref, dattn_ref, parts, g):
    left = row_half(left_ref, me)
    pieces = [dot(left, part[...]) for part in parts[3 * g : 3 * g + 3]]
    pieces.append(dot(row_half(ctxt_ref, me), dattn_ref[:, g * 256 : (g + 1) * 256]))
    return pieces


def qkv_send_kernel(pos_ref, after_ref, left_ref, ctxt_ref, dattn_ref, *refs, other, quads):
    parts, refs = refs[: 3 * quads], refs[3 * quads :]
    sums0, refs = refs[:quads], refs[quads:]
    sums1, inner_bias, send_ref = refs
    me = 1 - pos_ref[1] if other else pos_ref[1]
    count = left_ref.shape[0] // 2
    for g in range(quads):
        for t, piece in enumerate(quad_grads(me, left_ref, ctxt_ref, dattn_ref, parts, g)):
            send_ref[g * count : (g + 1) * count, t * 256 : (t + 1) * 256] = piece
    small_rows(sums0, sums1, inner_bias, send_ref, quads * count)


def qkv_send(pos, after, xt, ctxt, dattn, parts, sums0, sums1, inner_bias, other):
    width = xt.shape[0]
    assert inner_bias.shape[0] == 4 and width == 768
    return call(
        functools.partial(qkv_send_kernel, other=other, quads=len(sums0)),
        "qkv_weight_send",
        [(pos, "s"), (after, "a"), (xt, "v"), (ctxt, "v"), (dattn, "v")]
        + [(p, "v") for p in (*parts, *sums0, sums1, inner_bias)],
        [(near((len(sums0) * (width // 2) + SMALL, 1024)), "v")],
    )[0]


def rows24_from(base, index, r):
    return pl.ds(pl.multiple_of(base + index * r, 8), r)


def rows24(index, r):
    return pl.ds(pl.multiple_of(index * r, 8), r)


def pack(out, row, block):
    r, w = block.shape[0] // 4, block.shape[1]
    for j in range(4):
        out[row : row + r, j * w : (j + 1) * w] = block[j * r : (j + 1) * r]


def third_outer_kernel(pos_ref, after_ref, xk, xr, yk, yr, zk, zr, block, sent, kept, zs, zn, table_out):
    me_x, side = pos_ref[2], pos_ref[3]
    rows, wide = xk.shape[1:]
    for hi, (keep, send) in enumerate(((side, 1 - side), (3 - side, 2 + side))):
        to = slice(hi * rows, (hi + 1) * rows)
        sent[to, :wide] = xk[send] + xr[send]
        sent[to, wide:] = yk[send] + yr[send]
        kept[to, :wide] = xk[keep] + xr[keep]
        kept[to, wide:] = yk[keep] + yr[keep]
    table = block[...] + xr[4]
    table = jnp.concatenate([table[: rows // 2], table[rows // 2 :]], axis=1)
    table_out[...] = table
    sent[2 * rows :, :] = table
    r = rows // 4
    for y in range(2):
        pack(zs, y * r, zk[y, 1 - me_x] + zr[y, 1 - me_x])
        pack(zn, y * r, zk[y, me_x] + zr[y, me_x])


def third_outer(pos, after, *arrays):
    r, wide = arrays[0].shape[1:]
    shapes = [(2 * r + r // 2, 2 * wide), (2 * r, 2 * wide)] + [(r // 2, 4 * wide)] * 2 + [(r // 2, 2 * wide)]
    return call(
        third_outer_kernel,
        "third_outer_stage",
        [(pos, "s"), (after, "a")] + [(a, "v") for a in arrays],
        [(near(s), "v") for s in shapes],
    )


def fourth_outer_kernel(pos_ref, after_ref, k, got, table, sent, kept, table_out):
    me_hi = pos_ref[4]
    rows = k.shape[0] // 2
    there, here = rows24(1 - me_hi, rows), rows24(me_hi, rows)
    sent[:rows, :] = k[there, :] + got[there, :]
    kept[...] = k[here, :] + got[here, :]
    total = table[...] + got[2 * rows :, :]
    table_out[...] = total
    sent[rows:, :] = total


def fourth_outer_stage(pos, after, k, got, table):
    rows, wide = k.shape[0] // 2, k.shape[1]
    shapes = [(rows + rows // 2, wide), (rows, wide), (rows // 2, wide)]
    return call(
        fourth_outer_kernel,
        "fourth_stage_outer",
        [(pos, "s"), (after, "a"), (k, "v"), (got, "v"), (table, "v")],
        [(near(s), "v") for s in shapes],
    )


def qkv_keep_kernel(pos_ref, after_ref, left_ref, ctxt_ref, dattn_ref, own_ref, got_ref, ozs, *refs):
    *parts, sx, kx, sy, ky, sz, kz, small = refs
    count, width = left_ref.shape[0] // 2, left_ref.shape[0]
    r = width // 32
    me_y, me_c, me_x, side = pos_ref[0], pos_ref[1], pos_ref[2], pos_ref[3]
    total = own_ref[3 * count :, :] + got_ref[3 * count :, :]
    small[...] = total
    sy[8 * r :, :] = total
    sx[8 * r :, :] = ozs[...]

    def grads(g):
        for t, piece in enumerate(quad_grads(me_c, left_ref, ctxt_ref, dattn_ref, parts, g)):
            cols = slice(t * 256, (t + 1) * 256)
            yield cols, piece + got_ref[g * count : (g + 1) * count, cols]

    for cols, g in grads(0):
        for y in range(2):
            for x in range(2):
                zs = [g[(y * 8 + z * 2 + x) * r : (y * 8 + z * 2 + x + 1) * r] for z in range(4)]
                for hi, (even, odd) in enumerate(((0, 1), (3, 2))):
                    begin = ((y * 2 + hi) * 2 + x) * r
                    sz[begin : begin + r, cols] = jnp.where(side == 0, zs[odd], zs[even])
                    kz[begin : begin + r, cols] = jnp.where(side == 0, zs[even], zs[odd])
    for cols, g in grads(1):
        for y in range(2):
            for z in range(4):
                begin = (y * 8 + z * 2) * r
                zero, one = g[begin : begin + r], g[begin + r : begin + 2 * r]
                to = slice((y * 4 + z) * r, (y * 4 + z + 1) * r)
                sx[to, cols] = jnp.where(me_x == 0, one, zero)
                kx[to, cols] = jnp.where(me_x == 0, zero, one)
    for cols, g in grads(2):
        sy[: 8 * r, cols] = jnp.where(me_y == 0, g[8 * r :], g[: 8 * r])
        ky[:, cols] = jnp.where(me_y == 0, g[: 8 * r], g[8 * r :])


def qkv_keep(pos, after, xt, ctxt, dattn, own, got, ozs, parts):
    width = xt.shape[0]
    r = width // 32
    wide = own.shape[1]
    shapes = [(n, wide) for n in (10 * r, 8 * r, 8 * r + SMALL, 8 * r, 8 * r, 8 * r, SMALL)]
    return call(
        qkv_keep_kernel,
        "qkv_weight_keep",
        [(pos, "s"), (after, "a")]
        + [(a, "v") for a in (xt, ctxt, dattn, own, got, ozs, *parts)],
        [(near(n), "v") for n in shapes],
    )


def second_qkv_kernel(pos_ref, after_ref, kx, rx, ky, ry, kz, rz, small, oz, xs, xk, ys, yk, zs, zk, small_out, oz_out):
    me_y, me_x, me_hi = pos_ref[0], pos_ref[2], pos_ref[4]
    r = kx.shape[0] // 8
    total = small[...] + ry[8 * r :, :]
    small_out[...] = total
    ys[4 * r :, :] = total
    base = 8 * r
    xs[4 * r :, :] = oz[rows24(1 - me_y, r), :] + rx[rows24_from(base, 1 - me_y, r), :]
    oz_out[...] = oz[rows24(me_y, r), :] + rx[rows24_from(base, me_y, r), :]
    there, here = rows24(1 - me_y, 4 * r), rows24(me_y, 4 * r)
    xs[: 4 * r, :] = kx[there, :] + rx[there, :]
    xk[...] = kx[here, :] + rx[here, :]
    for z in range(4):
        there, here = rows24(2 * z + 1 - me_x, r), rows24(2 * z + me_x, r)
        to = slice(z * r, (z + 1) * r)
        ys[to, :] = ky[there, :] + ry[there, :]
        yk[to, :] = ky[here, :] + ry[here, :]
    for y in range(2):
        there, here = rows24(2 * y + 1 - me_hi, 2 * r), rows24(2 * y + me_hi, 2 * r)
        to = slice(y * 2 * r, (y + 1) * 2 * r)
        zs[to, :] = kz[there, :] + rz[there, :]
        zk[to, :] = kz[here, :] + rz[here, :]


def third_qkv_kernel(pos_ref, after_ref, xk, xr, yk, yr, zk, zr, small, sent, kept, zs, zn, small_out):
    me_x, side = pos_ref[2], pos_ref[3]
    r = xk.shape[0] // 4
    total = small[...] + yr[4 * r :, :]
    small_out[...] = total
    sent[4 * r :, :] = total
    for i, (k, got) in enumerate(((xk, xr), (yk, yr))):
        for hi, (keep, send) in enumerate(((side, 1 - side), (3 - side, 2 + side))):
            there, here = rows24(send, r), rows24(keep, r)
            to = slice((2 * i + hi) * r, (2 * i + hi + 1) * r)
            sent[to, :] = k[there, :] + got[there, :]
            kept[to, :] = k[here, :] + got[here, :]
    for y in range(2):
        there, here = rows24(2 * y + 1 - me_x, r), rows24(2 * y + me_x, r)
        to = slice(y * r, (y + 1) * r)
        zs[to, :] = zk[there, :] + zr[there, :]
        zn[to, :] = zk[here, :] + zr[here, :]


def fourth_qkv_kernel(pos_ref, after_ref, k, got, zk, zr, small, sent, kept, zs, zn, small_out):
    me_y, me_hi = pos_ref[0], pos_ref[4]
    r = k.shape[0] // 4
    total = small[...] + got[4 * r :, :]
    small_out[...] = total
    sent[2 * r :, :] = total
    for i in range(2):
        there, here = rows24(2 * i + 1 - me_hi, r), rows24(2 * i + me_hi, r)
        to = slice(i * r, (i + 1) * r)
        sent[to, :] = k[there, :] + got[there, :]
        kept[to, :] = k[here, :] + got[here, :]
    there, here = rows24(1 - me_y, r), rows24(me_y, r)
    zs[...] = zk[there, :] + zr[there, :]
    zn[...] = zk[here, :] + zr[here, :]


def qkv_stage(kernel, name, pos, after, arrays, counts):
    wide = arrays[0].shape[1]
    return call(
        kernel,
        name,
        [(pos, "s"), (after, "a")] + [(a, "v") for a in arrays],
        [(near((n, wide)), "v") for n in counts],
    )


def sum_outer_kernel(after_ref, k, got, table, out, table_out):
    rows, wide = k.shape
    out[...] = k[...] + got[:rows, :]
    total = table[...] + got[rows:, :]
    block = jnp.concatenate([total[:, : wide // 2], total[:, wide // 2 :]], axis=0)
    for i in range(3):
        table_out[:, i * 256 : (i + 1) * 256] = block[i * TABLE : (i + 1) * TABLE]


def sum_outer_stage(after, k, got, table):
    return call(
        sum_outer_kernel,
        "sum",
        [(after, "a"), (k, "v"), (got, "v"), (table, "v")],
        [(near(k.shape), "v"), (near((TABLE, 768)), "v")],
    )


def last_outer_kernel(after_ref, xy, zk, zr, out, done):
    done[...] = jnp.zeros_like(done)
    wide = xy.shape[1]
    out[:, :wide] = xy[...]
    r = zk.shape[0]
    z = zk[...] + zr[4 * r :, :]
    w = z.shape[1] // 4
    for j in range(4):
        out[j * r : (j + 1) * r, wide:] = z[:, j * w : (j + 1) * w]


def last_outer(after, xy, zk, zr):
    shape = (xy.shape[0], xy.shape[1] + zk.shape[1] // 4)
    return call(
        last_outer_kernel,
        "last_outer_stage",
        [(after, "a")] + [(a, "v") for a in (xy, zk, zr)],
        [(far(shape), "v"), (near((8, 128)), "v")],
    )


def last_qkv_kernel(pos_ref, k, got, zk, zr, small, table, q_out, k_out, v_out, o_out, *outs, classes, bias_rows):
    *vectors, inner_out, loss_out, head_out = outs
    r = zk.shape[0]
    width = table.shape[1]
    xs = k[:r, :] + got[:r, :]
    ys = k[r:, :] + got[r : 2 * r, :]
    zs = zk[...] + zr[...]
    for t, out in enumerate((q_out, k_out, v_out, o_out)):
        for g, data in enumerate((zs, xs, ys)):
            out[:, g * 256 : (g + 1) * 256] = data[:, t * 256 : (t + 1) * 256]
    small_sum = small[...] + got[2 * r :, :]
    total = small_sum[:, :width]
    tables = table[...]
    me = pos_ref[5]
    shift = lax.rem(width - me * r, width)
    rolled, rolled_table = pltpu.roll(total, shift, 1), pltpu.roll(tables[:8], shift, 1)
    for i, out in enumerate(vectors):
        out[...] = rolled[i : i + 1, :r] if i < 5 else rolled_table[i - 5 : i - 4, :r]
    part = inner_out.shape[1]
    per_row = width // part
    row = lax.broadcasted_iota(jnp.int32, total.shape, 0)
    tail = jnp.concatenate([small_sum[i : i + 1, width:] for i in range(3)], axis=1)
    mine = me // per_row
    one = jnp.sum(jnp.where(row == 5 + mine, total, 0.0), axis=0, keepdims=True)
    one = jnp.where(mine == bias_rows - 1, tail, one)
    one = jnp.broadcast_to(one, (8, width))
    inner_out[...] = pltpu.roll(one, lax.rem(width - (me % per_row) * part, width), 1)[0:1, :part]
    lane = lax.broadcasted_iota(jnp.int32, (1, width), 1)
    loss_out[...] = jnp.sum(jnp.where(lane == pos_ref[6], tables[3:4], 0.0), axis=1, keepdims=True)
    for t in range(head_out.shape[0]):
        head_out[t] = tables[4 + t * classes : 4 + (t + 1) * classes]


def last_qkv(pos, k, got, zk, zr, small, table, classes, tables, bias_rows):
    r, width = zk.shape[0], table.shape[1]
    shapes = [(r, width)] * 4 + [(1, r)] * 8 + [(1, r * bias_rows), (1, 1), (tables, classes, width)]
    return call(
        functools.partial(last_qkv_kernel, classes=classes, bias_rows=bias_rows),
        "last_qkv_stage",
        [(pos, "s")] + [(a, "v") for a in (k, got, zk, zr, small, table)],
        [(far(s), "v") for s in shapes],
    )


def token_grad_kernel(after_ref, dr1_ref, wq_ref, wk_ref, wv_ref, *refs):
    *parts, out_hbm, done_ref, out_ref, sems = refs
    done_ref[...] = jnp.zeros_like(done_ref)
    rows = out_ref.shape[0]
    quads = len(parts) // 3

    @pl.loop(0, rows // TILE)
    def _(step):
        tile = at(step, TILE)
        total = dr1_ref[tile, :]
        for t, w_ref in enumerate((wq_ref, wk_ref, wv_ref)):
            d = jnp.concatenate([parts[g * 3 + t][tile, :] for g in range(quads)], axis=1)
            total = total + dot(d, w_ref[...], NT)
        out_ref[tile, :] = total
        pltpu.make_async_copy(out_ref.at[tile, :], out_hbm.at[tile, :], sems.at[step]).start()

    for i in range(rows // TILE):
        tile = pl.ds(i * TILE, TILE)
        pltpu.make_async_copy(out_ref.at[tile, :], out_hbm.at[tile, :], sems.at[i]).wait()


def token_grads(after, dr1, wq, wk, wv, parts):
    rows, width = dr1.shape
    return call(
        token_grad_kernel,
        "token_grad",
        [(after, "a")] + [(a, "v") for a in (dr1, wq, wk, wv, *parts)],
        [(far((rows, width)), "a"), (near((8, 128)), "v")],
        [pltpu.VMEM((rows, width), single), pltpu.SemaphoreType.DMA((rows // TILE,))],
    )


def second_outer_kernel(pos_ref, after_ref, kx, rx, ky, ry, kz, rz, block, xs, xk, ys, yk, zs, zk, block_out):
    me_y, me_x, me_hi = pos_ref[0], pos_ref[2], pos_ref[4]
    table = block[...] + rx[8]
    block_out[...] = table
    xs[4] = table
    for z in range(4):
        there, here = 4 * (1 - me_y) + z, 4 * me_y + z
        xs[z] = kx[there] + rx[there]
        xk[z] = kx[here] + rx[here]
    ys[...] = ky[:, 1 - me_x] + ry[:, 1 - me_x]
    yk[...] = ky[:, me_x] + ry[:, me_x]
    zs[...] = kz[:, 1 - me_hi] + rz[:, 1 - me_hi]
    zk[...] = kz[:, me_hi] + rz[:, me_hi]


def second_outer_stage(pos, after, *arrays):
    r, third = arrays[0].shape[1:]
    shapes = [(5, r, third)] + [(4, r, third)] * 3 + [(2, 2, r, third)] * 2 + [(r, third)]
    return call(
        second_outer_kernel,
        "second_stage_outer",
        [(pos, "s"), (after, "a")] + [(a, "v") for a in arrays],
        [(near(s), "v") for s in shapes],
    )


def second_kernel(pos_ref, after_ref, kx, rx, ky, ry, xs, xk, ys, yk):
    me_y, me_x = pos_ref[0], pos_ref[2]
    xs[...] = kx[1 - me_y] + rx[1 - me_y]
    xk[...] = kx[me_y] + rx[me_y]
    ys[...] = ky[:, 1 - me_x] + ry[:, 1 - me_x]
    yk[...] = ky[:, me_x] + ry[:, me_x]


def second(pos, after, kx, rx, ky, ry):
    return call(
        second_kernel,
        "second_stage_inner",
        [(pos, "s"), (after, "a")] + [(a, "v") for a in (kx, rx, ky, ry)],
        [(near((4,) + kx.shape[2:]), "v")] * 4,
    )


def third_kernel(pos_ref, after_ref, xk, xr, yk, yr, *refs):
    me_x, side = pos_ref[2], pos_ref[3]
    wide = xk.shape[2]
    if len(refs) == 2:
        sent, kept = refs
    else:
        zk, zr, sent, kept, zs, zn = refs
        zs[...] = zk[:, 1 - me_x] + zr[:, 1 - me_x]
        zn[...] = zk[:, me_x] + zr[:, me_x]
    for hi, (keep, send) in enumerate(((side, 1 - side), (3 - side, 2 + side))):
        sent[hi, :, :wide] = xk[send] + xr[send]
        sent[hi, :, wide:] = yk[send] + yr[send]
        kept[hi, :, :wide] = xk[keep] + xr[keep]
        kept[hi, :, wide:] = yk[keep] + yr[keep]


def third(pos, after, xk, xr, yk, yr, zk=None, zr=None):
    r, wide = xk.shape[1:]
    inputs = [xk, xr, yk, yr]
    shapes = [(2, r, 2 * wide)] * 2
    if zk is not None:
        inputs += [zk, zr]
        shapes += [(2,) + zk.shape[2:]] * 2
    return call(
        third_kernel,
        "third_stage",
        [(pos, "s"), (after, "a")] + [(a, "v") for a in inputs],
        [(near(s), "v") for s in shapes],
    )


def fourth_kernel(pos_ref, after_ref, xyk, xyr, *refs):
    me_y, me_hi = pos_ref[0], pos_ref[4]
    if len(refs) == 2:
        sent, kept = refs
    else:
        zk, zr, sent, kept, zs, zn = refs
        zs[...] = zk[1 - me_y] + zr[1 - me_y]
        zn[...] = zk[me_y] + zr[me_y]
    sent[...] = xyk[1 - me_hi] + xyr[1 - me_hi]
    kept[...] = xyk[me_hi] + xyr[me_hi]


def fourth(pos, after, xyk, xyr):
    return call(
        fourth_kernel,
        "fourth_stage_inner",
        [(pos, "s"), (after, "a"), (xyk, "v"), (xyr, "v")],
        [(near(xyk.shape[1:]), "v")] * 2,
    )


def last_kernel(after_ref, xyk, xyr, *refs, layout):
    count = len(layout)
    outs = refs[-count - 1 : -1]
    refs[-1][...] = jnp.zeros_like(refs[-1])
    sources = [(xyk, xyr), refs[:2]]
    for out, pieces in zip(outs, layout):
        to = 0
        for source, begin, end in pieces:
            a, b = sources[source]
            out[:, to : to + end - begin] = a[:, begin:end] + b[:, begin:end]
            to += end - begin


def last(after, xyk, xyr, zk, zr, layout):
    inputs = [xyk, xyr] + ([] if zk is None else [zk, zr])
    shapes = [(xyk.shape[0], sum(e - b for _, b, e in pieces)) for pieces in layout]
    return call(
        functools.partial(last_kernel, layout=layout),
        "last_stage",
        [(after, "a")] + [(a, "v") for a in inputs],
        [(far(s), "v") for s in shapes] + [(near((8, 128)), "v")],
    )


def pair_list(change):
    pairs = []
    for y in range(2):
        for c in range(2):
            for z in range(4):
                for x in range(2):
                    py, pc, pz, px = change(y, c, z, x)
                    pairs.append((((y * 2 + c) * 4 + z) * 2 + x, ((py * 2 + pc) * 4 + pz) * 2 + px))
    return pairs


PAIRS = {
    "y": pair_list(lambda y, c, z, x: (1 - y, c, z, x)),
    "c": pair_list(lambda y, c, z, x: (y, 1 - c, z, x)),
    "x": pair_list(lambda y, c, z, x: (y, c, z, 1 - x)),
    "near": pair_list(lambda y, c, z, x: (y, c, z ^ 1, x)),
    "far": pair_list(lambda y, c, z, x: (y, c, 3 - z, x)),
}


def swap(array, name):
    return lax.ppermute(array, ALL_AXES, PAIRS[name])


def per_device(
    tokens,
    out_cot,
    lengths,
    labels,
    task_ids,
    task_weights,
    query_weight,
    key_weight,
    value_weight,
    query_bias,
    value_bias,
    output_weight,
    output_bias,
    norm1_gain,
    norm1_bias,
    inner_weight,
    inner_bias,
    outer_weight,
    outer_bias,
    norm2_gain,
    norm2_bias,
    head_table,
    *,
    staged,
):
    seqs, length, width = tokens.shape
    rows = seqs * length
    ff = inner_weight.shape[1]
    group_seqs = seqs * lax.axis_size("batch")
    task_index = lax.axis_index("task")
    batch_index = lax.axis_index("batch")
    my_y, my_c, my_z, my_x = task_index // 2, task_index % 2, batch_index // 2, batch_index % 2
    my_hi = my_z // 2
    my_side = (my_z // 2) ^ (my_z % 2)
    where = task_index * lax.axis_size("batch") + batch_index
    pos = jnp.stack([my_y, my_c, my_x, my_side, my_hi, where, task_index]).astype(jnp.int32)
    vectors = (output_bias, norm1_gain, norm1_bias, inner_bias, outer_bias, norm2_gain, norm2_bias)

    x, q, k, v, ctx, ctxt, lse, wo, wi, wd, cot = attention(
        tokens,
        lengths,
        query_weight,
        key_weight,
        value_weight,
        query_bias,
        value_bias,
        output_weight,
        inner_weight,
        outer_weight,
        out_cot,
    )
    block_out, normed1, root1, h1t, act, slope, ddown, sums2 = middle(
        x, ctx, cot, length, labels, task_ids, task_weights, wo, wi, wd, vectors, head_table.transpose(1, 0, 2), group_seqs
    )
    block_out = block_out.reshape(tokens.shape)

    classes, tables = head_table.shape[1], head_table.shape[0]
    f2, r, quads = ff // 2, width // 32, width // 256
    parts, sums0 = [None] * (3 * quads), [None] * quads

    def back(quad, after):
        *grads, sums = attention_back(lengths, after, q, k, v, ctx, e["dctx"], lse, length, quad)
        parts[3 * quad : 3 * quad + 3] = grads
        sums0[quad] = sums
        return sums

    def small_args():
        return (ctxt, e["dattn"], parts, sums0, e["sums1"], e["inner_bias"])

    e = {}

    def send_outer(after):
        e["o_send"], e["table"] = outer_send(pos, task_ids, after, act, ddown, sums2, classes, tables)
        return e["table"]

    def rest_outer(after):
        e["o_rest"] = outer_rest(pos, after, act, ddown)
        return e["o_rest"]

    def do_inner_grad(after):
        e["dinner"], e["inner_bias"] = inner_grad(after, ddown, wd, slope)
        return e["inner_bias"]

    def send_inner(after):
        e["i_send"] = inner_send(pos, after, h1t, e["dinner"], True)
        return e["i_send"]

    def do_first_norm(after):
        e["dr1"], e["dattn"], e["dctx"], e["xt"], e["sums1"] = first_norm(
            after,
            e["dinner"],
            inner_weight,
            ddown,
            normed1,
            root1,
            output_weight,
            norm1_gain,
            tokens.reshape(rows, width),
        )
        return e["sums1"]

    def do_tokens(after):
        e["token_grad"], after = token_grads(after, e["dr1"], query_weight, key_weight, value_weight, parts)
        return after

    def send_qkv(after):
        e["qkv_s"] = qkv_send(pos, after, e["xt"], *small_args(), True)
        return e["qkv_s"]

    def keep_outer(after):
        got = swap(e["o_send"], "c")
        osx, okx, osy, oky, osz, okz, block = outer_keep(pos, after, e["o_rest"], got, e["table"])
        e["o1"] = (okx, swap(osx, "x"), oky, swap(osy, "y"), okz, swap(osz, "near"), block)
        return block

    def keep_inner(after):
        isx, ikx, isy, iky = inner_keep(pos, after, h1t, e["dinner"], swap(e["i_send"], "c"))
        e["i1"] = (ikx, swap(isx, "x"), iky, swap(isy, "y"))
        return ikx

    def second_outer(after):
        xs, xk, ys, yk, zs, zk, block = second_outer_stage(pos, after, *e["o1"])
        e["o2"] = (xk, swap(xs, "y"), yk, swap(ys, "x"), zk, swap(zs, "far"), block)
        return block

    def second_inner(after):
        xs, xk, ys, yk = second(pos, after, *e["i1"])
        e["i2"] = (xk, swap(xs, "y"), yk, swap(ys, "x"))
        return xk

    def do_third_outer(after):
        sent, kept, e["ozs"], e["oz"], table = third_outer(pos, after, *e["o2"])
        e["o3"] = (kept, swap(sent, "near"), table)
        return table

    def third_inner(after):
        sent, kept = third(pos, after, *e["i2"])
        e["i3"] = (kept, swap(sent, "near"))
        return kept

    def fourth_outer(after):
        sent, kept, table = fourth_outer_stage(pos, after, *e["o3"])
        e["o4"] = (kept, swap(sent, "far"), table)
        return table

    def fourth_inner(after):
        sent, kept = fourth(pos, after, *e["i3"])
        e["i4"] = (kept, swap(sent, "far"))
        return kept

    def sum_outer(after):
        e["outer_xy"], e["table_sum"] = sum_outer_stage(after, *e["o4"])
        return e["table_sum"]

    def last_inner(after):
        e["inner_s"], after = last(after, *e["i4"], None, None, (((0, 0, 2 * f2),),))
        return after

    def do_last_outer(after):
        e["outer_s"], after = last_outer(after, e["outer_xy"], e["oz2"], e["q2"][1])
        return after

    def keep_qkv(after):
        sx, kx, sy, ky, sz, kz, small = qkv_keep(
            pos, after, e["xt"], ctxt, e["dattn"], e["qkv_s"], swap(e["qkv_s"], "c"), e["ozs"], parts
        )
        e["q1"] = (kx, swap(sx, "x"), ky, swap(sy, "y"), kz, swap(sz, "near"), small, e["oz"])
        return small

    def stage(kernel, name, after, arrays, counts):
        return qkv_stage(kernel, name, pos, after, arrays, counts)

    def second_qkv(after):
        xs, xk, ys, yk, zs, zk, small, e["oz2"] = stage(
            second_qkv_kernel,
            "second_qkv_stage",
            after,
            e["q1"],
            [5 * r, 4 * r, 4 * r + SMALL, 4 * r, 4 * r, 4 * r, SMALL, r],
        )
        e["q2"] = (xk, swap(xs, "y"), yk, swap(ys, "x"), zk, swap(zs, "far"), small)
        return small

    def third_qkv(after):
        sent, kept, zs, zk, small = stage(
            third_qkv_kernel, "third_qkv_stage", after, e["q2"], [4 * r + SMALL, 4 * r, 2 * r, 2 * r, SMALL]
        )
        e["q3"] = (kept, swap(sent, "near"), zk, swap(zs, "x"), small)
        return small

    def fourth_qkv(after):
        sent, kept, zs, zk, small = stage(
            fourth_qkv_kernel, "fourth_qkv_stage", after, e["q3"], [2 * r + SMALL, 2 * r, r, r, SMALL]
        )
        e["q4"] = (kept, swap(sent, "far"), zk, swap(zs, "y"), small)
        return small

    def do_last_qkv(after):
        e["last"] = last_qkv(pos, *e["q4"], e["table_sum"], classes, tables, ff // width)
        return after

    steps = {
        "send_outer": send_outer,
        "rest_outer": rest_outer,
        "inner_grad": do_inner_grad,
        "send_inner": send_inner,
        "keep_outer": keep_outer,
        "first_norm": do_first_norm,
        "keep_inner": keep_inner,
        "second_outer": second_outer,
        "send_qkv": send_qkv,
        "second_inner": second_inner,
        "third_outer": do_third_outer,
        "keep_qkv": keep_qkv,
        "third_inner": third_inner,
        "tokens": do_tokens,
        "fourth_outer": fourth_outer,
        "second_qkv": second_qkv,
        "sum_outer": sum_outer,
        "third_qkv": third_qkv,
        "fourth_inner": fourth_inner,
        "fourth_qkv": fourth_qkv,
        "last_inner": last_inner,
        "last_outer": do_last_outer,
        "last_qkv": do_last_qkv,
    }
    for quad in range(quads):
        steps[f"back_{quad}"] = functools.partial(back, quad)
    if staged:
        after = sums2
        for name in ORDER:
            after = steps[name](after)
        query_s, key_s, value_s, output_s, *rest = e["last"]
        inner_s, outer_s = e["inner_s"], e["outer_s"]
        vector_s = [v.reshape(-1) for v in rest[:-1]]
        head_grad = rest[-1]
    else:
        after = do_first_norm(send_inner(do_inner_grad(send_outer(sums2))))
        after = rest_outer(after)
        i_keep = inner_send(pos, after, h1t, e["dinner"], False)
        for quad in range(quads):
            after = back(quad, after)
        after = do_tokens(send_qkv(after))
        qkv_k = qkv_send(pos, after, e["xt"], *small_args(), False)
        o_send, i_send, qkv_s = e["o_send"], e["i_send"], e["qkv_s"]

        def whole_rows(sent, kept):
            both = jnp.stack([jnp.where(my_c == 0, kept, sent), jnp.where(my_c == 0, sent, kept)], axis=1)
            return both.reshape(-1, both.shape[-1])

        def scatter(grad):
            return lax.psum_scatter(grad, ALL_AXES, scatter_dimension=0, tiled=True)

        def by_rows(array):
            return array.reshape(2, -1, array.shape[-1])

        part = ff // 4
        outer_s = scatter(whole_rows(o_send[: 2 * part].reshape(2, part, width), e["o_rest"]))
        inner_s = scatter(
            jnp.concatenate([whole_rows(by_rows(i_send[j]), by_rows(i_keep[j])) for j in range(2)], axis=-1)
        )
        count = width // 2

        def tensor(array, t):
            cols = slice(t * 256, (t + 1) * 256)
            return by_rows(jnp.concatenate([array[g * count : (g + 1) * count, cols] for g in range(quads)], axis=1))

        query_s, key_s, value_s, output_s = [
            scatter(whole_rows(tensor(qkv_s, t), tensor(qkv_k, t))) for t in range(4)
        ]
        small = lax.psum(jnp.concatenate([qkv_s[quads * count :, :width], e["inner_bias"], e["table"]]), ALL_AXES)
        devices = lax.axis_size("task") * lax.axis_size("batch")

        def mine(array):
            flat = array.reshape(-1)
            size = flat.shape[0] // devices
            return lax.dynamic_slice(flat, (where * size,), (size,))

        table = small[SMALL + ff // width :]
        vector_s = [mine(a) for a in (*small[:5], *table[:3], small[SMALL : SMALL + ff // width])]
        vector_s.append(lax.dynamic_slice(table, (3, task_index), (1, 1)).reshape(1))
        head_grad = table[4 : 4 + classes * tables].reshape(head_table.shape)
    token_grad = e["token_grad"].reshape(tokens.shape)
    bias_q, bias_v, gain1, bias1, bias_o, gain2, bias2, bias_d, bias_i, loss = vector_s
    return (
        block_out,
        token_grad,
        loss,
        query_s,
        key_s,
        value_s,
        bias_q,
        bias_v,
        output_s,
        bias_o,
        gain1,
        bias1,
        inner_s,
        bias_i,
        outer_s,
        bias_d,
        gain2,
        bias2,
        head_grad,
    )


def solution(mesh):
    rows = P(ALL_AXES)
    plain = P()
    task = P("task")
    staged = mesh.shape["task"] == 4 and mesh.shape["batch"] == 8
    return jax.shard_map(
        functools.partial(per_device, staged=staged),
        mesh=mesh,
        in_specs=(rows, rows, rows, rows, task, task) + (plain,) * 16,
        out_specs=(rows, rows, task) + (rows,) * 15 + (plain,),
        check_vma=False,
    )
```

```python
import functools

import jax
import jax.numpy as jnp
from jax import lax
from jax.experimental import pallas as pl
from jax.experimental.pallas import tpu as pltpu
from jax.sharding import PartitionSpec as P

HD = 64
TILE = 256
ALL_AXES = ("task", "batch")
NN = (((1,), (0,)), ((), ()))
NT = (((1,), (1,)), ((), ()))
TN = (((0,), (0,)), ((), ()))
half = jnp.bfloat16
single = jnp.float32
eps_norm = 1e-12


def dot(left, right, dims=NN):
    return lax.dot_general(left, right, dims, preferred_element_type=single)


ANY = pl.BlockSpec(memory_space=pl.ANY)
SMEM = pl.BlockSpec(memory_space=pltpu.SMEM)
VMEM = pl.BlockSpec(memory_space=pltpu.VMEM)
HBM = pl.BlockSpec(memory_space=pltpu.HBM)


def near(shape, dtype=single):
    return pltpu.VMEM(shape, dtype)


def off(shape, dtype=single):
    return pltpu.HBM(shape, dtype)


def far(shape, dtype=single):
    return jax.ShapeDtypeStruct(shape, dtype)


COSTS = {
    "attention_back_0": 1,
    "attention_back_1": 1000,
    "attention_back_2": 1,
    "first_norm_back": 300,
    "fourth_qkv_stage": 100,
    "fourth_stage_inner": 1,
    "fourth_stage_outer": 1000,
    "inner_grad": 3000,
    "inner_weight_keep": 1000,
    "inner_weight_send": 10000,
    "last_outer_stage": 3000,
    "last_stage": 300,
    "outer_weight_keep": 3000,
    "outer_weight_rest": 1,
    "outer_weight_send": 3000,
    "qkv_weight_keep": 100,
    "qkv_weight_send": 3000,
    "second_qkv_stage": 100,
    "second_stage_inner": 1,
    "second_stage_outer": 3000,
    "sum": 10000,
    "third_outer_stage": 65000,
    "third_qkv_stage": 3000,
    "third_stage": 10000,
    "token_grad": 3000,
}
ORDER = [
    "send_outer",
    "inner_grad",
    "send_inner",
    "rest_outer",
    "keep_outer",
    "keep_inner",
    "first_norm",
    "back_0",
    "second_outer",
    "back_1",
    "back_2",
    "send_qkv",
    "second_inner",
    "third_outer",
    "keep_qkv",
    "third_inner",
    "tokens",
    "fourth_outer",
    "second_qkv",
    "sum_outer",
    "third_qkv",
    "fourth_inner",
    "last_outer",
    "fourth_qkv",
    "last_inner",
    "last_qkv",
]


def call(kernel, name, inputs, outputs, scratch=(), megabytes=7, aliases=None):
    specs = {"v": VMEM, "s": SMEM, "a": ANY, "h": HBM}
    spaces = {"v": pltpu.VMEM, "h": pltpu.HBM}
    arrays = [
        pltpu.with_memory_space_constraint(x, spaces[p]) if p in spaces and (x.ndim > 1 or p == "h") else x for x, p in inputs
    ]
    return pl.pallas_call(
        kernel,
        in_specs=[specs[p] for _, p in inputs],
        out_specs=[specs[p] for _, p in outputs],
        out_shape=[o for o, _ in outputs],
        scratch_shapes=list(scratch),
        input_output_aliases=aliases or {},
        compiler_params=pltpu.CompilerParams(vmem_limit_bytes=megabytes << 20),
        cost_estimate=pl.CostEstimate(flops=COSTS.get(name, 1) * 10**6, bytes_accessed=1024, transcendentals=0),
        name=name,
    )(*arrays)


def at(index, size):
    return pl.ds(pl.multiple_of(index * size, size), size)


def as_row(ref):
    return ref[...].astype(single).reshape(1, -1)


def pair_operands(q, k, parity, dead, scale):
    rows = q.shape[0]
    lane = lax.broadcasted_iota(jnp.int32, (rows, 128), 1)
    inside = (lane // HD) == parity
    spare = lane == HD * (1 - parity)
    q_one = jnp.where(inside, q.astype(single) * scale, jnp.where(spare, 1.0, 0.0)).astype(half)
    k_one = jnp.where(inside, k.astype(single), jnp.where(spare & dead, -1e30, 0.0)).astype(half)
    return q_one, k_one


def attention_kernel(
    n_ref, x_hbm, wq_hbm, wk_hbm, wv_hbm, bq_hbm, bv_hbm, wo_hbm, wi_hbm, wd_hbm, cot_hbm,
    x_ref, q_hbm, k_hbm, v_hbm, ctx_ref, ctxt_hbm, lse_ref, wo_ref, wi_ref, wd_ref, cot_ref,
    ctxt_ref, q_ref, k_ref, v_ref, wq_ref, wk_ref, wv_ref, bq_vmem, bv_vmem, sems, out_sems, ctxt_sems,
    *, length,
):
    rows, width = x_ref.shape
    sides = [pl.ds(i * (rows // 2), rows // 2) for i in range(2)]
    pairs = (
        (x_hbm.at[sides[0], :], x_ref.at[sides[0], :]), (bq_hbm, bq_vmem), (wq_hbm, wq_ref),
        (x_hbm.at[sides[1], :], x_ref.at[sides[1], :]), (bv_hbm, bv_vmem), (wk_hbm, wk_ref), (wv_hbm, wv_ref),
        (wo_hbm, wo_ref), (wi_hbm, wi_ref), (wd_hbm, wd_ref), (cot_hbm, cot_ref),
    )
    copies = [pltpu.make_async_copy(src, dst, sems.at[i]) for i, (src, dst) in enumerate(pairs)]
    for copy in copies[:7]:
        copy.start()
    zero = jnp.zeros((1, width), single)
    leaving = []
    for i, (waits, w_ref, bias, out, out_hbm) in enumerate((
        ((0, 1, 2), wq_ref, bq_vmem, q_ref, q_hbm),
        ((4, 5), wk_ref, None, k_ref, k_hbm),
        ((6,), wv_ref, bv_vmem, v_ref, v_hbm),
    )):
        for wait in waits:
            copies[wait].wait()
        shift = zero if bias is None else as_row(bias)
        for part, side in enumerate(sides):
            if i == 0 and part == 1:
                copies[3].wait()
            out[side, :] = (dot(x_ref[side, :], w_ref[...]) + shift).astype(half)
        if i == 0:
            for copy in copies[7:]:
                copy.start()
        leaving.append(pltpu.make_async_copy(out, out_hbm, out_sems.at[i]))
        leaving[-1].start()

    quads = width // 256

    @pl.loop(0, (rows // length) * quads)
    def _(step):
        seq, quad = step // quads, step % quads
        tokens, cols = at(seq, length), at(quad, 256)
        dead = lax.broadcasted_iota(jnp.int32, (length, 128), 0) >= n_ref[seq]
        q, k, v = q_ref[tokens, cols], k_ref[tokens, cols], v_ref[tokens, cols]
        vt = v.T
        scores = []
        for h in range(4):
            pair = slice(h // 2 * 128, h // 2 * 128 + 128)
            q_one, k_one = pair_operands(q[:, pair], k[:, pair], h % 2, dead, HD**-0.5)
            scores.append(dot(k_one, q_one, NT))
        weights = []
        for s in scores:
            top = jnp.max(s, axis=0, keepdims=True)
            e = jnp.exp(s - top)
            weights.append((e.astype(half), top, jnp.sum(e, axis=0, keepdims=True)))
        parts = []
        for h, (e, top, total) in enumerate(weights):
            parts.append((dot(vt[h * HD : (h + 1) * HD], e) * (1.0 / total)).astype(half))
            lse_ref[step, h : h + 1, :] = top + jnp.log(total)
        ctxt = jnp.concatenate(parts, axis=0)
        ctxt_ref[cols, tokens] = ctxt
        ctx_ref[tokens, cols] = ctxt.T
        pltpu.make_async_copy(ctxt_ref.at[cols, tokens], ctxt_hbm.at[cols, tokens], ctxt_sems.at[step]).start()

    for step in range((rows // length) * quads):
        seq, quad = step // quads, step % quads
        tokens, cols = pl.ds(seq * length, length), pl.ds(quad * 256, 256)
        pltpu.make_async_copy(ctxt_ref.at[cols, tokens], ctxt_hbm.at[cols, tokens], ctxt_sems.at[step]).wait()
    for copy in copies[7:] + leaving:
        copy.wait()


def attention(tokens, lengths, wq, wk, wv, bq, bv, wo, wi, wd, cot):
    seqs, length, width = tokens.shape
    rows = seqs * length
    flat = (rows, width)
    quads = width // 256
    return call(
        functools.partial(attention_kernel, length=length),
        "attention_forward",
        [(lengths, "s"), (tokens.reshape(flat), "h"), (wq, "h"), (wk, "h"), (wv, "h"), (bq, "h"), (bv, "h")]
        + [(wo, "h"), (wi, "h"), (wd, "h"), (cot.reshape(flat), "h")],
        [(near(flat, half), "v")]
        + [(off(flat, half), "h")] * 3
        + [(near(flat, half), "v"), (off((width, rows), half), "h"), (near((seqs * quads, 8, length)), "v")]
        + [(near(w.shape, half), "v") for w in (wo, wi, wd)]
        + [(near(flat, half), "v")],
        [pltpu.VMEM((width, rows), half)]
        + [pltpu.VMEM(flat, half)] * 3
        + [pltpu.VMEM(w.shape, half) for w in (wq, wk, wv, bq, bv)]
        + [pltpu.SemaphoreType.DMA((11,)), pltpu.SemaphoreType.DMA((3,))]
        + [pltpu.SemaphoreType.DMA((seqs * quads,))],
        20,
    )


def norm_parts(resid):
    center = resid - jnp.mean(resid, axis=-1, keepdims=True)
    inv_root = lax.rsqrt(jnp.mean(center * center, axis=-1, keepdims=True) + eps_norm)
    return center * inv_root, inv_root


def norm_back(grad_out, normed, inv_root, gain):
    scaled = grad_out * gain
    return inv_root * (
        scaled
        - jnp.mean(scaled, axis=-1, keepdims=True)
        - normed * jnp.mean(scaled * normed, axis=-1, keepdims=True)
    )


def gelu_parts(u):
    u = u.astype(half)
    w = u * u
    v = jnp.minimum(w, jnp.asarray(36.0, half))
    p = (v * jnp.asarray(-0.00031594874, half) + jnp.asarray(0.0367987, half)) * v + jnp.asarray(0.79771759, half)
    h = jnp.asarray(0.5, half)
    cdf = h + h * jnp.tanh(u * p)
    bell = jnp.exp2(w * jnp.asarray(-0.72134752, half) - jnp.asarray(1.32574806, half))
    return u * cdf, cdf + u * bell


def column_sum(array):
    return jnp.sum(array, axis=0, keepdims=True)


def middle_kernel(
    task_ref, label_ref, weight_ref, x_ref, ctx_ref, cot_ref, wo_ref, wi_ref, wd_ref,
    bo_ref, g1_ref, b1_ref, bi_ref, bd_ref, g2_ref, b2_ref, head_ref,
    out_hbm, normed1_ref, root1_ref, h1t_ref, act_ref, slope_ref, ddown_ref, sums_ref,
    out_ref, sems,
    *, length, group_seqs,
):
    rows, width = x_ref.shape
    ff = wi_ref.shape[1]
    part = 768
    bo, g1, b1, bd, g2, b2 = [as_row(r) for r in (bo_ref, g1_ref, b1_ref, bd_ref, g2_ref, b2_ref)]
    bi = as_row(bi_ref)
    w = weight_ref[0]
    table = head_ref[...].astype(single)
    chosen = lax.broadcasted_iota(jnp.int32, table.shape, 1) == task_ref[0]
    head = jnp.sum(jnp.where(chosen, table, 0.0), axis=1)
    classes = head.shape[0]
    sums_ref[...] = jnp.zeros_like(sums_ref)

    @pl.loop(0, rows // (2 * TILE))
    def _(step):
        tile = at(step, (2 * TILE))
        x = x_ref[tile, :].astype(single)
        normed1, root1 = norm_parts(x + dot(ctx_ref[tile, :], wo_ref[...]) + bo)
        normed1_ref[tile, :] = normed1.astype(half)
        root1_ref[tile, :] = jnp.broadcast_to(root1, ((2 * TILE), 128))
        hidden1 = normed1 * g1 + b1
        h1 = hidden1.astype(half)
        h1t_ref[:, tile] = h1.T

        def inner_part(j):
            return dot(h1, wi_ref[:, j : j + part]) + bi[:, j : j + part]

        down = None
        following = inner_part(0)
        for j in range(0, ff, part):
            inner = following
            if j + part < ff:
                following = inner_part(j + part)
            value, slope = gelu_parts(inner)
            act = value.astype(half)
            act_ref[tile, j : j + part] = act
            slope_ref[tile, j : j + part] = slope.astype(half)
            term = dot(act, wd_ref[j : j + part, :])
            down = term if down is None else down + term
        normed2, root2 = norm_parts(hidden1 + down + bd)
        final = normed2 * g2 + b2
        low = final.astype(half)
        out_ref[tile, :] = low
        pltpu.make_async_copy(out_ref.at[tile, :], out_hbm.at[tile, :], sems.at[step]).start()
        cls = low[0:1].astype(single)
        logits = [jnp.sum(cls * head[c : c + 1], axis=1, keepdims=True) for c in range(classes)]
        top = functools.reduce(jnp.maximum, logits)
        lse = top + jnp.log(sum(jnp.exp(v - top) for v in logits))
        per_seq = length // (2 * TILE)
        label = label_ref[step // per_seq]
        first = jnp.where(step % per_seq == 0, 1.0, 0.0)
        picked = sum(jnp.where(label == c, v, 0.0) for c, v in enumerate(logits))
        slopes = [
            (jnp.exp(v - lse) - jnp.where(label == c, 1.0, 0.0)) * (w / group_seqs * first)
            for c, v in enumerate(logits)
        ]
        d_cls = sum(s * head[c : c + 1] for c, s in enumerate(slopes))
        row = lax.broadcasted_iota(jnp.int32, final.shape, 0)
        d_final = cot_ref[tile, :].astype(single) * w + jnp.where(row == 0, d_cls, 0.0)
        dr2 = norm_back(d_final, normed2, root2, g2)
        ddown = dr2.astype(half)
        ddown_ref[tile, :] = ddown
        sums_ref[0:1] += column_sum(d_final * normed2)
        sums_ref[1:2] += column_sum(d_final)
        sums_ref[2:3] += column_sum(ddown.astype(single))
        for c in range(classes):
            sums_ref[3 + c : 4 + c] += slopes[c] * cls
        sums_ref[7:8] += jnp.broadcast_to((lse - picked) * (w / group_seqs * first), cls.shape)

    for i in range(rows // (2 * TILE)):
        tile = pl.ds(i * (2 * TILE), (2 * TILE))
        pltpu.make_async_copy(out_ref.at[tile, :], out_hbm.at[tile, :], sems.at[i]).wait()


def middle(x, ctx, cot, length, labels, task_ids, task_weights, wo, wi, wd, vectors, head_table, group_seqs):
    rows, width = x.shape
    ff = wi.shape[1]
    assert head_table.shape[0] <= 4
    flat = (rows, width)
    return call(
        functools.partial(middle_kernel, length=length, group_seqs=group_seqs),
        "middle_forward",
        [(task_ids, "s"), (labels, "s"), (task_weights, "s")]
        + [(a, "v") for a in (x, ctx, cot, wo, wi, wd, *vectors, head_table)],
        [(far(flat, half), "a")]
        + [
            (near(flat, half), "v"),
            (near((rows, 128)), "v"),
            (near((width, rows), half), "v"),
            (near((rows, ff), half), "v"),
            (near((rows, ff), half), "v"),
            (near(flat, half), "v"),
            (near((8, width)), "v"),
        ],
        [pltpu.VMEM(flat, half), pltpu.SemaphoreType.DMA((rows // (2 * TILE),))],
        20,
    )


def inner_grad_kernel(after_ref, ddown_ref, wd_ref, slope_ref, dinner_ref, bias_ref):
    part = 768

    @pl.loop(0, wd_ref.shape[0] // part)
    def _(j):
        cols = at(j, part)
        d = dot(ddown_ref[...], wd_ref[cols, :], NT) * slope_ref[:, cols].astype(single)
        low = d.astype(half)
        dinner_ref[:, cols] = low
        bias_ref[pl.ds(j, 1), :] = column_sum(low.astype(single))


def inner_grad(after, ddown, wd, slope):
    ff, width = wd.shape
    return call(
        inner_grad_kernel,
        "inner_grad",
        [(after, "a"), (ddown, "v"), (wd, "v"), (slope, "v")],
        [(near(slope.shape, half), "v"), (near((ff // width, width)), "v")],
        aliases={3: 0},
    )


def first_norm_kernel(
    after_ref, dinner_ref, wi_ref, ddown_ref, normed1_ref, root1_ref, wo_ref, g1_ref, x_ref,
    dr1_ref, dattn_ref, dctx_ref, xt_ref, sums_ref,
):
    rows, width = dr1_ref.shape
    g1 = as_row(g1_ref)
    sums_ref[...] = jnp.zeros_like(sums_ref)

    @pl.loop(0, rows // TILE)
    def _(step):
        tile = at(step, TILE)
        normed1 = normed1_ref[tile, :].astype(single)
        dh1 = ddown_ref[tile, :].astype(single) + dot(dinner_ref[tile, :], wi_ref[...], NT)
        dr1 = norm_back(dh1, normed1, root1_ref[tile, 0:1], g1)
        dr1_ref[tile, :] = dr1
        dattn = dr1.astype(half)
        dattn_ref[tile, :] = dattn
        dctx_ref[tile, :] = dot(dattn, wo_ref[...], NT).astype(half)
        xt_ref[:, tile] = x_ref[tile, :].T
        sums_ref[0:1] += column_sum(dh1 * normed1)
        sums_ref[1:2] += column_sum(dh1)
        sums_ref[2:3] += column_sum(dattn.astype(single))


def first_norm(after, dinner, wi, ddown, normed1, root1, wo, g1, x):
    rows, width = ddown.shape
    flat = (rows, width)
    return call(
        first_norm_kernel,
        "first_norm_back",
        [(after, "a")] + [(a, "v") for a in (dinner, wi, ddown, normed1, root1, wo, g1, x)],
        [(near(flat), "v"), (near(flat, half), "v"), (near(flat, half), "v")]
        + [(near((width, rows), half), "v"), (near((8, width)), "v")],
    )


def attention_back_kernel(
    n_ref, after_ref, q_ref, k_ref, v_ref, ctx_ref, dctx_ref, lse_ref, dq_ref, dk_ref, dv_ref, sums_ref,
    *, length, quad,
):
    scale = HD**-0.5
    quads = q_ref.shape[1] // 256
    cols = slice(quad * 256, quad * 256 + 256)
    sums_ref[...] = jnp.zeros_like(sums_ref)

    @pl.loop(0, q_ref.shape[0] // length)
    def _(seq):
        tokens = at(seq, length)
        dead = lax.broadcasted_iota(jnp.int32, (length, 128), 0) >= n_ref[seq]
        low_half = lax.broadcasted_iota(jnp.int32, (length, 128), 1) < HD
        q, k, v, dctx = [r[tokens, cols] for r in (q_ref, k_ref, v_ref, dctx_ref)]
        kt = k.T
        prod_t = (ctx_ref[tokens, cols].astype(single) * dctx.astype(single)).T
        dqt = []
        for pair in range(2):
            side = slice(pair * 128, pair * 128 + 128)
            q_pair, k_pair, v_pair, d_pair = q[:, side], k[:, side], v[:, side], dctx[:, side]
            first = []
            for parity in range(2):
                q_one, k_one = pair_operands(q_pair, k_pair, parity, dead, scale)
                inside = low_half if parity == 0 else ~low_half
                v_one = jnp.where(inside, v_pair.astype(single), 0.0).astype(half)
                first.append((dot(k_one, q_one, NT), dot(v_one, d_pair, NT)))
            dks, dvs = [], []
            for parity, (s, dp) in enumerate(first):
                h = pair * 2 + parity
                p = jnp.exp(s - lse_ref[seq * quads + quad, h : h + 1, :])
                delta = jnp.sum(prod_t[h * HD : (h + 1) * HD], axis=0, keepdims=True)
                ds = (p * (dp - delta)).astype(half)
                dvs.append(dot(p.astype(half), d_pair))
                dks.append(dot(ds, q_pair))
                dqt.append((dot(kt[h * HD : (h + 1) * HD], ds) * scale).astype(half))
            dk_ref[tokens, side] = (jnp.where(low_half, dks[0], dks[1]) * scale).astype(half)
            dv = jnp.where(low_half, dvs[0], dvs[1]).astype(half)
            dv_ref[tokens, side] = dv
            sums_ref[1:2, side] += column_sum(dv.astype(single))
        dq = jnp.concatenate(dqt, axis=0).T
        dq_ref[tokens, :] = dq
        sums_ref[0:1, :] += column_sum(dq.astype(single))


def attention_back(lengths, after, q, k, v, ctx, dctx, lse, length, quad):
    rows = q.shape[0]
    return call(
        functools.partial(attention_back_kernel, length=length, quad=quad),
        f"attention_back_{quad}",
        [(lengths, "s"), (after, "a")] + [(a, "v") for a in (q, k, v, ctx, dctx, lse)],
        [(near((rows, 256), half), "v")] * 3 + [(near((8, 256)), "v")],
    )


def outer_half(me, act_ref, ddown_ref, y):
    part = act_ref.shape[1] // 4
    return dot(act_ref[:, at(2 * y + me, part)], ddown_ref[...], TN)


TABLE = 32


def table_rows(pos_ref, task_ref, sums2, out, classes, tables):
    width = out.shape[1]
    out[...] = jnp.zeros_like(out)
    out[0:3, :] = sums2[0:3]
    lane = lax.broadcasted_iota(jnp.int32, (1, width), 1)
    out[3:4, :] = jnp.where(lane == pos_ref[6], sums2[7:8], 0.0)
    for t in range(tables):
        mine = jnp.where(task_ref[0] == t, 1.0, 0.0)
        out[4 + t * classes : 4 + (t + 1) * classes, :] = sums2[3 : 3 + classes] * mine


def outer_send_kernel(pos_ref, task_ref, after_ref, act_ref, ddown_ref, sums2, send_ref, table_ref, *, classes, tables):
    part = act_ref.shape[1] // 4
    for y in range(2):
        send_ref[y * part : (y + 1) * part, :] = outer_half(1 - pos_ref[1], act_ref, ddown_ref, y)
    table_rows(pos_ref, task_ref, sums2, table_ref, classes, tables)
    send_ref[2 * part :, :] = table_ref[...]


def outer_rest_kernel(pos_ref, after_ref, act_ref, ddown_ref, rest_ref):
    for y in range(2):
        rest_ref[y] = outer_half(pos_ref[1], act_ref, ddown_ref, y)


def outer_send(pos, task_ids, after, act, ddown, sums2, classes, tables):
    width = ddown.shape[1]
    assert 4 + classes * tables <= TABLE
    return call(
        functools.partial(outer_send_kernel, classes=classes, tables=tables),
        "outer_weight_send",
        [(pos, "s"), (task_ids, "s"), (after, "a"), (act, "v"), (ddown, "v"), (sums2, "v")],
        [(near((act.shape[1] // 2 + TABLE, width)), "v"), (near((TABLE, width)), "v")],
    )


def outer_rest(pos, after, act, ddown):
    return call(
        outer_rest_kernel,
        "outer_weight_rest",
        [(pos, "s"), (after, "a"), (act, "v"), (ddown, "v")],
        [(near((2, act.shape[1] // 4, ddown.shape[1])), "v")],
    )[0]


def split_x(pos, block, rows, cols, lead, sx, kx, to):
    me = pos[2]
    for z in range(4):
        zero = block[(2 * z) * rows : (2 * z + 1) * rows, cols]
        one = block[(2 * z + 1) * rows : (2 * z + 2) * rows, cols]
        sx[lead + (z, slice(None), to)] = jnp.where(me == 0, one, zero)
        kx[lead + (z, slice(None), to)] = jnp.where(me == 0, zero, one)


def split_z(pos, block, rows, cols, lead, sz, kz, to):
    side = pos[3]
    for x in range(2):
        zs = [block[(2 * z + x) * rows : (2 * z + x + 1) * rows, cols] for z in range(4)]
        for hi, (even, odd) in enumerate(((0, 1), (3, 2))):
            sz[lead + (hi, x, slice(None), to)] = jnp.where(side == 0, zs[odd], zs[even])
            kz[lead + (hi, x, slice(None), to)] = jnp.where(side == 0, zs[even], zs[odd])


def split_y(pos, data, rows, sy, ky, to):
    me = pos[0]
    zero = data[: 8 * rows].reshape(4, 2, rows, data.shape[1])
    one = data[8 * rows :].reshape(4, 2, rows, data.shape[1])
    sy[:, :, :, to] = jnp.where(me == 0, one, zero)
    ky[:, :, :, to] = jnp.where(me == 0, zero, one)


def outer_keep_kernel(
    pos_ref, after_ref, own_ref, got_ref, table_ref, sx_ref, kx_ref, sy_ref, ky_ref, sz_ref, kz_ref, block_ref
):
    third, part = own_ref.shape[2] // 3, own_ref.shape[1]
    rows = own_ref.shape[1] // 8
    me_y, me_x, side = pos_ref[0], pos_ref[2], pos_ref[3]
    xs, ys, zs = [slice(i * third, (i + 1) * third) for i in range(3)]

    def at_rows(y, z, x, cols):
        begin = (2 * z + x) * rows
        there = y * part + begin
        return own_ref[y, begin : begin + rows, cols] + got_ref[there : there + rows, cols]

    table = table_ref[...] + got_ref[2 * part :, :]
    block_ref[...] = jnp.concatenate([table[:, i * third : (i + 1) * third] for i in range(3)], axis=0)
    sx_ref[8] = block_ref[...]

    for y in range(2):
        for z in range(4):
            zero, one = at_rows(y, z, 0, xs), at_rows(y, z, 1, xs)
            sx_ref[4 * y + z] = jnp.where(me_x == 0, one, zero)
            kx_ref[4 * y + z] = jnp.where(me_x == 0, zero, one)
        for x in range(2):
            for hi, (even, odd) in enumerate(((0, 1), (3, 2))):
                zero, one = at_rows(y, even, x, zs), at_rows(y, odd, x, zs)
                sz_ref[y, hi, x] = jnp.where(side == 0, one, zero)
                kz_ref[y, hi, x] = jnp.where(side == 0, zero, one)
    for z in range(4):
        for x in range(2):
            zero, one = at_rows(0, z, x, ys), at_rows(1, z, x, ys)
            sy_ref[z, x] = jnp.where(me_y == 0, one, zero)
            ky_ref[z, x] = jnp.where(me_y == 0, zero, one)


def outer_keep(pos, after, own, got, table):
    width = own.shape[2]
    r, third = own.shape[1] // 8, width // 3
    assert 3 * TABLE == r and third == 256
    shapes = [(9, r, third), (8, r, third)] + [(4, 2, r, third)] * 2 + [(2, 2, 2, r, third)] * 2 + [(r, third)]
    return call(
        outer_keep_kernel,
        "outer_weight_keep",
        [(pos, "s"), (after, "a"), (own, "v"), (got, "v"), (table, "v")],
        [(near(s), "v") for s in shapes],
    )


def row_half(left_ref, me):
    quarter = left_ref.shape[0] // 4
    return jnp.concatenate([left_ref[at(me, quarter), :], left_ref[at(2 + me, quarter), :]], axis=0)


def inner_send_kernel(pos_ref, after_ref, left_ref, right_ref, send_ref, *, other):
    me = 1 - pos_ref[1] if other else pos_ref[1]
    left = row_half(left_ref, me)
    parts, _, columns = send_ref.shape
    for j in range(parts):
        send_ref[j] = dot(left, right_ref[:, j * columns : (j + 1) * columns])


def inner_send(pos, after, left_t, right, other):
    width = left_t.shape[0]
    return call(
        functools.partial(inner_send_kernel, other=other),
        "inner_weight_send",
        [(pos, "s"), (after, "a"), (left_t, "v"), (right, "v")],
        [(near((2, width // 2, right.shape[1] // 2)), "v")],
    )[0]


def inner_keep_kernel(pos_ref, after_ref, left_ref, right_ref, got_ref, sx_ref, kx_ref, sy_ref, ky_ref):
    left = row_half(left_ref, pos_ref[1])
    count, columns = got_ref.shape[1:]
    rows = count // 16

    def block(j):
        return dot(left, right_ref[:, j * columns : (j + 1) * columns]) + got_ref[j]

    data = block(0)
    for y in range(2):
        sub = slice(y * 8 * rows, (y + 1) * 8 * rows)
        split_x(pos_ref, data[sub], rows, slice(None), (y,), sx_ref, kx_ref, slice(None))
    split_y(pos_ref, block(1), rows, sy_ref, ky_ref, slice(None))


def inner_keep(pos, after, left_t, right, got):
    r = left_t.shape[0] // 32
    wide = right.shape[1] // 2
    shapes = [(2, 4, r, wide)] * 2 + [(4, 2, r, wide)] * 2
    return call(
        inner_keep_kernel,
        "inner_weight_keep",
        [(pos, "s"), (after, "a")] + [(a, "v") for a in (left_t, right, got)],
        [(near(s), "v") for s in shapes],
    )


SMALL = 8


def small_rows(sums0, sums1, inner_bias, out, base):
    width = sums1.shape[1]
    count = inner_bias.shape[0]
    lanes = slice(0, width)
    out[base : base + SMALL, :] = jnp.zeros((SMALL, out.shape[1]), single)
    for g, sums in enumerate(sums0):
        out[base : base + 2, g * 256 : (g + 1) * 256] = sums[0:2]
    out[base + 2 : base + 5, lanes] = sums1[0:3]
    out[base + 5 : base + 4 + count, lanes] = inner_bias[: count - 1, :]
    for i in range(3):
        out[base + i : base + i + 1, width:] = inner_bias[count - 1 : count, i * 256 : (i + 1) * 256]


def quad_grads(me, left_ref, ctxt_ref, dattn_ref, parts, g):
    left = row_half(left_ref, me)
    pieces = [dot(left, part[...]) for part in parts[3 * g : 3 * g + 3]]
    pieces.append(dot(row_half(ctxt_ref, me), dattn_ref[:, g * 256 : (g + 1) * 256]))
    return pieces


def qkv_send_kernel(pos_ref, after_ref, left_ref, ctxt_ref, dattn_ref, *refs, other, quads):
    parts, refs = refs[: 3 * quads], refs[3 * quads :]
    sums0, refs = refs[:quads], refs[quads:]
    sums1, inner_bias, send_ref = refs
    me = 1 - pos_ref[1] if other else pos_ref[1]
    count = left_ref.shape[0] // 2
    for g in range(quads):
        for t, piece in enumerate(quad_grads(me, left_ref, ctxt_ref, dattn_ref, parts, g)):
            send_ref[g * count : (g + 1) * count, t * 256 : (t + 1) * 256] = piece
    small_rows(sums0, sums1, inner_bias, send_ref, quads * count)


def qkv_send(pos, after, xt, ctxt, dattn, parts, sums0, sums1, inner_bias, other):
    width = xt.shape[0]
    assert inner_bias.shape[0] == 4 and width == 768
    return call(
        functools.partial(qkv_send_kernel, other=other, quads=len(sums0)),
        "qkv_weight_send",
        [(pos, "s"), (after, "a"), (xt, "v"), (ctxt, "v"), (dattn, "v")]
        + [(p, "v") for p in (*parts, *sums0, sums1, inner_bias)],
        [(near((len(sums0) * (width // 2) + SMALL, 1024)), "v")],
    )[0]


def rows24_from(base, index, r):
    return pl.ds(pl.multiple_of(base + index * r, 8), r)


def rows24(index, r):
    return pl.ds(pl.multiple_of(index * r, 8), r)


def pack(out, row, block):
    r, w = block.shape[0] // 4, block.shape[1]
    for j in range(4):
        out[row : row + r, j * w : (j + 1) * w] = block[j * r : (j + 1) * r]


def third_outer_kernel(pos_ref, after_ref, xk, xr, yk, yr, zk, zr, block, sent, kept, zs, zn, table_out):
    me_x, side = pos_ref[2], pos_ref[3]
    rows, wide = xk.shape[1:]
    for hi, (keep, send) in enumerate(((side, 1 - side), (3 - side, 2 + side))):
        to = slice(hi * rows, (hi + 1) * rows)
        sent[to, :wide] = xk[send] + xr[send]
        sent[to, wide:] = yk[send] + yr[send]
        kept[to, :wide] = xk[keep] + xr[keep]
        kept[to, wide:] = yk[keep] + yr[keep]
    table = block[...] + xr[4]
    table = jnp.concatenate([table[: rows // 2], table[rows // 2 :]], axis=1)
    table_out[...] = table
    sent[2 * rows :, :] = table
    r = rows // 4
    for y in range(2):
        pack(zs, y * r, zk[y, 1 - me_x] + zr[y, 1 - me_x])
        pack(zn, y * r, zk[y, me_x] + zr[y, me_x])


def third_outer(pos, after, *arrays):
    r, wide = arrays[0].shape[1:]
    shapes = [(2 * r + r // 2, 2 * wide), (2 * r, 2 * wide)] + [(r // 2, 4 * wide)] * 2 + [(r // 2, 2 * wide)]
    return call(
        third_outer_kernel,
        "third_outer_stage",
        [(pos, "s"), (after, "a")] + [(a, "v") for a in arrays],
        [(near(s), "v") for s in shapes],
    )


def fourth_outer_kernel(pos_ref, after_ref, k, got, table, sent, kept, table_out):
    me_hi = pos_ref[4]
    rows = k.shape[0] // 2
    there, here = rows24(1 - me_hi, rows), rows24(me_hi, rows)
    sent[:rows, :] = k[there, :] + got[there, :]
    kept[...] = k[here, :] + got[here, :]
    total = table[...] + got[2 * rows :, :]
    table_out[...] = total
    sent[rows:, :] = total


def fourth_outer_stage(pos, after, k, got, table):
    rows, wide = k.shape[0] // 2, k.shape[1]
    shapes = [(rows + rows // 2, wide), (rows, wide), (rows // 2, wide)]
    return call(
        fourth_outer_kernel,
        "fourth_stage_outer",
        [(pos, "s"), (after, "a"), (k, "v"), (got, "v"), (table, "v")],
        [(near(s), "v") for s in shapes],
    )


def qkv_keep_kernel(pos_ref, after_ref, left_ref, ctxt_ref, dattn_ref, own_ref, got_ref, ozs, *refs):
    *parts, sx, kx, sy, ky, sz, kz, small = refs
    count, width = left_ref.shape[0] // 2, left_ref.shape[0]
    r = width // 32
    me_y, me_c, me_x, side = pos_ref[0], pos_ref[1], pos_ref[2], pos_ref[3]
    total = own_ref[3 * count :, :] + got_ref[3 * count :, :]
    small[...] = total
    sy[8 * r :, :] = total
    sx[8 * r :, :] = ozs[...]

    def grads(g):
        for t, piece in enumerate(quad_grads(me_c, left_ref, ctxt_ref, dattn_ref, parts, g)):
            cols = slice(t * 256, (t + 1) * 256)
            yield cols, piece + got_ref[g * count : (g + 1) * count, cols]

    for cols, g in grads(0):
        for y in range(2):
            for x in range(2):
                zs = [g[(y * 8 + z * 2 + x) * r : (y * 8 + z * 2 + x + 1) * r] for z in range(4)]
                for hi, (even, odd) in enumerate(((0, 1), (3, 2))):
                    begin = ((y * 2 + hi) * 2 + x) * r
                    sz[begin : begin + r, cols] = jnp.where(side == 0, zs[odd], zs[even])
                    kz[begin : begin + r, cols] = jnp.where(side == 0, zs[even], zs[odd])
    for cols, g in grads(1):
        for y in range(2):
            for z in range(4):
                begin = (y * 8 + z * 2) * r
                zero, one = g[begin : begin + r], g[begin + r : begin + 2 * r]
                to = slice((y * 4 + z) * r, (y * 4 + z + 1) * r)
                sx[to, cols] = jnp.where(me_x == 0, one, zero)
                kx[to, cols] = jnp.where(me_x == 0, zero, one)
    for cols, g in grads(2):
        sy[: 8 * r, cols] = jnp.where(me_y == 0, g[8 * r :], g[: 8 * r])
        ky[:, cols] = jnp.where(me_y == 0, g[: 8 * r], g[8 * r :])


def qkv_keep(pos, after, xt, ctxt, dattn, own, got, ozs, parts):
    width = xt.shape[0]
    r = width // 32
    wide = own.shape[1]
    shapes = [(n, wide) for n in (10 * r, 8 * r, 8 * r + SMALL, 8 * r, 8 * r, 8 * r, SMALL)]
    return call(
        qkv_keep_kernel,
        "qkv_weight_keep",
        [(pos, "s"), (after, "a")]
        + [(a, "v") for a in (xt, ctxt, dattn, own, got, ozs, *parts)],
        [(near(n), "v") for n in shapes],
    )


def second_qkv_kernel(pos_ref, after_ref, kx, rx, ky, ry, kz, rz, small, oz, xs, xk, ys, yk, zs, zk, small_out, oz_out):
    me_y, me_x, me_hi = pos_ref[0], pos_ref[2], pos_ref[4]
    r = kx.shape[0] // 8
    total = small[...] + ry[8 * r :, :]
    small_out[...] = total
    ys[4 * r :, :] = total
    base = 8 * r
    xs[4 * r :, :] = oz[rows24(1 - me_y, r), :] + rx[rows24_from(base, 1 - me_y, r), :]
    oz_out[...] = oz[rows24(me_y, r), :] + rx[rows24_from(base, me_y, r), :]
    there, here = rows24(1 - me_y, 4 * r), rows24(me_y, 4 * r)
    xs[: 4 * r, :] = kx[there, :] + rx[there, :]
    xk[...] = kx[here, :] + rx[here, :]
    for z in range(4):
        there, here = rows24(2 * z + 1 - me_x, r), rows24(2 * z + me_x, r)
        to = slice(z * r, (z + 1) * r)
        ys[to, :] = ky[there, :] + ry[there, :]
        yk[to, :] = ky[here, :] + ry[here, :]
    for y in range(2):
        there, here = rows24(2 * y + 1 - me_hi, 2 * r), rows24(2 * y + me_hi, 2 * r)
        to = slice(y * 2 * r, (y + 1) * 2 * r)
        zs[to, :] = kz[there, :] + rz[there, :]
        zk[to, :] = kz[here, :] + rz[here, :]


def third_qkv_kernel(pos_ref, after_ref, xk, xr, yk, yr, zk, zr, small, sent, kept, zs, zn, small_out):
    me_x, side = pos_ref[2], pos_ref[3]
    r = xk.shape[0] // 4
    total = small[...] + yr[4 * r :, :]
    small_out[...] = total
    sent[4 * r :, :] = total
    for i, (k, got) in enumerate(((xk, xr), (yk, yr))):
        for hi, (keep, send) in enumerate(((side, 1 - side), (3 - side, 2 + side))):
            there, here = rows24(send, r), rows24(keep, r)
            to = slice((2 * i + hi) * r, (2 * i + hi + 1) * r)
            sent[to, :] = k[there, :] + got[there, :]
            kept[to, :] = k[here, :] + got[here, :]
    for y in range(2):
        there, here = rows24(2 * y + 1 - me_x, r), rows24(2 * y + me_x, r)
        to = slice(y * r, (y + 1) * r)
        zs[to, :] = zk[there, :] + zr[there, :]
        zn[to, :] = zk[here, :] + zr[here, :]


def fourth_qkv_kernel(pos_ref, after_ref, k, got, zk, zr, small, sent, kept, zs, zn, small_out):
    me_y, me_hi = pos_ref[0], pos_ref[4]
    r = k.shape[0] // 4
    total = small[...] + got[4 * r :, :]
    small_out[...] = total
    sent[2 * r :, :] = total
    for i in range(2):
        there, here = rows24(2 * i + 1 - me_hi, r), rows24(2 * i + me_hi, r)
        to = slice(i * r, (i + 1) * r)
        sent[to, :] = k[there, :] + got[there, :]
        kept[to, :] = k[here, :] + got[here, :]
    there, here = rows24(1 - me_y, r), rows24(me_y, r)
    zs[...] = zk[there, :] + zr[there, :]
    zn[...] = zk[here, :] + zr[here, :]


def qkv_stage(kernel, name, pos, after, arrays, counts):
    wide = arrays[0].shape[1]
    return call(
        kernel,
        name,
        [(pos, "s"), (after, "a")] + [(a, "v") for a in arrays],
        [(near((n, wide)), "v") for n in counts],
    )


def sum_outer_kernel(after_ref, k, got, table, out, table_out):
    rows, wide = k.shape
    out[...] = k[...] + got[:rows, :]
    total = table[...] + got[rows:, :]
    block = jnp.concatenate([total[:, : wide // 2], total[:, wide // 2 :]], axis=0)
    for i in range(3):
        table_out[:, i * 256 : (i + 1) * 256] = block[i * TABLE : (i + 1) * TABLE]


def sum_outer_stage(after, k, got, table):
    return call(
        sum_outer_kernel,
        "sum",
        [(after, "a"), (k, "v"), (got, "v"), (table, "v")],
        [(near(k.shape), "v"), (near((TABLE, 768)), "v")],
    )


def last_outer_kernel(after_ref, xy, zk, zr, out, done):
    done[...] = jnp.zeros_like(done)
    wide = xy.shape[1]
    out[:, :wide] = xy[...]
    r = zk.shape[0]
    z = zk[...] + zr[4 * r :, :]
    w = z.shape[1] // 4
    for j in range(4):
        out[j * r : (j + 1) * r, wide:] = z[:, j * w : (j + 1) * w]


def last_outer(after, xy, zk, zr):
    shape = (xy.shape[0], xy.shape[1] + zk.shape[1] // 4)
    return call(
        last_outer_kernel,
        "last_outer_stage",
        [(after, "a")] + [(a, "v") for a in (xy, zk, zr)],
        [(far(shape), "v"), (near((8, 128)), "v")],
    )


def last_qkv_kernel(pos_ref, k, got, zk, zr, small, table, q_out, k_out, v_out, o_out, *outs, classes, bias_rows):
    *vectors, inner_out, loss_out, head_out = outs
    r = zk.shape[0]
    width = table.shape[1]
    xs = k[:r, :] + got[:r, :]
    ys = k[r:, :] + got[r : 2 * r, :]
    zs = zk[...] + zr[...]
    for t, out in enumerate((q_out, k_out, v_out, o_out)):
        for g, data in enumerate((zs, xs, ys)):
            out[:, g * 256 : (g + 1) * 256] = data[:, t * 256 : (t + 1) * 256]
    small_sum = small[...] + got[2 * r :, :]
    total = small_sum[:, :width]
    tables = table[...]
    me = pos_ref[5]
    shift = lax.rem(width - me * r, width)
    rolled, rolled_table = pltpu.roll(total, shift, 1), pltpu.roll(tables[:8], shift, 1)
    for i, out in enumerate(vectors):
        out[...] = rolled[i : i + 1, :r] if i < 5 else rolled_table[i - 5 : i - 4, :r]
    part = inner_out.shape[1]
    per_row = width // part
    row = lax.broadcasted_iota(jnp.int32, total.shape, 0)
    tail = jnp.concatenate([small_sum[i : i + 1, width:] for i in range(3)], axis=1)
    mine = me // per_row
    one = jnp.sum(jnp.where(row == 5 + mine, total, 0.0), axis=0, keepdims=True)
    one = jnp.where(mine == bias_rows - 1, tail, one)
    one = jnp.broadcast_to(one, (8, width))
    inner_out[...] = pltpu.roll(one, lax.rem(width - (me % per_row) * part, width), 1)[0:1, :part]
    lane = lax.broadcasted_iota(jnp.int32, (1, width), 1)
    loss_out[...] = jnp.sum(jnp.where(lane == pos_ref[6], tables[3:4], 0.0), axis=1, keepdims=True)
    for t in range(head_out.shape[0]):
        head_out[t] = tables[4 + t * classes : 4 + (t + 1) * classes]


def last_qkv(pos, k, got, zk, zr, small, table, classes, tables, bias_rows):
    r, width = zk.shape[0], table.shape[1]
    shapes = [(r, width)] * 4 + [(1, r)] * 8 + [(1, r * bias_rows), (1, 1), (tables, classes, width)]
    return call(
        functools.partial(last_qkv_kernel, classes=classes, bias_rows=bias_rows),
        "last_qkv_stage",
        [(pos, "s")] + [(a, "v") for a in (k, got, zk, zr, small, table)],
        [(far(s), "v") for s in shapes],
    )


def token_grad_kernel(after_ref, dr1_ref, wq_ref, wk_ref, wv_ref, *refs):
    *parts, out_hbm, done_ref, out_ref, sems = refs
    done_ref[...] = jnp.zeros_like(done_ref)
    rows = out_ref.shape[0]
    quads = len(parts) // 3

    @pl.loop(0, rows // TILE)
    def _(step):
        tile = at(step, TILE)
        total = dr1_ref[tile, :]
        for t, w_ref in enumerate((wq_ref, wk_ref, wv_ref)):
            d = jnp.concatenate([parts[g * 3 + t][tile, :] for g in range(quads)], axis=1)
            total = total + dot(d, w_ref[...], NT)
        out_ref[tile, :] = total
        pltpu.make_async_copy(out_ref.at[tile, :], out_hbm.at[tile, :], sems.at[step]).start()

    for i in range(rows // TILE):
        tile = pl.ds(i * TILE, TILE)
        pltpu.make_async_copy(out_ref.at[tile, :], out_hbm.at[tile, :], sems.at[i]).wait()


def token_grads(after, dr1, wq, wk, wv, parts):
    rows, width = dr1.shape
    return call(
        token_grad_kernel,
        "token_grad",
        [(after, "a")] + [(a, "v") for a in (dr1, wq, wk, wv, *parts)],
        [(far((rows, width)), "a"), (near((8, 128)), "v")],
        [pltpu.VMEM((rows, width), single), pltpu.SemaphoreType.DMA((rows // TILE,))],
    )


def second_outer_kernel(pos_ref, after_ref, kx, rx, ky, ry, kz, rz, block, xs, xk, ys, yk, zs, zk, block_out):
    me_y, me_x, me_hi = pos_ref[0], pos_ref[2], pos_ref[4]
    table = block[...] + rx[8]
    block_out[...] = table
    xs[4] = table
    for z in range(4):
        there, here = 4 * (1 - me_y) + z, 4 * me_y + z
        xs[z] = kx[there] + rx[there]
        xk[z] = kx[here] + rx[here]
    ys[...] = ky[:, 1 - me_x] + ry[:, 1 - me_x]
    yk[...] = ky[:, me_x] + ry[:, me_x]
    zs[...] = kz[:, 1 - me_hi] + rz[:, 1 - me_hi]
    zk[...] = kz[:, me_hi] + rz[:, me_hi]


def second_outer_stage(pos, after, *arrays):
    r, third = arrays[0].shape[1:]
    shapes = [(5, r, third)] + [(4, r, third)] * 3 + [(2, 2, r, third)] * 2 + [(r, third)]
    return call(
        second_outer_kernel,
        "second_stage_outer",
        [(pos, "s"), (after, "a")] + [(a, "v") for a in arrays],
        [(near(s), "v") for s in shapes],
    )


def second_kernel(pos_ref, after_ref, kx, rx, ky, ry, xs, xk, ys, yk):
    me_y, me_x = pos_ref[0], pos_ref[2]
    xs[...] = kx[1 - me_y] + rx[1 - me_y]
    xk[...] = kx[me_y] + rx[me_y]
    ys[...] = ky[:, 1 - me_x] + ry[:, 1 - me_x]
    yk[...] = ky[:, me_x] + ry[:, me_x]


def second(pos, after, kx, rx, ky, ry):
    return call(
        second_kernel,
        "second_stage_inner",
        [(pos, "s"), (after, "a")] + [(a, "v") for a in (kx, rx, ky, ry)],
        [(near((4,) + kx.shape[2:]), "v")] * 4,
    )


def third_kernel(pos_ref, after_ref, xk, xr, yk, yr, *refs):
    me_x, side = pos_ref[2], pos_ref[3]
    wide = xk.shape[2]
    if len(refs) == 2:
        sent, kept = refs
    else:
        zk, zr, sent, kept, zs, zn = refs
        zs[...] = zk[:, 1 - me_x] + zr[:, 1 - me_x]
        zn[...] = zk[:, me_x] + zr[:, me_x]
    for hi, (keep, send) in enumerate(((side, 1 - side), (3 - side, 2 + side))):
        sent[hi, :, :wide] = xk[send] + xr[send]
        sent[hi, :, wide:] = yk[send] + yr[send]
        kept[hi, :, :wide] = xk[keep] + xr[keep]
        kept[hi, :, wide:] = yk[keep] + yr[keep]


def third(pos, after, xk, xr, yk, yr, zk=None, zr=None):
    r, wide = xk.shape[1:]
    inputs = [xk, xr, yk, yr]
    shapes = [(2, r, 2 * wide)] * 2
    if zk is not None:
        inputs += [zk, zr]
        shapes += [(2,) + zk.shape[2:]] * 2
    return call(
        third_kernel,
        "third_stage",
        [(pos, "s"), (after, "a")] + [(a, "v") for a in inputs],
        [(near(s), "v") for s in shapes],
    )


def fourth_kernel(pos_ref, after_ref, xyk, xyr, *refs):
    me_y, me_hi = pos_ref[0], pos_ref[4]
    if len(refs) == 2:
        sent, kept = refs
    else:
        zk, zr, sent, kept, zs, zn = refs
        zs[...] = zk[1 - me_y] + zr[1 - me_y]
        zn[...] = zk[me_y] + zr[me_y]
    sent[...] = xyk[1 - me_hi] + xyr[1 - me_hi]
    kept[...] = xyk[me_hi] + xyr[me_hi]


def fourth(pos, after, xyk, xyr):
    return call(
        fourth_kernel,
        "fourth_stage_inner",
        [(pos, "s"), (after, "a"), (xyk, "v"), (xyr, "v")],
        [(near(xyk.shape[1:]), "v")] * 2,
    )


def last_kernel(after_ref, xyk, xyr, *refs, layout):
    count = len(layout)
    outs = refs[-count - 1 : -1]
    refs[-1][...] = jnp.zeros_like(refs[-1])
    sources = [(xyk, xyr), refs[:2]]
    for out, pieces in zip(outs, layout):
        to = 0
        for source, begin, end in pieces:
            a, b = sources[source]
            out[:, to : to + end - begin] = a[:, begin:end] + b[:, begin:end]
            to += end - begin


def last(after, xyk, xyr, zk, zr, layout):
    inputs = [xyk, xyr] + ([] if zk is None else [zk, zr])
    shapes = [(xyk.shape[0], sum(e - b for _, b, e in pieces)) for pieces in layout]
    return call(
        functools.partial(last_kernel, layout=layout),
        "last_stage",
        [(after, "a")] + [(a, "v") for a in inputs],
        [(far(s), "v") for s in shapes] + [(near((8, 128)), "v")],
    )


def pair_list(change):
    pairs = []
    for y in range(2):
        for c in range(2):
            for z in range(4):
                for x in range(2):
                    py, pc, pz, px = change(y, c, z, x)
                    pairs.append((((y * 2 + c) * 4 + z) * 2 + x, ((py * 2 + pc) * 4 + pz) * 2 + px))
    return pairs


PAIRS = {
    "y": pair_list(lambda y, c, z, x: (1 - y, c, z, x)),
    "c": pair_list(lambda y, c, z, x: (y, 1 - c, z, x)),
    "x": pair_list(lambda y, c, z, x: (y, c, z, 1 - x)),
    "near": pair_list(lambda y, c, z, x: (y, c, z ^ 1, x)),
    "far": pair_list(lambda y, c, z, x: (y, c, 3 - z, x)),
}


def swap(array, name):
    return lax.ppermute(array, ALL_AXES, PAIRS[name])


def per_device(
    tokens,
    out_cot,
    lengths,
    labels,
    task_ids,
    task_weights,
    query_weight,
    key_weight,
    value_weight,
    query_bias,
    value_bias,
    output_weight,
    output_bias,
    norm1_gain,
    norm1_bias,
    inner_weight,
    inner_bias,
    outer_weight,
    outer_bias,
    norm2_gain,
    norm2_bias,
    head_table,
    *,
    staged,
):
    seqs, length, width = tokens.shape
    rows = seqs * length
    ff = inner_weight.shape[1]
    group_seqs = seqs * lax.axis_size("batch")
    task_index = lax.axis_index("task")
    batch_index = lax.axis_index("batch")
    my_y, my_c, my_z, my_x = task_index // 2, task_index % 2, batch_index // 2, batch_index % 2
    my_hi = my_z // 2
    my_side = (my_z // 2) ^ (my_z % 2)
    where = task_index * lax.axis_size("batch") + batch_index
    pos = jnp.stack([my_y, my_c, my_x, my_side, my_hi, where, task_index]).astype(jnp.int32)
    vectors = (output_bias, norm1_gain, norm1_bias, inner_bias, outer_bias, norm2_gain, norm2_bias)

    x, q, k, v, ctx, ctxt, lse, wo, wi, wd, cot = attention(
        tokens,
        lengths,
        query_weight,
        key_weight,
        value_weight,
        query_bias,
        value_bias,
        output_weight,
        inner_weight,
        outer_weight,
        out_cot,
    )
    block_out, normed1, root1, h1t, act, slope, ddown, sums2 = middle(
        x, ctx, cot, length, labels, task_ids, task_weights, wo, wi, wd, vectors, head_table.transpose(1, 0, 2), group_seqs
    )
    block_out = block_out.reshape(tokens.shape)

    classes, tables = head_table.shape[1], head_table.shape[0]
    f2, r, quads = ff // 2, width // 32, width // 256
    parts, sums0 = [None] * (3 * quads), [None] * quads

    def back(quad, after):
        *grads, sums = attention_back(lengths, after, q, k, v, ctx, e["dctx"], lse, length, quad)
        parts[3 * quad : 3 * quad + 3] = grads
        sums0[quad] = sums
        return sums

    def small_args():
        return (ctxt, e["dattn"], parts, sums0, e["sums1"], e["inner_bias"])

    e = {}

    def send_outer(after):
        e["o_send"], e["table"] = outer_send(pos, task_ids, after, act, ddown, sums2, classes, tables)
        return e["table"]

    def rest_outer(after):
        e["o_rest"] = outer_rest(pos, after, act, ddown)
        return e["o_rest"]

    def do_inner_grad(after):
        e["dinner"], e["inner_bias"] = inner_grad(after, ddown, wd, slope)
        return e["inner_bias"]

    def send_inner(after):
        e["i_send"] = inner_send(pos, after, h1t, e["dinner"], True)
        return e["i_send"]

    def do_first_norm(after):
        e["dr1"], e["dattn"], e["dctx"], e["xt"], e["sums1"] = first_norm(
            after,
            e["dinner"],
            inner_weight,
            ddown,
            normed1,
            root1,
            output_weight,
            norm1_gain,
            tokens.reshape(rows, width),
        )
        return e["sums1"]

    def do_tokens(after):
        e["token_grad"], after = token_grads(after, e["dr1"], query_weight, key_weight, value_weight, parts)
        return after

    def send_qkv(after):
        e["qkv_s"] = qkv_send(pos, after, e["xt"], *small_args(), True)
        return e["qkv_s"]

    def keep_outer(after):
        got = swap(e["o_send"], "c")
        osx, okx, osy, oky, osz, okz, block = outer_keep(pos, after, e["o_rest"], got, e["table"])
        e["o1"] = (okx, swap(osx, "x"), oky, swap(osy, "y"), okz, swap(osz, "near"), block)
        return block

    def keep_inner(after):
        isx, ikx, isy, iky = inner_keep(pos, after, h1t, e["dinner"], swap(e["i_send"], "c"))
        e["i1"] = (ikx, swap(isx, "x"), iky, swap(isy, "y"))
        return ikx

    def second_outer(after):
        xs, xk, ys, yk, zs, zk, block = second_outer_stage(pos, after, *e["o1"])
        e["o2"] = (xk, swap(xs, "y"), yk, swap(ys, "x"), zk, swap(zs, "far"), block)
        return block

    def second_inner(after):
        xs, xk, ys, yk = second(pos, after, *e["i1"])
        e["i2"] = (xk, swap(xs, "y"), yk, swap(ys, "x"))
        return xk

    def do_third_outer(after):
        sent, kept, e["ozs"], e["oz"], table = third_outer(pos, after, *e["o2"])
        e["o3"] = (kept, swap(sent, "near"), table)
        return table

    def third_inner(after):
        sent, kept = third(pos, after, *e["i2"])
        e["i3"] = (kept, swap(sent, "near"))
        return kept

    def fourth_outer(after):
        sent, kept, table = fourth_outer_stage(pos, after, *e["o3"])
        e["o4"] = (kept, swap(sent, "far"), table)
        return table

    def fourth_inner(after):
        sent, kept = fourth(pos, after, *e["i3"])
        e["i4"] = (kept, swap(sent, "far"))
        return kept

    def sum_outer(after):
        e["outer_xy"], e["table_sum"] = sum_outer_stage(after, *e["o4"])
        return e["table_sum"]

    def last_inner(after):
        e["inner_s"], after = last(after, *e["i4"], None, None, (((0, 0, 2 * f2),),))
        return after

    def do_last_outer(after):
        e["outer_s"], after = last_outer(after, e["outer_xy"], e["oz2"], e["q2"][1])
        return after

    def keep_qkv(after):
        sx, kx, sy, ky, sz, kz, small = qkv_keep(
            pos, after, e["xt"], ctxt, e["dattn"], e["qkv_s"], swap(e["qkv_s"], "c"), e["ozs"], parts
        )
        e["q1"] = (kx, swap(sx, "x"), ky, swap(sy, "y"), kz, swap(sz, "near"), small, e["oz"])
        return small

    def stage(kernel, name, after, arrays, counts):
        return qkv_stage(kernel, name, pos, after, arrays, counts)

    def second_qkv(after):
        xs, xk, ys, yk, zs, zk, small, e["oz2"] = stage(
            second_qkv_kernel,
            "second_qkv_stage",
            after,
            e["q1"],
            [5 * r, 4 * r, 4 * r + SMALL, 4 * r, 4 * r, 4 * r, SMALL, r],
        )
        e["q2"] = (xk, swap(xs, "y"), yk, swap(ys, "x"), zk, swap(zs, "far"), small)
        return small

    def third_qkv(after):
        sent, kept, zs, zk, small = stage(
            third_qkv_kernel, "third_qkv_stage", after, e["q2"], [4 * r + SMALL, 4 * r, 2 * r, 2 * r, SMALL]
        )
        e["q3"] = (kept, swap(sent, "near"), zk, swap(zs, "x"), small)
        return small

    def fourth_qkv(after):
        sent, kept, zs, zk, small = stage(
            fourth_qkv_kernel, "fourth_qkv_stage", after, e["q3"], [2 * r + SMALL, 2 * r, r, r, SMALL]
        )
        e["q4"] = (kept, swap(sent, "far"), zk, swap(zs, "y"), small)
        return small

    def do_last_qkv(after):
        e["last"] = last_qkv(pos, *e["q4"], e["table_sum"], classes, tables, ff // width)
        return after

    steps = {
        "send_outer": send_outer,
        "rest_outer": rest_outer,
        "inner_grad": do_inner_grad,
        "send_inner": send_inner,
        "keep_outer": keep_outer,
        "first_norm": do_first_norm,
        "keep_inner": keep_inner,
        "second_outer": second_outer,
        "send_qkv": send_qkv,
        "second_inner": second_inner,
        "third_outer": do_third_outer,
        "keep_qkv": keep_qkv,
        "third_inner": third_inner,
        "tokens": do_tokens,
        "fourth_outer": fourth_outer,
        "second_qkv": second_qkv,
        "sum_outer": sum_outer,
        "third_qkv": third_qkv,
        "fourth_inner": fourth_inner,
        "fourth_qkv": fourth_qkv,
        "last_inner": last_inner,
        "last_outer": do_last_outer,
        "last_qkv": do_last_qkv,
    }
    for quad in range(quads):
        steps[f"back_{quad}"] = functools.partial(back, quad)
    if staged:
        after = sums2
        for name in ORDER:
            after = steps[name](after)
        query_s, key_s, value_s, output_s, *rest = e["last"]
        inner_s, outer_s = e["inner_s"], e["outer_s"]
        vector_s = [v.reshape(-1) for v in rest[:-1]]
        head_grad = rest[-1]
    else:
        after = do_first_norm(send_inner(do_inner_grad(send_outer(sums2))))
        after = rest_outer(after)
        i_keep = inner_send(pos, after, h1t, e["dinner"], False)
        for quad in range(quads):
            after = back(quad, after)
        after = do_tokens(send_qkv(after))
        qkv_k = qkv_send(pos, after, e["xt"], *small_args(), False)
        o_send, i_send, qkv_s = e["o_send"], e["i_send"], e["qkv_s"]

        def whole_rows(sent, kept):
            both = jnp.stack([jnp.where(my_c == 0, kept, sent), jnp.where(my_c == 0, sent, kept)], axis=1)
            return both.reshape(-1, both.shape[-1])

        def scatter(grad):
            return lax.psum_scatter(grad, ALL_AXES, scatter_dimension=0, tiled=True)

        def by_rows(array):
            return array.reshape(2, -1, array.shape[-1])

        part = ff // 4
        outer_s = scatter(whole_rows(o_send[: 2 * part].reshape(2, part, width), e["o_rest"]))
        inner_s = scatter(
            jnp.concatenate([whole_rows(by_rows(i_send[j]), by_rows(i_keep[j])) for j in range(2)], axis=-1)
        )
        count = width // 2

        def tensor(array, t):
            cols = slice(t * 256, (t + 1) * 256)
            return by_rows(jnp.concatenate([array[g * count : (g + 1) * count, cols] for g in range(quads)], axis=1))

        query_s, key_s, value_s, output_s = [
            scatter(whole_rows(tensor(qkv_s, t), tensor(qkv_k, t))) for t in range(4)
        ]
        small = lax.psum(jnp.concatenate([qkv_s[quads * count :, :width], e["inner_bias"], e["table"]]), ALL_AXES)
        devices = lax.axis_size("task") * lax.axis_size("batch")

        def mine(array):
            flat = array.reshape(-1)
            size = flat.shape[0] // devices
            return lax.dynamic_slice(flat, (where * size,), (size,))

        table = small[SMALL + ff // width :]
        vector_s = [mine(a) for a in (*small[:5], *table[:3], small[SMALL : SMALL + ff // width])]
        vector_s.append(lax.dynamic_slice(table, (3, task_index), (1, 1)).reshape(1))
        head_grad = table[4 : 4 + classes * tables].reshape(head_table.shape)
    token_grad = e["token_grad"].reshape(tokens.shape)
    bias_q, bias_v, gain1, bias1, bias_o, gain2, bias2, bias_d, bias_i, loss = vector_s
    return (
        block_out,
        token_grad,
        loss,
        query_s,
        key_s,
        value_s,
        bias_q,
        bias_v,
        output_s,
        bias_o,
        gain1,
        bias1,
        inner_s,
        bias_i,
        outer_s,
        bias_d,
        gain2,
        bias2,
        head_grad,
    )


def solution(mesh):
    rows = P(ALL_AXES)
    plain = P()
    task = P("task")
    staged = mesh.shape["task"] == 4 and mesh.shape["batch"] == 8
    return jax.shard_map(
        functools.partial(per_device, staged=staged),
        mesh=mesh,
        in_specs=(rows, rows, rows, rows, task, task) + (plain,) * 16,
        out_specs=(rows, rows, task) + (rows,) * 15 + (plain,),
        check_vma=False,
    )
```

```python
import functools

import jax
import jax.numpy as jnp
from jax import lax
from jax.experimental import pallas as pl
from jax.experimental.pallas import tpu as pltpu
from jax.sharding import PartitionSpec as P

HD = 64
TILE = 256
ALL_AXES = ("task", "batch")
NN = (((1,), (0,)), ((), ()))
NT = (((1,), (1,)), ((), ()))
TN = (((0,), (0,)), ((), ()))
half = jnp.bfloat16
single = jnp.float32
eps_norm = 1e-12


def dot(left, right, dims=NN):
    return lax.dot_general(left, right, dims, preferred_element_type=single)


ANY = pl.BlockSpec(memory_space=pl.ANY)
SMEM = pl.BlockSpec(memory_space=pltpu.SMEM)
VMEM = pl.BlockSpec(memory_space=pltpu.VMEM)
HBM = pl.BlockSpec(memory_space=pltpu.HBM)


def near(shape, dtype=single):
    return pltpu.VMEM(shape, dtype)


def off(shape, dtype=single):
    return pltpu.HBM(shape, dtype)


def far(shape, dtype=single):
    return jax.ShapeDtypeStruct(shape, dtype)


COSTS = {
    "attention_back_0": 1,
    "attention_back_1": 1000,
    "attention_back_2": 1,
    "first_norm_back": 300,
    "fourth_qkv_stage": 100,
    "fourth_stage_inner": 1,
    "fourth_stage_outer": 1000,
    "inner_grad": 3000,
    "inner_weight_keep": 1000,
    "inner_weight_send": 10000,
    "last_outer_stage": 3000,
    "last_stage": 300,
    "outer_weight_keep": 3000,
    "outer_weight_rest": 1,
    "outer_weight_send": 3000,
    "qkv_weight_keep": 100,
    "qkv_weight_send": 3000,
    "second_qkv_stage": 100,
    "second_stage_inner": 1,
    "second_stage_outer": 3000,
    "sum": 10000,
    "third_outer_stage": 65000,
    "third_qkv_stage": 3000,
    "third_stage": 10000,
    "token_grad": 3000,
}
ORDER = [
    "send_outer",
    "inner_grad",
    "send_inner",
    "rest_outer",
    "keep_outer",
    "keep_inner",
    "first_norm",
    "back_0",
    "second_outer",
    "back_1",
    "back_2",
    "send_qkv",
    "second_inner",
    "third_outer",
    "keep_qkv",
    "third_inner",
    "tokens",
    "fourth_outer",
    "second_qkv",
    "sum_outer",
    "third_qkv",
    "fourth_inner",
    "last_outer",
    "fourth_qkv",
    "last_inner",
    "last_qkv",
]


def call(kernel, name, inputs, outputs, scratch=(), megabytes=7, aliases=None):
    specs = {"v": VMEM, "s": SMEM, "a": ANY, "h": HBM}
    spaces = {"v": pltpu.VMEM, "h": pltpu.HBM}
    arrays = [
        pltpu.with_memory_space_constraint(x, spaces[p]) if p in spaces and (x.ndim > 1 or p == "h") else x for x, p in inputs
    ]
    return pl.pallas_call(
        kernel,
        in_specs=[specs[p] for _, p in inputs],
        out_specs=[specs[p] for _, p in outputs],
        out_shape=[o for o, _ in outputs],
        scratch_shapes=list(scratch),
        input_output_aliases=aliases or {},
        compiler_params=pltpu.CompilerParams(vmem_limit_bytes=megabytes << 20),
        cost_estimate=pl.CostEstimate(flops=COSTS.get(name, 1) * 10**6, bytes_accessed=1024, transcendentals=0),
        name=name,
    )(*arrays)


def at(index, size):
    return pl.ds(pl.multiple_of(index * size, size), size)


def as_row(ref):
    return ref[...].astype(single).reshape(1, -1)


def pair_operands(q, k, parity, dead, scale):
    rows = q.shape[0]
    lane = lax.broadcasted_iota(jnp.int32, (rows, 128), 1)
    inside = (lane // HD) == parity
    spare = lane == HD * (1 - parity)
    q_one = jnp.where(inside, q.astype(single) * scale, jnp.where(spare, 1.0, 0.0)).astype(half)
    k_one = jnp.where(inside, k.astype(single), jnp.where(spare & dead, -1e30, 0.0)).astype(half)
    return q_one, k_one


def attention_kernel(
    n_ref, x_hbm, wq_hbm, wk_hbm, wv_hbm, bq_hbm, bv_hbm, wo_hbm, wi_hbm, wd_hbm, cot_hbm,
    x_ref, q_hbm, k_hbm, v_hbm, ctx_ref, ctxt_hbm, lse_ref, wo_ref, wi_ref, wd_ref, cot_ref,
    ctxt_ref, q_ref, k_ref, v_ref, wq_ref, wk_ref, wv_ref, bq_vmem, bv_vmem, sems, out_sems, ctxt_sems,
    *, length,
):
    rows, width = x_ref.shape
    sides = [pl.ds(i * (rows // 2), rows // 2) for i in range(2)]
    pairs = (
        (x_hbm.at[sides[0], :], x_ref.at[sides[0], :]), (bq_hbm, bq_vmem), (wq_hbm, wq_ref),
        (x_hbm.at[sides[1], :], x_ref.at[sides[1], :]), (bv_hbm, bv_vmem), (wk_hbm, wk_ref), (wv_hbm, wv_ref),
        (wo_hbm, wo_ref), (wi_hbm, wi_ref), (wd_hbm, wd_ref), (cot_hbm, cot_ref),
    )
    copies = [pltpu.make_async_copy(src, dst, sems.at[i]) for i, (src, dst) in enumerate(pairs)]
    for copy in copies[:7]:
        copy.start()
    zero = jnp.zeros((1, width), single)
    leaving = []
    for i, (waits, w_ref, bias, out, out_hbm) in enumerate((
        ((0, 1, 2), wq_ref, bq_vmem, q_ref, q_hbm),
        ((4, 5), wk_ref, None, k_ref, k_hbm),
        ((6,), wv_ref, bv_vmem, v_ref, v_hbm),
    )):
        for wait in waits:
            copies[wait].wait()
        shift = zero if bias is None else as_row(bias)
        for part, side in enumerate(sides):
            if i == 0 and part == 1:
                copies[3].wait()
            out[side, :] = (dot(x_ref[side, :], w_ref[...]) + shift).astype(half)
        if i == 0:
            for copy in copies[7:]:
                copy.start()
        leaving.append(pltpu.make_async_copy(out, out_hbm, out_sems.at[i]))
        leaving[-1].start()

    quads = width // 256

    @pl.loop(0, (rows // length) * quads)
    def _(step):
        seq, quad = step // quads, step % quads
        tokens, cols = at(seq, length), at(quad, 256)
        dead = lax.broadcasted_iota(jnp.int32, (length, 128), 0) >= n_ref[seq]
        q, k, v = q_ref[tokens, cols], k_ref[tokens, cols], v_ref[tokens, cols]
        vt = v.T
        scores = []
        for h in range(4):
            pair = slice(h // 2 * 128, h // 2 * 128 + 128)
            q_one, k_one = pair_operands(q[:, pair], k[:, pair], h % 2, dead, HD**-0.5)
            scores.append(dot(k_one, q_one, NT))
        weights = []
        for s in scores:
            top = jnp.max(s, axis=0, keepdims=True)
            e = jnp.exp(s - top)
            weights.append((e.astype(half), top, jnp.sum(e, axis=0, keepdims=True)))
        parts = []
        for h, (e, top, total) in enumerate(weights):
            parts.append((dot(vt[h * HD : (h + 1) * HD], e) * (1.0 / total)).astype(half))
            lse_ref[step, h : h + 1, :] = top + jnp.log(total)
        ctxt = jnp.concatenate(parts, axis=0)
        ctxt_ref[cols, tokens] = ctxt
        ctx_ref[tokens, cols] = ctxt.T
        pltpu.make_async_copy(ctxt_ref.at[cols, tokens], ctxt_hbm.at[cols, tokens], ctxt_sems.at[step]).start()

    for step in range((rows // length) * quads):
        seq, quad = step // quads, step % quads
        tokens, cols = pl.ds(seq * length, length), pl.ds(quad * 256, 256)
        pltpu.make_async_copy(ctxt_ref.at[cols, tokens], ctxt_hbm.at[cols, tokens], ctxt_sems.at[step]).wait()
    for copy in copies[7:] + leaving:
        copy.wait()


def attention(tokens, lengths, wq, wk, wv, bq, bv, wo, wi, wd, cot):
    seqs, length, width = tokens.shape
    rows = seqs * length
    flat = (rows, width)
    quads = width // 256
    return call(
        functools.partial(attention_kernel, length=length),
        "attention_forward",
        [(lengths, "s"), (tokens.reshape(flat), "h"), (wq, "h"), (wk, "h"), (wv, "h"), (bq, "h"), (bv, "h")]
        + [(wo, "h"), (wi, "h"), (wd, "h"), (cot.reshape(flat), "h")],
        [(near(flat, half), "v")]
        + [(off(flat, half), "h")] * 3
        + [(near(flat, half), "v"), (off((width, rows), half), "h"), (near((seqs * quads, 8, length)), "v")]
        + [(near(w.shape, half), "v") for w in (wo, wi, wd)]
        + [(near(flat, half), "v")],
        [pltpu.VMEM((width, rows), half)]
        + [pltpu.VMEM(flat, half)] * 3
        + [pltpu.VMEM(w.shape, half) for w in (wq, wk, wv, bq, bv)]
        + [pltpu.SemaphoreType.DMA((11,)), pltpu.SemaphoreType.DMA((3,))]
        + [pltpu.SemaphoreType.DMA((seqs * quads,))],
        20,
    )


def norm_parts(resid):
    center = resid - jnp.mean(resid, axis=-1, keepdims=True)
    inv_root = lax.rsqrt(jnp.mean(center * center, axis=-1, keepdims=True) + eps_norm)
    return center * inv_root, inv_root


def norm_back(grad_out, normed, inv_root, gain):
    scaled = grad_out * gain
    return inv_root * (
        scaled
        - jnp.mean(scaled, axis=-1, keepdims=True)
        - normed * jnp.mean(scaled * normed, axis=-1, keepdims=True)
    )


def gelu_parts(u):
    u = u.astype(half)
    w = u * u
    v = jnp.minimum(w, jnp.asarray(36.0, half))
    p = (v * jnp.asarray(-0.00031594874, half) + jnp.asarray(0.0367987, half)) * v + jnp.asarray(0.79771759, half)
    h = jnp.asarray(0.5, half)
    cdf = h + h * jnp.tanh(u * p)
    bell = jnp.exp2(w * jnp.asarray(-0.72134752, half) - jnp.asarray(1.32574806, half))
    return u * cdf, cdf + u * bell


def column_sum(array):
    return jnp.sum(array, axis=0, keepdims=True)


def middle_kernel(
    task_ref, label_ref, weight_ref, x_ref, ctx_ref, cot_ref, wo_ref, wi_ref, wd_ref,
    bo_ref, g1_ref, b1_ref, bi_ref, bd_ref, g2_ref, b2_ref, head_ref,
    out_hbm, normed1_ref, root1_ref, h1t_ref, act_ref, slope_ref, ddown_ref, sums_ref,
    out_ref, sems,
    *, length, group_seqs,
):
    rows, width = x_ref.shape
    ff = wi_ref.shape[1]
    part = 768
    bo, g1, b1, bd, g2, b2 = [as_row(r) for r in (bo_ref, g1_ref, b1_ref, bd_ref, g2_ref, b2_ref)]
    bi = as_row(bi_ref)
    w = weight_ref[0]
    table = head_ref[...].astype(single)
    chosen = lax.broadcasted_iota(jnp.int32, table.shape, 1) == task_ref[0]
    head = jnp.sum(jnp.where(chosen, table, 0.0), axis=1)
    classes = head.shape[0]
    sums_ref[...] = jnp.zeros_like(sums_ref)

    @pl.loop(0, rows // (2 * TILE))
    def _(step):
        tile = at(step, (2 * TILE))
        x = x_ref[tile, :].astype(single)
        normed1, root1 = norm_parts(x + dot(ctx_ref[tile, :], wo_ref[...]) + bo)
        normed1_ref[tile, :] = normed1.astype(half)
        root1_ref[tile, :] = jnp.broadcast_to(root1, ((2 * TILE), 128))
        hidden1 = normed1 * g1 + b1
        h1 = hidden1.astype(half)
        h1t_ref[:, tile] = h1.T

        def inner_part(j):
            return dot(h1, wi_ref[:, j : j + part]) + bi[:, j : j + part]

        down = None
        following = inner_part(0)
        for j in range(0, ff, part):
            inner = following
            if j + part < ff:
                following = inner_part(j + part)
            value, slope = gelu_parts(inner)
            act = value.astype(half)
            act_ref[tile, j : j + part] = act
            slope_ref[tile, j : j + part] = slope.astype(half)
            term = dot(act, wd_ref[j : j + part, :])
            down = term if down is None else down + term
        normed2, root2 = norm_parts(hidden1 + down + bd)
        final = normed2 * g2 + b2
        low = final.astype(half)
        out_ref[tile, :] = low
        pltpu.make_async_copy(out_ref.at[tile, :], out_hbm.at[tile, :], sems.at[step]).start()
        cls = low[0:1].astype(single)
        logits = [jnp.sum(cls * head[c : c + 1], axis=1, keepdims=True) for c in range(classes)]
        top = functools.reduce(jnp.maximum, logits)
        lse = top + jnp.log(sum(jnp.exp(v - top) for v in logits))
        per_seq = length // (2 * TILE)
        label = label_ref[step // per_seq]
        first = jnp.where(step % per_seq == 0, 1.0, 0.0)
        picked = sum(jnp.where(label == c, v, 0.0) for c, v in enumerate(logits))
        slopes = [
            (jnp.exp(v - lse) - jnp.where(label == c, 1.0, 0.0)) * (w / group_seqs * first)
            for c, v in enumerate(logits)
        ]
        d_cls = sum(s * head[c : c + 1] for c, s in enumerate(slopes))
        row = lax.broadcasted_iota(jnp.int32, final.shape, 0)
        d_final = cot_ref[tile, :].astype(single) * w + jnp.where(row == 0, d_cls, 0.0)
        dr2 = norm_back(d_final, normed2, root2, g2)
        ddown = dr2.astype(half)
        ddown_ref[tile, :] = ddown
        sums_ref[0:1] += column_sum(d_final * normed2)
        sums_ref[1:2] += column_sum(d_final)
        sums_ref[2:3] += column_sum(ddown.astype(single))
        for c in range(classes):
            sums_ref[3 + c : 4 + c] += slopes[c] * cls
        sums_ref[7:8] += jnp.broadcast_to((lse - picked) * (w / group_seqs * first), cls.shape)

    for i in range(rows // (2 * TILE)):
        tile = pl.ds(i * (2 * TILE), (2 * TILE))
        pltpu.make_async_copy(out_ref.at[tile, :], out_hbm.at[tile, :], sems.at[i]).wait()


def middle(x, ctx, cot, length, labels, task_ids, task_weights, wo, wi, wd, vectors, head_table, group_seqs):
    rows, width = x.shape
    ff = wi.shape[1]
    assert head_table.shape[0] <= 4
    flat = (rows, width)
    return call(
        functools.partial(middle_kernel, length=length, group_seqs=group_seqs),
        "middle_forward",
        [(task_ids, "s"), (labels, "s"), (task_weights, "s")]
        + [(a, "v") for a in (x, ctx, cot, wo, wi, wd, *vectors, head_table)],
        [(far(flat, half), "a")]
        + [
            (near(flat, half), "v"),
            (near((rows, 128)), "v"),
            (near((width, rows), half), "v"),
            (near((rows, ff), half), "v"),
            (near((rows, ff), half), "v"),
            (near(flat, half), "v"),
            (near((8, width)), "v"),
        ],
        [pltpu.VMEM(flat, half), pltpu.SemaphoreType.DMA((rows // (2 * TILE),))],
        20,
    )


def inner_grad_kernel(after_ref, ddown_ref, wd_ref, slope_ref, dinner_ref, bias_ref):
    part = 768

    @pl.loop(0, wd_ref.shape[0] // part)
    def _(j):
        cols = at(j, part)
        d = dot(ddown_ref[...], wd_ref[cols, :], NT) * slope_ref[:, cols].astype(single)
        low = d.astype(half)
        dinner_ref[:, cols] = low
        bias_ref[pl.ds(j, 1), :] = column_sum(low.astype(single))


def inner_grad(after, ddown, wd, slope):
    ff, width = wd.shape
    return call(
        inner_grad_kernel,
        "inner_grad",
        [(after, "a"), (ddown, "v"), (wd, "v"), (slope, "v")],
        [(near(slope.shape, half), "v"), (near((ff // width, width)), "v")],
        aliases={3: 0},
    )


def first_norm_kernel(
    after_ref, dinner_ref, wi_ref, ddown_ref, normed1_ref, root1_ref, wo_ref, g1_ref, x_ref,
    dr1_ref, dattn_ref, dctx_ref, xt_ref, sums_ref,
):
    rows, width = dr1_ref.shape
    g1 = as_row(g1_ref)
    sums_ref[...] = jnp.zeros_like(sums_ref)

    @pl.loop(0, rows // TILE)
    def _(step):
        tile = at(step, TILE)
        normed1 = normed1_ref[tile, :].astype(single)
        dh1 = ddown_ref[tile, :].astype(single) + dot(dinner_ref[tile, :], wi_ref[...], NT)
        dr1 = norm_back(dh1, normed1, root1_ref[tile, 0:1], g1)
        dr1_ref[tile, :] = dr1
        dattn = dr1.astype(half)
        dattn_ref[tile, :] = dattn
        dctx_ref[tile, :] = dot(dattn, wo_ref[...], NT).astype(half)
        xt_ref[:, tile] = x_ref[tile, :].T
        sums_ref[0:1] += column_sum(dh1 * normed1)
        sums_ref[1:2] += column_sum(dh1)
        sums_ref[2:3] += column_sum(dattn.astype(single))


def first_norm(after, dinner, wi, ddown, normed1, root1, wo, g1, x):
    rows, width = ddown.shape
    flat = (rows, width)
    return call(
        first_norm_kernel,
        "first_norm_back",
        [(after, "a")] + [(a, "v") for a in (dinner, wi, ddown, normed1, root1, wo, g1, x)],
        [(near(flat), "v"), (near(flat, half), "v"), (near(flat, half), "v")]
        + [(near((width, rows), half), "v"), (near((8, width)), "v")],
    )


def attention_back_kernel(
    n_ref, after_ref, q_ref, k_ref, v_ref, ctx_ref, dctx_ref, lse_ref, dq_ref, dk_ref, dv_ref, sums_ref,
    *, length, quad,
):
    scale = HD**-0.5
    quads = q_ref.shape[1] // 256
    cols = slice(quad * 256, quad * 256 + 256)
    sums_ref[...] = jnp.zeros_like(sums_ref)

    @pl.loop(0, q_ref.shape[0] // length)
    def _(seq):
        tokens = at(seq, length)
        dead = lax.broadcasted_iota(jnp.int32, (length, 128), 0) >= n_ref[seq]
        low_half = lax.broadcasted_iota(jnp.int32, (length, 128), 1) < HD
        q, k, v, dctx = [r[tokens, cols] for r in (q_ref, k_ref, v_ref, dctx_ref)]
        kt = k.T
        prod_t = (ctx_ref[tokens, cols].astype(single) * dctx.astype(single)).T
        dqt = []
        for pair in range(2):
            side = slice(pair * 128, pair * 128 + 128)
            q_pair, k_pair, v_pair, d_pair = q[:, side], k[:, side], v[:, side], dctx[:, side]
            first = []
            for parity in range(2):
                q_one, k_one = pair_operands(q_pair, k_pair, parity, dead, scale)
                inside = low_half if parity == 0 else ~low_half
                v_one = jnp.where(inside, v_pair.astype(single), 0.0).astype(half)
                first.append((dot(k_one, q_one, NT), dot(v_one, d_pair, NT)))
            dks, dvs = [], []
            for parity, (s, dp) in enumerate(first):
                h = pair * 2 + parity
                p = jnp.exp(s - lse_ref[seq * quads + quad, h : h + 1, :])
                delta = jnp.sum(prod_t[h * HD : (h + 1) * HD], axis=0, keepdims=True)
                ds = (p * (dp - delta)).astype(half)
                dvs.append(dot(p.astype(half), d_pair))
                dks.append(dot(ds, q_pair))
                dqt.append((dot(kt[h * HD : (h + 1) * HD], ds) * scale).astype(half))
            dk_ref[tokens, side] = (jnp.where(low_half, dks[0], dks[1]) * scale).astype(half)
            dv = jnp.where(low_half, dvs[0], dvs[1]).astype(half)
            dv_ref[tokens, side] = dv
            sums_ref[1:2, side] += column_sum(dv.astype(single))
        dq = jnp.concatenate(dqt, axis=0).T
        dq_ref[tokens, :] = dq
        sums_ref[0:1, :] += column_sum(dq.astype(single))


def attention_back(lengths, after, q, k, v, ctx, dctx, lse, length, quad):
    rows = q.shape[0]
    return call(
        functools.partial(attention_back_kernel, length=length, quad=quad),
        f"attention_back_{quad}",
        [(lengths, "s"), (after, "a")] + [(a, "v") for a in (q, k, v, ctx, dctx, lse)],
        [(near((rows, 256), half), "v")] * 3 + [(near((8, 256)), "v")],
    )


def outer_half(me, act_ref, ddown_ref, y):
    part = act_ref.shape[1] // 4
    return dot(act_ref[:, at(2 * y + me, part)], ddown_ref[...], TN)


TABLE = 32


def table_rows(pos_ref, task_ref, sums2, out, classes, tables):
    width = out.shape[1]
    out[...] = jnp.zeros_like(out)
    out[0:3, :] = sums2[0:3]
    lane = lax.broadcasted_iota(jnp.int32, (1, width), 1)
    out[3:4, :] = jnp.where(lane == pos_ref[6], sums2[7:8], 0.0)
    for t in range(tables):
        mine = jnp.where(task_ref[0] == t, 1.0, 0.0)
        out[4 + t * classes : 4 + (t + 1) * classes, :] = sums2[3 : 3 + classes] * mine


def outer_send_kernel(pos_ref, task_ref, after_ref, act_ref, ddown_ref, sums2, send_ref, table_ref, *, classes, tables):
    part = act_ref.shape[1] // 4
    for y in range(2):
        send_ref[y * part : (y + 1) * part, :] = outer_half(1 - pos_ref[1], act_ref, ddown_ref, y)
    table_rows(pos_ref, task_ref, sums2, table_ref, classes, tables)
    send_ref[2 * part :, :] = table_ref[...]


def outer_rest_kernel(pos_ref, after_ref, act_ref, ddown_ref, rest_ref):
    for y in range(2):
        rest_ref[y] = outer_half(pos_ref[1], act_ref, ddown_ref, y)


def outer_send(pos, task_ids, after, act, ddown, sums2, classes, tables):
    width = ddown.shape[1]
    assert 4 + classes * tables <= TABLE
    return call(
        functools.partial(outer_send_kernel, classes=classes, tables=tables),
        "outer_weight_send",
        [(pos, "s"), (task_ids, "s"), (after, "a"), (act, "v"), (ddown, "v"), (sums2, "v")],
        [(near((act.shape[1] // 2 + TABLE, width)), "v"), (near((TABLE, width)), "v")],
    )


def outer_rest(pos, after, act, ddown):
    return call(
        outer_rest_kernel,
        "outer_weight_rest",
        [(pos, "s"), (after, "a"), (act, "v"), (ddown, "v")],
        [(near((2, act.shape[1] // 4, ddown.shape[1])), "v")],
    )[0]


def split_x(pos, block, rows, cols, lead, sx, kx, to):
    me = pos[2]
    for z in range(4):
        zero = block[(2 * z) * rows : (2 * z + 1) * rows, cols]
        one = block[(2 * z + 1) * rows : (2 * z + 2) * rows, cols]
        sx[lead + (z, slice(None), to)] = jnp.where(me == 0, one, zero)
        kx[lead + (z, slice(None), to)] = jnp.where(me == 0, zero, one)


def split_z(pos, block, rows, cols, lead, sz, kz, to):
    side = pos[3]
    for x in range(2):
        zs = [block[(2 * z + x) * rows : (2 * z + x + 1) * rows, cols] for z in range(4)]
        for hi, (even, odd) in enumerate(((0, 1), (3, 2))):
            sz[lead + (hi, x, slice(None), to)] = jnp.where(side == 0, zs[odd], zs[even])
            kz[lead + (hi, x, slice(None), to)] = jnp.where(side == 0, zs[even], zs[odd])


def split_y(pos, data, rows, sy, ky, to):
    me = pos[0]
    zero = data[: 8 * rows].reshape(4, 2, rows, data.shape[1])
    one = data[8 * rows :].reshape(4, 2, rows, data.shape[1])
    sy[:, :, :, to] = jnp.where(me == 0, one, zero)
    ky[:, :, :, to] = jnp.where(me == 0, zero, one)


def outer_keep_kernel(
    pos_ref, after_ref, own_ref, got_ref, table_ref, sx_ref, kx_ref, sy_ref, ky_ref, sz_ref, kz_ref, block_ref
):
    third, part = own_ref.shape[2] // 3, own_ref.shape[1]
    rows = own_ref.shape[1] // 8
    me_y, me_x, side = pos_ref[0], pos_ref[2], pos_ref[3]
    xs, ys, zs = [slice(i * third, (i + 1) * third) for i in range(3)]

    def at_rows(y, z, x, cols):
        begin = (2 * z + x) * rows
        there = y * part + begin
        return own_ref[y, begin : begin + rows, cols] + got_ref[there : there + rows, cols]

    table = table_ref[...] + got_ref[2 * part :, :]
    block_ref[...] = jnp.concatenate([table[:, i * third : (i + 1) * third] for i in range(3)], axis=0)
    sx_ref[8] = block_ref[...]

    for y in range(2):
        for z in range(4):
            zero, one = at_rows(y, z, 0, xs), at_rows(y, z, 1, xs)
            sx_ref[4 * y + z] = jnp.where(me_x == 0, one, zero)
            kx_ref[4 * y + z] = jnp.where(me_x == 0, zero, one)
        for x in range(2):
            for hi, (even, odd) in enumerate(((0, 1), (3, 2))):
                zero, one = at_rows(y, even, x, zs), at_rows(y, odd, x, zs)
                sz_ref[y, hi, x] = jnp.where(side == 0, one, zero)
                kz_ref[y, hi, x] = jnp.where(side == 0, zero, one)
    for z in range(4):
        for x in range(2):
            zero, one = at_rows(0, z, x, ys), at_rows(1, z, x, ys)
            sy_ref[z, x] = jnp.where(me_y == 0, one, zero)
            ky_ref[z, x] = jnp.where(me_y == 0, zero, one)


def outer_keep(pos, after, own, got, table):
    width = own.shape[2]
    r, third = own.shape[1] // 8, width // 3
    assert 3 * TABLE == r and third == 256
    shapes = [(9, r, third), (8, r, third)] + [(4, 2, r, third)] * 2 + [(2, 2, 2, r, third)] * 2 + [(r, third)]
    return call(
        outer_keep_kernel,
        "outer_weight_keep",
        [(pos, "s"), (after, "a"), (own, "v"), (got, "v"), (table, "v")],
        [(near(s), "v") for s in shapes],
    )


def row_half(left_ref, me):
    quarter = left_ref.shape[0] // 4
    return jnp.concatenate([left_ref[at(me, quarter), :], left_ref[at(2 + me, quarter), :]], axis=0)


def inner_send_kernel(pos_ref, after_ref, left_ref, right_ref, send_ref, *, other):
    me = 1 - pos_ref[1] if other else pos_ref[1]
    left = row_half(left_ref, me)
    parts, _, columns = send_ref.shape
    for j in range(parts):
        send_ref[j] = dot(left, right_ref[:, j * columns : (j + 1) * columns])


def inner_send(pos, after, left_t, right, other):
    width = left_t.shape[0]
    return call(
        functools.partial(inner_send_kernel, other=other),
        "inner_weight_send",
        [(pos, "s"), (after, "a"), (left_t, "v"), (right, "v")],
        [(near((2, width // 2, right.shape[1] // 2)), "v")],
    )[0]


def inner_keep_kernel(pos_ref, after_ref, left_ref, right_ref, got_ref, sx_ref, kx_ref, sy_ref, ky_ref):
    left = row_half(left_ref, pos_ref[1])
    count, columns = got_ref.shape[1:]
    rows = count // 16

    def block(j):
        return dot(left, right_ref[:, j * columns : (j + 1) * columns]) + got_ref[j]

    data = block(0)
    for y in range(2):
        sub = slice(y * 8 * rows, (y + 1) * 8 * rows)
        split_x(pos_ref, data[sub], rows, slice(None), (y,), sx_ref, kx_ref, slice(None))
    split_y(pos_ref, block(1), rows, sy_ref, ky_ref, slice(None))


def inner_keep(pos, after, left_t, right, got):
    r = left_t.shape[0] // 32
    wide = right.shape[1] // 2
    shapes = [(2, 4, r, wide)] * 2 + [(4, 2, r, wide)] * 2
    return call(
        inner_keep_kernel,
        "inner_weight_keep",
        [(pos, "s"), (after, "a")] + [(a, "v") for a in (left_t, right, got)],
        [(near(s), "v") for s in shapes],
    )


SMALL = 8


def small_rows(sums0, sums1, inner_bias, out, base):
    width = sums1.shape[1]
    count = inner_bias.shape[0]
    lanes = slice(0, width)
    out[base : base + SMALL, :] = jnp.zeros((SMALL, out.shape[1]), single)
    for g, sums in enumerate(sums0):
        out[base : base + 2, g * 256 : (g + 1) * 256] = sums[0:2]
    out[base + 2 : base + 5, lanes] = sums1[0:3]
    out[base + 5 : base + 4 + count, lanes] = inner_bias[: count - 1, :]
    for i in range(3):
        out[base + i : base + i + 1, width:] = inner_bias[count - 1 : count, i * 256 : (i + 1) * 256]


def quad_grads(me, left_ref, ctxt_ref, dattn_ref, parts, g):
    left = row_half(left_ref, me)
    pieces = [dot(left, part[...]) for part in parts[3 * g : 3 * g + 3]]
    pieces.append(dot(row_half(ctxt_ref, me), dattn_ref[:, g * 256 : (g + 1) * 256]))
    return pieces


def qkv_send_kernel(pos_ref, after_ref, left_ref, ctxt_ref, dattn_ref, *refs, other, quads):
    parts, refs = refs[: 3 * quads], refs[3 * quads :]
    sums0, refs = refs[:quads], refs[quads:]
    sums1, inner_bias, send_ref = refs
    me = 1 - pos_ref[1] if other else pos_ref[1]
    count = left_ref.shape[0] // 2
    for g in range(quads):
        for t, piece in enumerate(quad_grads(me, left_ref, ctxt_ref, dattn_ref, parts, g)):
            send_ref[g * count : (g + 1) * count, t * 256 : (t + 1) * 256] = piece
    small_rows(sums0, sums1, inner_bias, send_ref, quads * count)


def qkv_send(pos, after, xt, ctxt, dattn, parts, sums0, sums1, inner_bias, other):
    width = xt.shape[0]
    assert inner_bias.shape[0] == 4 and width == 768
    return call(
        functools.partial(qkv_send_kernel, other=other, quads=len(sums0)),
        "qkv_weight_send",
        [(pos, "s"), (after, "a"), (xt, "v"), (ctxt, "v"), (dattn, "v")]
        + [(p, "v") for p in (*parts, *sums0, sums1, inner_bias)],
        [(near((len(sums0) * (width // 2) + SMALL, 1024)), "v")],
    )[0]


def rows24_from(base, index, r):
    return pl.ds(pl.multiple_of(base + index * r, 8), r)


def rows24(index, r):
    return pl.ds(pl.multiple_of(index * r, 8), r)


def pack(out, row, block):
    r, w = block.shape[0] // 4, block.shape[1]
    for j in range(4):
        out[row : row + r, j * w : (j + 1) * w] = block[j * r : (j + 1) * r]


def third_outer_kernel(pos_ref, after_ref, xk, xr, yk, yr, zk, zr, block, sent, kept, zs, zn, table_out):
    me_x, side = pos_ref[2], pos_ref[3]
    rows, wide = xk.shape[1:]
    for hi, (keep, send) in enumerate(((side, 1 - side), (3 - side, 2 + side))):
        to = slice(hi * rows, (hi + 1) * rows)
        sent[to, :wide] = xk[send] + xr[send]
        sent[to, wide:] = yk[send] + yr[send]
        kept[to, :wide] = xk[keep] + xr[keep]
        kept[to, wide:] = yk[keep] + yr[keep]
    table = block[...] + xr[4]
    table = jnp.concatenate([table[: rows // 2], table[rows // 2 :]], axis=1)
    table_out[...] = table
    sent[2 * rows :, :] = table
    r = rows // 4
    for y in range(2):
        pack(zs, y * r, zk[y, 1 - me_x] + zr[y, 1 - me_x])
        pack(zn, y * r, zk[y, me_x] + zr[y, me_x])


def third_outer(pos, after, *arrays):
    r, wide = arrays[0].shape[1:]
    shapes = [(2 * r + r // 2, 2 * wide), (2 * r, 2 * wide)] + [(r // 2, 4 * wide)] * 2 + [(r // 2, 2 * wide)]
    return call(
        third_outer_kernel,
        "third_outer_stage",
        [(pos, "s"), (after, "a")] + [(a, "v") for a in arrays],
        [(near(s), "v") for s in shapes],
    )


def fourth_outer_kernel(pos_ref, after_ref, k, got, table, sent, kept, table_out):
    me_hi = pos_ref[4]
    rows = k.shape[0] // 2
    there, here = rows24(1 - me_hi, rows), rows24(me_hi, rows)
    sent[:rows, :] = k[there, :] + got[there, :]
    kept[...] = k[here, :] + got[here, :]
    total = table[...] + got[2 * rows :, :]
    table_out[...] = total
    sent[rows:, :] = total


def fourth_outer_stage(pos, after, k, got, table):
    rows, wide = k.shape[0] // 2, k.shape[1]
    shapes = [(rows + rows // 2, wide), (rows, wide), (rows // 2, wide)]
    return call(
        fourth_outer_kernel,
        "fourth_stage_outer",
        [(pos, "s"), (after, "a"), (k, "v"), (got, "v"), (table, "v")],
        [(near(s), "v") for s in shapes],
    )


def qkv_keep_kernel(pos_ref, after_ref, left_ref, ctxt_ref, dattn_ref, own_ref, got_ref, ozs, *refs):
    *parts, sx, kx, sy, ky, sz, kz, small = refs
    count, width = left_ref.shape[0] // 2, left_ref.shape[0]
    r = width // 32
    me_y, me_c, me_x, side = pos_ref[0], pos_ref[1], pos_ref[2], pos_ref[3]
    total = own_ref[3 * count :, :] + got_ref[3 * count :, :]
    small[...] = total
    sy[8 * r :, :] = total
    sx[8 * r :, :] = ozs[...]

    def grads(g):
        for t, piece in enumerate(quad_grads(me_c, left_ref, ctxt_ref, dattn_ref, parts, g)):
            cols = slice(t * 256, (t + 1) * 256)
            yield cols, piece + got_ref[g * count : (g + 1) * count, cols]

    for cols, g in grads(0):
        for y in range(2):
            for x in range(2):
                zs = [g[(y * 8 + z * 2 + x) * r : (y * 8 + z * 2 + x + 1) * r] for z in range(4)]
                for hi, (even, odd) in enumerate(((0, 1), (3, 2))):
                    begin = ((y * 2 + hi) * 2 + x) * r
                    sz[begin : begin + r, cols] = jnp.where(side == 0, zs[odd], zs[even])
                    kz[begin : begin + r, cols] = jnp.where(side == 0, zs[even], zs[odd])
    for cols, g in grads(1):
        for y in range(2):
            for z in range(4):
                begin = (y * 8 + z * 2) * r
                zero, one = g[begin : begin + r], g[begin + r : begin + 2 * r]
                to = slice((y * 4 + z) * r, (y * 4 + z + 1) * r)
                sx[to, cols] = jnp.where(me_x == 0, one, zero)
                kx[to, cols] = jnp.where(me_x == 0, zero, one)
    for cols, g in grads(2):
        sy[: 8 * r, cols] = jnp.where(me_y == 0, g[8 * r :], g[: 8 * r])
        ky[:, cols] = jnp.where(me_y == 0, g[: 8 * r], g[8 * r :])


def qkv_keep(pos, after, xt, ctxt, dattn, own, got, ozs, parts):
    width = xt.shape[0]
    r = width // 32
    wide = own.shape[1]
    shapes = [(n, wide) for n in (10 * r, 8 * r, 8 * r + SMALL, 8 * r, 8 * r, 8 * r, SMALL)]
    return call(
        qkv_keep_kernel,
        "qkv_weight_keep",
        [(pos, "s"), (after, "a")]
        + [(a, "v") for a in (xt, ctxt, dattn, own, got, ozs, *parts)],
        [(near(n), "v") for n in shapes],
    )


def second_qkv_kernel(pos_ref, after_ref, kx, rx, ky, ry, kz, rz, small, oz, xs, xk, ys, yk, zs, zk, small_out, oz_out):
    me_y, me_x, me_hi = pos_ref[0], pos_ref[2], pos_ref[4]
    r = kx.shape[0] // 8
    total = small[...] + ry[8 * r :, :]
    small_out[...] = total
    ys[4 * r :, :] = total
    base = 8 * r
    xs[4 * r :, :] = oz[rows24(1 - me_y, r), :] + rx[rows24_from(base, 1 - me_y, r), :]
    oz_out[...] = oz[rows24(me_y, r), :] + rx[rows24_from(base, me_y, r), :]
    there, here = rows24(1 - me_y, 4 * r), rows24(me_y, 4 * r)
    xs[: 4 * r, :] = kx[there, :] + rx[there, :]
    xk[...] = kx[here, :] + rx[here, :]
    for z in range(4):
        there, here = rows24(2 * z + 1 - me_x, r), rows24(2 * z + me_x, r)
        to = slice(z * r, (z + 1) * r)
        ys[to, :] = ky[there, :] + ry[there, :]
        yk[to, :] = ky[here, :] + ry[here, :]
    for y in range(2):
        there, here = rows24(2 * y + 1 - me_hi, 2 * r), rows24(2 * y + me_hi, 2 * r)
        to = slice(y * 2 * r, (y + 1) * 2 * r)
        zs[to, :] = kz[there, :] + rz[there, :]
        zk[to, :] = kz[here, :] + rz[here, :]


def third_qkv_kernel(pos_ref, after_ref, xk, xr, yk, yr, zk, zr, small, sent, kept, zs, zn, small_out):
    me_x, side = pos_ref[2], pos_ref[3]
    r = xk.shape[0] // 4
    total = small[...] + yr[4 * r :, :]
    small_out[...] = total
    sent[4 * r :, :] = total
    for i, (k, got) in enumerate(((xk, xr), (yk, yr))):
        for hi, (keep, send) in enumerate(((side, 1 - side), (3 - side, 2 + side))):
            there, here = rows24(send, r), rows24(keep, r)
            to = slice((2 * i + hi) * r, (2 * i + hi + 1) * r)
            sent[to, :] = k[there, :] + got[there, :]
            kept[to, :] = k[here, :] + got[here, :]
    for y in range(2):
        there, here = rows24(2 * y + 1 - me_x, r), rows24(2 * y + me_x, r)
        to = slice(y * r, (y + 1) * r)
        zs[to, :] = zk[there, :] + zr[there, :]
        zn[to, :] = zk[here, :] + zr[here, :]


def fourth_qkv_kernel(pos_ref, after_ref, k, got, zk, zr, small, sent, kept, zs, zn, small_out):
    me_y, me_hi = pos_ref[0], pos_ref[4]
    r = k.shape[0] // 4
    total = small[...] + got[4 * r :, :]
    small_out[...] = total
    sent[2 * r :, :] = total
    for i in range(2):
        there, here = rows24(2 * i + 1 - me_hi, r), rows24(2 * i + me_hi, r)
        to = slice(i * r, (i + 1) * r)
        sent[to, :] = k[there, :] + got[there, :]
        kept[to, :] = k[here, :] + got[here, :]
    there, here = rows24(1 - me_y, r), rows24(me_y, r)
    zs[...] = zk[there, :] + zr[there, :]
    zn[...] = zk[here, :] + zr[here, :]


def qkv_stage(kernel, name, pos, after, arrays, counts):
    wide = arrays[0].shape[1]
    return call(
        kernel,
        name,
        [(pos, "s"), (after, "a")] + [(a, "v") for a in arrays],
        [(near((n, wide)), "v") for n in counts],
    )


def sum_outer_kernel(after_ref, k, got, table, out, table_out):
    rows, wide = k.shape
    out[...] = k[...] + got[:rows, :]
    total = table[...] + got[rows:, :]
    block = jnp.concatenate([total[:, : wide // 2], total[:, wide // 2 :]], axis=0)
    for i in range(3):
        table_out[:, i * 256 : (i + 1) * 256] = block[i * TABLE : (i + 1) * TABLE]


def sum_outer_stage(after, k, got, table):
    return call(
        sum_outer_kernel,
        "sum",
        [(after, "a"), (k, "v"), (got, "v"), (table, "v")],
        [(near(k.shape), "v"), (near((TABLE, 768)), "v")],
    )


def last_outer_kernel(after_ref, xy, zk, zr, out, done):
    done[...] = jnp.zeros_like(done)
    wide = xy.shape[1]
    out[:, :wide] = xy[...]
    r = zk.shape[0]
    z = zk[...] + zr[4 * r :, :]
    w = z.shape[1] // 4
    for j in range(4):
        out[j * r : (j + 1) * r, wide:] = z[:, j * w : (j + 1) * w]


def last_outer(after, xy, zk, zr):
    shape = (xy.shape[0], xy.shape[1] + zk.shape[1] // 4)
    return call(
        last_outer_kernel,
        "last_outer_stage",
        [(after, "a")] + [(a, "v") for a in (xy, zk, zr)],
        [(far(shape), "v"), (near((8, 128)), "v")],
    )


def last_qkv_kernel(pos_ref, k, got, zk, zr, small, table, q_out, k_out, v_out, o_out, *outs, classes, bias_rows):
    *vectors, inner_out, loss_out, head_out = outs
    r = zk.shape[0]
    width = table.shape[1]
    xs = k[:r, :] + got[:r, :]
    ys = k[r:, :] + got[r : 2 * r, :]
    zs = zk[...] + zr[...]
    for t, out in enumerate((q_out, k_out, v_out, o_out)):
        for g, data in enumerate((zs, xs, ys)):
            out[:, g * 256 : (g + 1) * 256] = data[:, t * 256 : (t + 1) * 256]
    small_sum = small[...] + got[2 * r :, :]
    total = small_sum[:, :width]
    tables = table[...]
    me = pos_ref[5]
    shift = lax.rem(width - me * r, width)
    rolled, rolled_table = pltpu.roll(total, shift, 1), pltpu.roll(tables[:8], shift, 1)
    for i, out in enumerate(vectors):
        out[...] = rolled[i : i + 1, :r] if i < 5 else rolled_table[i - 5 : i - 4, :r]
    part = inner_out.shape[1]
    per_row = width // part
    row = lax.broadcasted_iota(jnp.int32, total.shape, 0)
    tail = jnp.concatenate([small_sum[i : i + 1, width:] for i in range(3)], axis=1)
    mine = me // per_row
    one = jnp.sum(jnp.where(row == 5 + mine, total, 0.0), axis=0, keepdims=True)
    one = jnp.where(mine == bias_rows - 1, tail, one)
    one = jnp.broadcast_to(one, (8, width))
    inner_out[...] = pltpu.roll(one, lax.rem(width - (me % per_row) * part, width), 1)[0:1, :part]
    lane = lax.broadcasted_iota(jnp.int32, (1, width), 1)
    loss_out[...] = jnp.sum(jnp.where(lane == pos_ref[6], tables[3:4], 0.0), axis=1, keepdims=True)
    for t in range(head_out.shape[1]):
        for c in range(classes):
            row_at = 4 + t * classes + c
            head_out[c, t : t + 1, :] = tables[row_at : row_at + 1]


def last_qkv(pos, k, got, zk, zr, small, table, classes, tables, bias_rows):
    r, width = zk.shape[0], table.shape[1]
    shapes = [(r, width)] * 4 + [(1, r)] * 8 + [(1, r * bias_rows), (1, 1), (classes, tables, width)]
    return call(
        functools.partial(last_qkv_kernel, classes=classes, bias_rows=bias_rows),
        "last_qkv_stage",
        [(pos, "s")] + [(a, "v") for a in (k, got, zk, zr, small, table)],
        [(far(s), "v") for s in shapes],
    )


def token_grad_kernel(after_ref, dr1_ref, wq_ref, wk_ref, wv_ref, *refs):
    *parts, out_hbm, done_ref, out_ref, sems = refs
    done_ref[...] = jnp.zeros_like(done_ref)
    rows = out_ref.shape[0]
    quads = len(parts) // 3

    @pl.loop(0, rows // TILE)
    def _(step):
        tile = at(step, TILE)
        total = dr1_ref[tile, :]
        for t, w_ref in enumerate((wq_ref, wk_ref, wv_ref)):
            d = jnp.concatenate([parts[g * 3 + t][tile, :] for g in range(quads)], axis=1)
            total = total + dot(d, w_ref[...], NT)
        out_ref[tile, :] = total
        pltpu.make_async_copy(out_ref.at[tile, :], out_hbm.at[tile, :], sems.at[step]).start()

    for i in range(rows // TILE):
        tile = pl.ds(i * TILE, TILE)
        pltpu.make_async_copy(out_ref.at[tile, :], out_hbm.at[tile, :], sems.at[i]).wait()


def token_grads(after, dr1, wq, wk, wv, parts):
    rows, width = dr1.shape
    return call(
        token_grad_kernel,
        "token_grad",
        [(after, "a")] + [(a, "v") for a in (dr1, wq, wk, wv, *parts)],
        [(far((rows, width)), "a"), (near((8, 128)), "v")],
        [pltpu.VMEM((rows, width), single), pltpu.SemaphoreType.DMA((rows // TILE,))],
    )


def second_outer_kernel(pos_ref, after_ref, kx, rx, ky, ry, kz, rz, block, xs, xk, ys, yk, zs, zk, block_out):
    me_y, me_x, me_hi = pos_ref[0], pos_ref[2], pos_ref[4]
    table = block[...] + rx[8]
    block_out[...] = table
    xs[4] = table
    for z in range(4):
        there, here = 4 * (1 - me_y) + z, 4 * me_y + z
        xs[z] = kx[there] + rx[there]
        xk[z] = kx[here] + rx[here]
    ys[...] = ky[:, 1 - me_x] + ry[:, 1 - me_x]
    yk[...] = ky[:, me_x] + ry[:, me_x]
    zs[...] = kz[:, 1 - me_hi] + rz[:, 1 - me_hi]
    zk[...] = kz[:, me_hi] + rz[:, me_hi]


def second_outer_stage(pos, after, *arrays):
    r, third = arrays[0].shape[1:]
    shapes = [(5, r, third)] + [(4, r, third)] * 3 + [(2, 2, r, third)] * 2 + [(r, third)]
    return call(
        second_outer_kernel,
        "second_stage_outer",
        [(pos, "s"), (after, "a")] + [(a, "v") for a in arrays],
        [(near(s), "v") for s in shapes],
    )


def second_kernel(pos_ref, after_ref, kx, rx, ky, ry, xs, xk, ys, yk):
    me_y, me_x = pos_ref[0], pos_ref[2]
    xs[...] = kx[1 - me_y] + rx[1 - me_y]
    xk[...] = kx[me_y] + rx[me_y]
    ys[...] = ky[:, 1 - me_x] + ry[:, 1 - me_x]
    yk[...] = ky[:, me_x] + ry[:, me_x]


def second(pos, after, kx, rx, ky, ry):
    return call(
        second_kernel,
        "second_stage_inner",
        [(pos, "s"), (after, "a")] + [(a, "v") for a in (kx, rx, ky, ry)],
        [(near((4,) + kx.shape[2:]), "v")] * 4,
    )


def third_kernel(pos_ref, after_ref, xk, xr, yk, yr, *refs):
    me_x, side = pos_ref[2], pos_ref[3]
    wide = xk.shape[2]
    if len(refs) == 2:
        sent, kept = refs
    else:
        zk, zr, sent, kept, zs, zn = refs
        zs[...] = zk[:, 1 - me_x] + zr[:, 1 - me_x]
        zn[...] = zk[:, me_x] + zr[:, me_x]
    for hi, (keep, send) in enumerate(((side, 1 - side), (3 - side, 2 + side))):
        sent[hi, :, :wide] = xk[send] + xr[send]
        sent[hi, :, wide:] = yk[send] + yr[send]
        kept[hi, :, :wide] = xk[keep] + xr[keep]
        kept[hi, :, wide:] = yk[keep] + yr[keep]


def third(pos, after, xk, xr, yk, yr, zk=None, zr=None):
    r, wide = xk.shape[1:]
    inputs = [xk, xr, yk, yr]
    shapes = [(2, r, 2 * wide)] * 2
    if zk is not None:
        inputs += [zk, zr]
        shapes += [(2,) + zk.shape[2:]] * 2
    return call(
        third_kernel,
        "third_stage",
        [(pos, "s"), (after, "a")] + [(a, "v") for a in inputs],
        [(near(s), "v") for s in shapes],
    )


def fourth_kernel(pos_ref, after_ref, xyk, xyr, *refs):
    me_y, me_hi = pos_ref[0], pos_ref[4]
    if len(refs) == 2:
        sent, kept = refs
    else:
        zk, zr, sent, kept, zs, zn = refs
        zs[...] = zk[1 - me_y] + zr[1 - me_y]
        zn[...] = zk[me_y] + zr[me_y]
    sent[...] = xyk[1 - me_hi] + xyr[1 - me_hi]
    kept[...] = xyk[me_hi] + xyr[me_hi]


def fourth(pos, after, xyk, xyr):
    return call(
        fourth_kernel,
        "fourth_stage_inner",
        [(pos, "s"), (after, "a"), (xyk, "v"), (xyr, "v")],
        [(near(xyk.shape[1:]), "v")] * 2,
    )


def last_kernel(after_ref, xyk, xyr, *refs, layout):
    count = len(layout)
    outs = refs[-count - 1 : -1]
    refs[-1][...] = jnp.zeros_like(refs[-1])
    sources = [(xyk, xyr), refs[:2]]
    for out, pieces in zip(outs, layout):
        to = 0
        for source, begin, end in pieces:
            a, b = sources[source]
            out[:, to : to + end - begin] = a[:, begin:end] + b[:, begin:end]
            to += end - begin


def last(after, xyk, xyr, zk, zr, layout):
    inputs = [xyk, xyr] + ([] if zk is None else [zk, zr])
    shapes = [(xyk.shape[0], sum(e - b for _, b, e in pieces)) for pieces in layout]
    return call(
        functools.partial(last_kernel, layout=layout),
        "last_stage",
        [(after, "a")] + [(a, "v") for a in inputs],
        [(far(s), "v") for s in shapes] + [(near((8, 128)), "v")],
    )


def pair_list(change):
    pairs = []
    for y in range(2):
        for c in range(2):
            for z in range(4):
                for x in range(2):
                    py, pc, pz, px = change(y, c, z, x)
                    pairs.append((((y * 2 + c) * 4 + z) * 2 + x, ((py * 2 + pc) * 4 + pz) * 2 + px))
    return pairs


PAIRS = {
    "y": pair_list(lambda y, c, z, x: (1 - y, c, z, x)),
    "c": pair_list(lambda y, c, z, x: (y, 1 - c, z, x)),
    "x": pair_list(lambda y, c, z, x: (y, c, z, 1 - x)),
    "near": pair_list(lambda y, c, z, x: (y, c, z ^ 1, x)),
    "far": pair_list(lambda y, c, z, x: (y, c, 3 - z, x)),
}


def swap(array, name):
    return lax.ppermute(array, ALL_AXES, PAIRS[name])


def per_device(
    tokens,
    out_cot,
    lengths,
    labels,
    task_ids,
    task_weights,
    query_weight,
    key_weight,
    value_weight,
    query_bias,
    value_bias,
    output_weight,
    output_bias,
    norm1_gain,
    norm1_bias,
    inner_weight,
    inner_bias,
    outer_weight,
    outer_bias,
    norm2_gain,
    norm2_bias,
    head_table,
    *,
    staged,
):
    seqs, length, width = tokens.shape
    rows = seqs * length
    ff = inner_weight.shape[1]
    group_seqs = seqs * lax.axis_size("batch")
    task_index = lax.axis_index("task")
    batch_index = lax.axis_index("batch")
    my_y, my_c, my_z, my_x = task_index // 2, task_index % 2, batch_index // 2, batch_index % 2
    my_hi = my_z // 2
    my_side = (my_z // 2) ^ (my_z % 2)
    where = task_index * lax.axis_size("batch") + batch_index
    pos = jnp.stack([my_y, my_c, my_x, my_side, my_hi, where, task_index]).astype(jnp.int32)
    vectors = (output_bias, norm1_gain, norm1_bias, inner_bias, outer_bias, norm2_gain, norm2_bias)

    x, q, k, v, ctx, ctxt, lse, wo, wi, wd, cot = attention(
        tokens,
        lengths,
        query_weight,
        key_weight,
        value_weight,
        query_bias,
        value_bias,
        output_weight,
        inner_weight,
        outer_weight,
        out_cot,
    )
    block_out, normed1, root1, h1t, act, slope, ddown, sums2 = middle(
        x, ctx, cot, length, labels, task_ids, task_weights, wo, wi, wd, vectors, head_table.transpose(1, 0, 2), group_seqs
    )
    block_out = block_out.reshape(tokens.shape)

    classes, tables = head_table.shape[1], head_table.shape[0]
    f2, r, quads = ff // 2, width // 32, width // 256
    parts, sums0 = [None] * (3 * quads), [None] * quads

    def back(quad, after):
        *grads, sums = attention_back(lengths, after, q, k, v, ctx, e["dctx"], lse, length, quad)
        parts[3 * quad : 3 * quad + 3] = grads
        sums0[quad] = sums
        return sums

    def small_args():
        return (ctxt, e["dattn"], parts, sums0, e["sums1"], e["inner_bias"])

    e = {}

    def send_outer(after):
        e["o_send"], e["table"] = outer_send(pos, task_ids, after, act, ddown, sums2, classes, tables)
        return e["table"]

    def rest_outer(after):
        e["o_rest"] = outer_rest(pos, after, act, ddown)
        return e["o_rest"]

    def do_inner_grad(after):
        e["dinner"], e["inner_bias"] = inner_grad(after, ddown, wd, slope)
        return e["inner_bias"]

    def send_inner(after):
        e["i_send"] = inner_send(pos, after, h1t, e["dinner"], True)
        return e["i_send"]

    def do_first_norm(after):
        e["dr1"], e["dattn"], e["dctx"], e["xt"], e["sums1"] = first_norm(
            after,
            e["dinner"],
            inner_weight,
            ddown,
            normed1,
            root1,
            output_weight,
            norm1_gain,
            tokens.reshape(rows, width),
        )
        return e["sums1"]

    def do_tokens(after):
        e["token_grad"], after = token_grads(after, e["dr1"], query_weight, key_weight, value_weight, parts)
        return after

    def send_qkv(after):
        e["qkv_s"] = qkv_send(pos, after, e["xt"], *small_args(), True)
        return e["qkv_s"]

    def keep_outer(after):
        got = swap(e["o_send"], "c")
        osx, okx, osy, oky, osz, okz, block = outer_keep(pos, after, e["o_rest"], got, e["table"])
        e["o1"] = (okx, swap(osx, "x"), oky, swap(osy, "y"), okz, swap(osz, "near"), block)
        return block

    def keep_inner(after):
        isx, ikx, isy, iky = inner_keep(pos, after, h1t, e["dinner"], swap(e["i_send"], "c"))
        e["i1"] = (ikx, swap(isx, "x"), iky, swap(isy, "y"))
        return ikx

    def second_outer(after):
        xs, xk, ys, yk, zs, zk, block = second_outer_stage(pos, after, *e["o1"])
        e["o2"] = (xk, swap(xs, "y"), yk, swap(ys, "x"), zk, swap(zs, "far"), block)
        return block

    def second_inner(after):
        xs, xk, ys, yk = second(pos, after, *e["i1"])
        e["i2"] = (xk, swap(xs, "y"), yk, swap(ys, "x"))
        return xk

    def do_third_outer(after):
        sent, kept, e["ozs"], e["oz"], table = third_outer(pos, after, *e["o2"])
        e["o3"] = (kept, swap(sent, "near"), table)
        return table

    def third_inner(after):
        sent, kept = third(pos, after, *e["i2"])
        e["i3"] = (kept, swap(sent, "near"))
        return kept

    def fourth_outer(after):
        sent, kept, table = fourth_outer_stage(pos, after, *e["o3"])
        e["o4"] = (kept, swap(sent, "far"), table)
        return table

    def fourth_inner(after):
        sent, kept = fourth(pos, after, *e["i3"])
        e["i4"] = (kept, swap(sent, "far"))
        return kept

    def sum_outer(after):
        e["outer_xy"], e["table_sum"] = sum_outer_stage(after, *e["o4"])
        return e["table_sum"]

    def last_inner(after):
        e["inner_s"], after = last(after, *e["i4"], None, None, (((0, 0, 2 * f2),),))
        return after

    def do_last_outer(after):
        e["outer_s"], after = last_outer(after, e["outer_xy"], e["oz2"], e["q2"][1])
        return after

    def keep_qkv(after):
        sx, kx, sy, ky, sz, kz, small = qkv_keep(
            pos, after, e["xt"], ctxt, e["dattn"], e["qkv_s"], swap(e["qkv_s"], "c"), e["ozs"], parts
        )
        e["q1"] = (kx, swap(sx, "x"), ky, swap(sy, "y"), kz, swap(sz, "near"), small, e["oz"])
        return small

    def stage(kernel, name, after, arrays, counts):
        return qkv_stage(kernel, name, pos, after, arrays, counts)

    def second_qkv(after):
        xs, xk, ys, yk, zs, zk, small, e["oz2"] = stage(
            second_qkv_kernel,
            "second_qkv_stage",
            after,
            e["q1"],
            [5 * r, 4 * r, 4 * r + SMALL, 4 * r, 4 * r, 4 * r, SMALL, r],
        )
        e["q2"] = (xk, swap(xs, "y"), yk, swap(ys, "x"), zk, swap(zs, "far"), small)
        return small

    def third_qkv(after):
        sent, kept, zs, zk, small = stage(
            third_qkv_kernel, "third_qkv_stage", after, e["q2"], [4 * r + SMALL, 4 * r, 2 * r, 2 * r, SMALL]
        )
        e["q3"] = (kept, swap(sent, "near"), zk, swap(zs, "x"), small)
        return small

    def fourth_qkv(after):
        sent, kept, zs, zk, small = stage(
            fourth_qkv_kernel, "fourth_qkv_stage", after, e["q3"], [2 * r + SMALL, 2 * r, r, r, SMALL]
        )
        e["q4"] = (kept, swap(sent, "far"), zk, swap(zs, "y"), small)
        return small

    def do_last_qkv(after):
        e["last"] = last_qkv(pos, *e["q4"], e["table_sum"], classes, tables, ff // width)
        return after

    steps = {
        "send_outer": send_outer,
        "rest_outer": rest_outer,
        "inner_grad": do_inner_grad,
        "send_inner": send_inner,
        "keep_outer": keep_outer,
        "first_norm": do_first_norm,
        "keep_inner": keep_inner,
        "second_outer": second_outer,
        "send_qkv": send_qkv,
        "second_inner": second_inner,
        "third_outer": do_third_outer,
        "keep_qkv": keep_qkv,
        "third_inner": third_inner,
        "tokens": do_tokens,
        "fourth_outer": fourth_outer,
        "second_qkv": second_qkv,
        "sum_outer": sum_outer,
        "third_qkv": third_qkv,
        "fourth_inner": fourth_inner,
        "fourth_qkv": fourth_qkv,
        "last_inner": last_inner,
        "last_outer": do_last_outer,
        "last_qkv": do_last_qkv,
    }
    for quad in range(quads):
        steps[f"back_{quad}"] = functools.partial(back, quad)
    if staged:
        after = sums2
        for name in ORDER:
            after = steps[name](after)
        query_s, key_s, value_s, output_s, *rest = e["last"]
        inner_s, outer_s = e["inner_s"], e["outer_s"]
        vector_s = [v.reshape(-1) for v in rest[:-1]]
        head_grad = rest[-1].transpose(1, 0, 2)
    else:
        after = do_first_norm(send_inner(do_inner_grad(send_outer(sums2))))
        after = rest_outer(after)
        i_keep = inner_send(pos, after, h1t, e["dinner"], False)
        for quad in range(quads):
            after = back(quad, after)
        after = do_tokens(send_qkv(after))
        qkv_k = qkv_send(pos, after, e["xt"], *small_args(), False)
        o_send, i_send, qkv_s = e["o_send"], e["i_send"], e["qkv_s"]

        def whole_rows(sent, kept):
            both = jnp.stack([jnp.where(my_c == 0, kept, sent), jnp.where(my_c == 0, sent, kept)], axis=1)
            return both.reshape(-1, both.shape[-1])

        def scatter(grad):
            return lax.psum_scatter(grad, ALL_AXES, scatter_dimension=0, tiled=True)

        def by_rows(array):
            return array.reshape(2, -1, array.shape[-1])

        part = ff // 4
        outer_s = scatter(whole_rows(o_send[: 2 * part].reshape(2, part, width), e["o_rest"]))
        inner_s = scatter(
            jnp.concatenate([whole_rows(by_rows(i_send[j]), by_rows(i_keep[j])) for j in range(2)], axis=-1)
        )
        count = width // 2

        def tensor(array, t):
            cols = slice(t * 256, (t + 1) * 256)
            return by_rows(jnp.concatenate([array[g * count : (g + 1) * count, cols] for g in range(quads)], axis=1))

        query_s, key_s, value_s, output_s = [
            scatter(whole_rows(tensor(qkv_s, t), tensor(qkv_k, t))) for t in range(4)
        ]
        small = lax.psum(jnp.concatenate([qkv_s[quads * count :, :width], e["inner_bias"], e["table"]]), ALL_AXES)
        devices = lax.axis_size("task") * lax.axis_size("batch")

        def mine(array):
            flat = array.reshape(-1)
            size = flat.shape[0] // devices
            return lax.dynamic_slice(flat, (where * size,), (size,))

        table = small[SMALL + ff // width :]
        vector_s = [mine(a) for a in (*small[:5], *table[:3], small[SMALL : SMALL + ff // width])]
        vector_s.append(lax.dynamic_slice(table, (3, task_index), (1, 1)).reshape(1))
        head_grad = table[4 : 4 + classes * tables].reshape(head_table.shape)
    token_grad = e["token_grad"].reshape(tokens.shape)
    bias_q, bias_v, gain1, bias1, bias_o, gain2, bias2, bias_d, bias_i, loss = vector_s
    return (
        block_out,
        token_grad,
        loss,
        query_s,
        key_s,
        value_s,
        bias_q,
        bias_v,
        output_s,
        bias_o,
        gain1,
        bias1,
        inner_s,
        bias_i,
        outer_s,
        bias_d,
        gain2,
        bias2,
        head_grad,
    )


def solution(mesh):
    rows = P(ALL_AXES)
    plain = P()
    task = P("task")
    staged = mesh.shape["task"] == 4 and mesh.shape["batch"] == 8
    return jax.shard_map(
        functools.partial(per_device, staged=staged),
        mesh=mesh,
        in_specs=(rows, rows, rows, rows, task, task) + (plain,) * 16,
        out_specs=(rows, rows, task) + (rows,) * 15 + (plain,),
        check_vma=False,
    )
```
